32 devices in a mesh: leaf: 8 (over z, y), sep: 4 (over x, core).
Axes of the slice: x: 2, y: 2, z: 4, core: 2. Of those that a mesh axis runs over, the one named last changes fastest.
Arguments:
- leaf_rhs: float32 [12288, 128], P(('leaf', 'sep')), may hold values from -6 to 6
- leaf_inverse: float32 [12288, 64], P(('leaf', 'sep')), may hold values from -1 to 1
- leaf_coupling: bfloat16 [2, 8192, 12288], P(None, None, ('leaf', 'sep')), may hold values from -0.21875 to 0.21875
- tile_mask: int32 [2, 128, 192], P(None, None, ('leaf', 'sep')), may hold values 0 or 1
- low_rhs: float32 [16384, 128], P(('leaf', 'sep')), may hold values from -6 to 6
- top_rhs: float32 [8192, 128], P(('leaf', 'sep')), may hold values from -6 to 6
- low_inverse: float32 [16384, 8192], P(('leaf', 'sep')), may hold values from -0.0625 to 0.0625
- top_inverse: float32 [8192, 8192], P(('leaf', 'sep')), may hold values from -0.0625 to 0.0625
- low_coupling: float32 [8192, 16384], P(None, ('leaf', 'sep')), may hold values from -0.0625 to 0.0625
Outputs:
- interior_solution: float32 [12288, 128], P(('leaf', 'sep'))
- top_solution: float32 [8192, 128], P(('leaf', 'sep'))
The draws below stay inside these ranges and needn't reach their ends.
All inputs are finite; a program needn't handle non-finite values. No bound on the sum of `tile_mask` on one device may be relied on, other than what follows from the above.
Results may differ from the reference program's by a relative error of at most 0.0033.
Values may be sent and summed in bfloat16 or wider, within the bound.
No kernel may reach another device: no remote copies, remote signals or barrier semaphores. Data moves between devices by JAX's collectives and lax.ppermute only.
A program may use at most 192 MiB of HBM per device.

```python
import jax
import jax.numpy as jnp
from jax import lax

LEVELS = 2
BLK = 64
SEPR = 8192
R = 128
ROWS = 12288


def touch_ends(array, stream_key, least, high):
    extent = array.shape
    spot = [jax.random.randint(jax.random.fold_in(stream_key, axis), (), 0, extent[axis]) for axis in range(len(extent))]
    array = array.at[tuple(spot)].set(least)
    longest = extent.index(max(extent))
    spot[longest] = (spot[longest] + 1) % extent[longest]
    return array.at[tuple(spot)].set(high)


def shard_levels(key, dims, shards, least, top_value):
    gain = 1.0
    for position, shards_of in shards:
        heights = jax.random.uniform(jax.random.fold_in(jax.random.fold_in(key, 6), position), (shards_of,), jnp.float32, least / len(shards), top_value / len(shards))
        gain = gain * jnp.repeat(jnp.exp(heights), dims[position] // shards_of).reshape((-1,) + (1,) * (len(dims) - 1 - position))
    return gain


def centred(key, extent, width, most, split=(), kind=jnp.bfloat16):
    drawn = jax.random.normal(key, extent, jnp.float32) * width
    if len(split) > 0:
        drawn = shard_levels(key, extent, split, -0.22, 0.18) * drawn
    return jnp.clip(drawn, min=-most, max=most).astype(kind)


def setup_inputs(seed: int = 0) -> dict:
    streams_of = jax.random.split(jax.random.key(seed), 10)
    leaf_rhs = centred(streams_of[0], (ROWS, R), 1.0, 6.0, ((0, 32),), jnp.float32)
    leaf_inverse = centred(streams_of[1], (ROWS, BLK), (BLK // 2) ** -0.5, 1.0, ((0, 32),), jnp.float32)
    leaf_coupling = centred(streams_of[2], (LEVELS, SEPR, ROWS), (ROWS // 16) ** -0.5, 0.21875, ((2, 32),))
    tile_mask = touch_ends((jax.random.randint(streams_of[3], (LEVELS, SEPR // BLK, ROWS // BLK), 0, 4) < 3).astype(jnp.int32), jax.random.fold_in(streams_of[3], 1), 0, 1)
    low_rhs = centred(streams_of[4], (2 * SEPR, R), 1.0, 6.0, ((0, 32),), jnp.float32)
    top_rhs = centred(streams_of[5], (SEPR, R), 1.0, 6.0, ((0, 32),), jnp.float32)
    low_inverse = centred(streams_of[6], (2 * SEPR, SEPR), SEPR ** -0.5, 0.0625, ((0, 32),), jnp.float32)
    top_inverse = centred(streams_of[7], (SEPR, SEPR), SEPR ** -0.5, 0.0625, ((0, 32),), jnp.float32)
    low_coupling = centred(streams_of[8], (SEPR, 2 * SEPR), SEPR ** -0.5, 0.0625, ((1, 32),), jnp.float32)
    return dict(leaf_rhs=leaf_rhs, leaf_inverse=leaf_inverse, leaf_coupling=leaf_coupling, tile_mask=tile_mask, low_rhs=low_rhs, top_rhs=top_rhs, low_inverse=low_inverse, top_inverse=top_inverse, low_coupling=low_coupling)


PRECISE = lax.Precision.HIGHEST


def lower_mask(block_size):
    row_index = lax.broadcasted_iota(jnp.int32, (block_size, block_size), 0)
    column_index = lax.broadcasted_iota(jnp.int32, (block_size, block_size), 1)
    return (row_index >= column_index).astype(jnp.float32)


def reference(leaf_rhs, leaf_inverse, leaf_coupling, tile_mask, low_rhs, top_rhs, low_inverse, top_inverse, low_coupling):
    leaf_blocks = ROWS // BLK
    triangle = lower_mask(BLK)
    inverses = leaf_inverse.reshape(leaf_blocks, BLK, BLK) * triangle
    forward_leaf = jnp.einsum("nij,njc->nic", inverses, leaf_rhs.reshape(leaf_blocks, BLK, R), precision=PRECISE).reshape(ROWS, R)
    rounded_leaf = forward_leaf.astype(jnp.bfloat16)
    masked_all = []
    for level_at in range(LEVELS):
        spread = tile_mask[level_at].astype(jnp.bfloat16)[:, None, :, None]
        masked_all.append((leaf_coupling[level_at].reshape(SEPR // BLK, BLK, ROWS // BLK, BLK) * spread).reshape(SEPR, ROWS))
    half_rows = ROWS // 2
    triangle_all = lower_mask(SEPR)
    factors = []
    first = []
    for member in range(2):
        lower_row = member * half_rows
        leaf_term = jnp.dot(masked_all[0][:, lower_row:lower_row + half_rows], rounded_leaf[lower_row:lower_row + half_rows], preferred_element_type=jnp.float32)
        factor = low_inverse[member * SEPR:(member + 1) * SEPR] * triangle_all
        factors.append(factor)
        first.append(jnp.dot(factor, low_rhs[member * SEPR:(member + 1) * SEPR] - leaf_term, precision=PRECISE))
    top_term = jnp.dot(masked_all[1], rounded_leaf, preferred_element_type=jnp.float32)
    coupled = jnp.dot(low_coupling, jnp.concatenate(first, 0), precision=PRECISE)
    top_factor = top_inverse * triangle_all
    top_forward = jnp.dot(top_factor, top_rhs - (top_term + coupled), precision=PRECISE)
    top_solution = jnp.dot(top_factor.T, top_forward, precision=PRECISE)
    first_back = []
    for member in range(2):
        carried = jnp.dot(low_coupling[:, member * SEPR:(member + 1) * SEPR].T, top_solution, precision=PRECISE)
        first_back.append(jnp.dot(factors[member].T, first[member] - carried, precision=PRECISE))
    top_rounded = top_solution.astype(jnp.bfloat16)
    pieces = []
    for member in range(2):
        lower_row = member * half_rows
        pieces.append(jnp.dot(masked_all[0][:, lower_row:lower_row + half_rows].T, first_back[member].astype(jnp.bfloat16), preferred_element_type=jnp.float32))
    leaf_back = jnp.concatenate(pieces, 0) + jnp.dot(masked_all[1].T, top_rounded, preferred_element_type=jnp.float32)
    interior_solution = jnp.einsum("nji,njc->nic", inverses, (forward_leaf - leaf_back).reshape(leaf_blocks, BLK, R), precision=PRECISE).reshape(ROWS, R)
    return interior_solution, top_solution
```

```python
import functools

import jax
import jax.numpy as jnp
from jax import lax
from jax.experimental import pallas as pl
from jax.experimental.pallas import tpu as pltpu
from jax.sharding import PartitionSpec as P

PRECISE = lax.Precision.HIGHEST
F32 = jnp.float32
BF16 = jnp.bfloat16
I16 = jnp.int16
AXES = ("leaf", "sep")
NEAR = 8
GROUP = 2 * NEAR
PAD = 16
VMEM = 56 << 20


def swap(block, offset):
    count = lax.axis_size("leaf") * lax.axis_size("sep")
    return lax.ppermute(block, AXES, [(at, at ^ offset) for at in range(count)])


def chunk_at(step, place, flip):
    return ((place[1] ^ step) << 1) | (place[0] ^ flip)


def encode(value):
    peak = jnp.max(jnp.abs(value), axis=0, keepdims=True)
    power = jnp.ceil(jnp.log2(jnp.maximum(peak, 1e-30)))
    scaled = jnp.floor(value * jnp.exp2(15.0 - power) + 0.5)
    code = jnp.clip(scaled, -32767.0, 32767.0).astype(jnp.int32).astype(I16)
    powers = jnp.broadcast_to(power, (PAD, value.shape[1])).astype(jnp.int32).astype(I16)
    return code, powers


def put(ref, coded):
    code, powers = coded
    rows = code.shape[0]
    ref[:rows, :] = code
    ref[rows:, :] = powers


def decode(block):
    rows = block.shape[0] - PAD
    power = block[rows:, :].astype(jnp.int32).astype(F32)[0:1, :]
    return block[:rows, :].astype(jnp.int32).astype(F32) * jnp.exp2(power - 15.0)


def halves(value):
    high = value.astype(BF16)
    return high, (value - high.astype(F32)).astype(BF16)


def dot(left, right):
    return jnp.dot(left, right, preferred_element_type=F32)


def masked(block, tiles, size):
    count, across = tiles.shape
    width = block.shape[1]
    lane = lax.broadcasted_iota(jnp.int32, (count, width), 1) // size
    spread = jnp.zeros((count, width), F32)
    for at in range(across):
        spread = jnp.where(lane == at, tiles[:, at : at + 1].astype(F32), spread)
    parts = []
    for at in range(count):
        row = jnp.broadcast_to(spread[at : at + 1, :], (16, width)).astype(BF16)
        tile = block[at * size : (at + 1) * size, :].reshape(size // 16, 16, width)
        parts.append((tile * row[None]).reshape(size, width))
    return jnp.concatenate(parts, 0)


def triangular(block, row_start, column_start):
    row = lax.broadcasted_iota(jnp.int32, block.shape, 0) + row_start
    column = lax.broadcasted_iota(jnp.int32, block.shape, 1) + column_start
    return jnp.where(row >= column, block, 0.0)


def add_rows(total, chunk, start, rhs):
    count = rhs.shape[0]
    size = total.shape[0]

    @pl.when(start // size == chunk)
    def _():
        where = pl.ds(pl.multiple_of(start % size, count), count)
        total[where, :] += rhs[...]


def emit(step, value, outs):
    own = outs[0]
    coded = encode(value)

    @pl.when(step == 0)
    def _():
        own[...] = value

    for at in range(1, NEAR):

        @pl.when(step == at)
        def _(at=at):
            put(outs[at], coded)


def call(kernel, place, grid, ins, outs, scratch, args, flops, moved):
    return pl.pallas_call(
        kernel,
        grid_spec=pltpu.PrefetchScalarGridSpec(
            num_scalar_prefetch=1,
            grid=grid,
            in_specs=ins,
            out_specs=[spec for spec, _ in outs],
            scratch_shapes=scratch,
        ),
        out_shape=[shape for _, shape in outs],
        compiler_params=pltpu.CompilerParams(vmem_limit_bytes=VMEM),
        cost_estimate=pl.CostEstimate(flops=flops, bytes_accessed=moved, transcendentals=0),
    )(place, *args)


def whole(shape):
    return pl.BlockSpec(shape, lambda *_: (0,) * len(shape))


def out_whole(shape, dtype):
    return whole(shape), jax.ShapeDtypeStruct(shape, dtype)


def leaf_value(place, chunk, level_block, tiles, rounded, rhs, total, size, start_at):
    total[...] = -dot(masked(level_block[0], tiles[0], size), rounded)
    add_rows(total, chunk, place[start_at], rhs)
    return total[...]


def leaf_send_kernel(size, place, leaf_rhs, inverse, coupling, tiles, rhs, sent, forward, rounded, total):
    step = pl.program_id(0)

    @pl.when(step == 0)
    def _():
        for at in range(leaf_rhs.shape[0] // size):
            rows = slice(at * size, (at + 1) * size)
            block = triangular(inverse[rows, :], 0, 0)
            value = jnp.dot(block, leaf_rhs[rows, :], precision=PRECISE, preferred_element_type=F32)
            forward[rows, :] = value
            rounded[rows, :] = value.astype(BF16)

    value = leaf_value(
        place, chunk_at(step, place, 1), coupling, tiles, rounded[...], rhs, total, size, 2
    )
    put(sent.at[0], encode(value))


def leaf_keep_kernel(size, place, rounded, coupling, tiles, rhs, received, *rest):
    step = pl.program_id(0)
    outs, total = rest[:NEAR], rest[NEAR]
    value = leaf_value(
        place, chunk_at(step, place, 0), coupling, tiles, rounded[...], rhs, total, size, 2
    )
    emit(step, value + decode(received[0]), outs)


def leaf_top_kernel(size, place, rounded, coupling, tiles, part):
    part[...] = dot(masked(coupling[0], tiles[0], size), rounded[...])


def sum_kernel(final, place, own, *rest):
    received, out = rest[:-1], rest[-1]
    value = own[...] if own.dtype == F32 else decode(own[...])
    for block in received:
        value = value + decode(block[...])
    if final:
        out[...] = value.astype(BF16)
    else:
        put(out, encode(value))


def summed(place, own, received, final=False):
    rows, columns = received[0].shape
    rows -= PAD
    shape = (rows, columns) if final else (rows + PAD, columns)
    return call(
        functools.partial(sum_kernel, final),
        place,
        (1,),
        [whole(own.shape)] + [whole(r.shape) for r in received],
        [out_whole(shape, BF16 if final else I16)],
        [],
        [own, *received],
        rows * columns * 8,
        rows * columns * 20,
    )[0]


def reduce_and_gather(place, outs, far, final=False):
    received = [swap(outs[at], at << 1) for at in range(1, NEAR)]
    coded = summed(place, outs[0], received, final and len(far) == 0)
    if far:
        coded = summed(place, coded, [swap(coded, offset) for offset in far], final)
    mine = [coded] + [swap(coded, at << 1) for at in range(1, NEAR)]
    return mine + [swap(block, 1) for block in mine]


def chunk_of(at, place):
    return chunk_at(at % NEAR, place, at // NEAR)


def factor_kernel(start_at, place, factor, *rest):
    blocks = rest[:GROUP]
    rows_out, columns_out, vector, wide, narrow = rest[GROUP:]
    step = pl.program_id(0)
    count, depth = factor.shape
    columns = vector.shape[1] // 2
    start = place[start_at]

    @pl.when(step == 0)
    def _():
        for at, block in enumerate(blocks):
            size = block.shape[0] - PAD
            high, low = halves(decode(block[...]))
            where = pl.ds(pl.multiple_of(chunk_of(at, place) * size, size), size)
            vector[where, :columns] = high
            vector[where, columns:] = low
        wide[...] = jnp.zeros_like(wide)
        narrow[...] = jnp.zeros_like(narrow)

    @pl.when(step * depth < start + count)
    def _():
        high, low = halves(triangular(factor[...], start, step * depth))
        where = pl.ds(pl.multiple_of(step * depth, depth), depth)
        wide[...] += dot(high, vector[where, :])
        narrow[...] += dot(low, vector[where, :columns])

    @pl.when(step == pl.num_programs(0) - 1)
    def _():
        value = wide[:, :columns] + wide[:, columns:] + narrow[...]
        rows_out[...] = value
        columns_out[...] = value.T


def factor_apply(place, factor, blocks, start_at):
    count, size = factor.shape
    columns = blocks[0].shape[1]
    depth = size // NEAR

    def at_factor(step, where):
        return (0, jnp.minimum(step, (where[start_at] + count - 1) // depth))

    return call(
        functools.partial(factor_kernel, start_at),
        place,
        (size // depth,),
        [pl.BlockSpec((count, depth), at_factor)] + [whole(b.shape) for b in blocks],
        [out_whole((count, columns), F32), out_whole((columns, count), F32)],
        [
            pltpu.VMEM((size, 2 * columns), BF16),
            pltpu.VMEM((count, 2 * columns), F32),
            pltpu.VMEM((count, columns), F32),
        ],
        [factor, *blocks],
        8 * count * size * columns,
        4 * count * size,
    )


def coupled_value(place, chunk, coupling, part, first, rhs, packed, total):
    columns = first.shape[1]

    @pl.when(pl.program_id(0) == 0)
    def _():
        high, low = halves(first[...])
        packed[:, :columns] = high
        packed[:, columns:] = low

    high, low = halves(coupling[...])
    product = dot(high, packed[...])
    total[...] = -(
        part[...] + (product[:, :columns] + product[:, columns:] + dot(low, packed[:, :columns]))
    )
    add_rows(total, chunk, place[3], rhs)
    return total[...]


def coupled_send_kernel(place, coupling, part, first, rhs, sent, packed, total):
    chunk = chunk_at(pl.program_id(0), place, 1)
    put(sent.at[0], encode(coupled_value(place, chunk, coupling, part, first, rhs, packed, total)))


def coupled_keep_kernel(place, coupling, part, first, rhs, received, *rest):
    step = pl.program_id(0)
    outs, packed, total = rest[:NEAR], rest[NEAR], rest[NEAR + 1]
    value = coupled_value(
        place, chunk_at(step, place, 0), coupling, part, first, rhs, packed, total
    )
    emit(step, value + decode(received[0]), outs)


def back_value(place, chunk, factor, vector, packed, start_at):
    columns = vector.shape[0]
    count, size = factor.shape

    @pl.when(pl.program_id(0) == 0)
    def _():
        high, low = halves(vector[...])
        packed[:columns, :] = high
        packed[columns:, :] = low

    high, low = halves(triangular(factor[...], place[start_at], chunk * size))
    product = dot(packed[...], high)
    return product[:columns, :] + product[columns:, :] + dot(packed[:columns, :], low)


def back_send_kernel(start_at, place, factor, vector, sent, packed):
    chunk = chunk_at(pl.program_id(0), place, 1)
    put(sent.at[0], encode(back_value(place, chunk, factor, vector, packed, start_at)))


def back_keep_kernel(start_at, place, factor, vector, received, *rest):
    step = pl.program_id(0)
    outs, packed = rest[:NEAR], rest[NEAR]
    value = back_value(place, chunk_at(step, place, 0), factor, vector, packed, start_at)
    emit(step, value + decode(received[0]), outs)


def back_apply(place, factor, vector, start_at):
    count, size = factor.shape
    columns = vector.shape[0]
    chunk = size // GROUP
    flops = 4 * count * size * columns
    moved = 2 * count * size
    coded = (columns + PAD, chunk)

    def specs(flip):
        return [
            pl.BlockSpec((count, chunk), lambda k, p: (0, chunk_at(k, p, flip))),
            whole(vector.shape),
        ]

    step_block = pl.BlockSpec((1, *coded), lambda k, p: (k, 0, 0))
    scratch = [pltpu.VMEM((2 * columns, count), BF16)]
    sent = call(
        functools.partial(back_send_kernel, start_at),
        place,
        (NEAR,),
        specs(1),
        [(step_block, jax.ShapeDtypeStruct((NEAR, *coded), I16))],
        scratch,
        [factor, vector],
        flops,
        moved,
    )[0]
    return call(
        functools.partial(back_keep_kernel, start_at),
        place,
        (NEAR,),
        specs(0) + [step_block],
        [out_whole((columns, chunk), F32)] + [out_whole(coded, I16)] * (NEAR - 1),
        scratch,
        [factor, vector, swap(sent, 1)],
        flops,
        moved,
    )


def carry_kernel(span, place, coupling, first, *rest):
    blocks = rest[:GROUP]
    gap, rounded, own, vector, wide, narrow = rest[GROUP:]
    step = pl.program_id(0)
    depth = coupling.shape[0]
    columns = first.shape[0]

    @pl.when(step == 0)
    def _():
        for at, block in enumerate(blocks):
            size = block.shape[1]
            high, low = halves(decode(block[...]))
            where = pl.ds(pl.multiple_of(chunk_of(at, place) * size, size), size)
            vector[:columns, where] = high
            vector[columns:, where] = low
        rounded[...] = vector[:columns, :]
        where = pl.ds(pl.multiple_of(place[3] // span * span, span), span)
        value = vector[:columns, where].astype(F32) + vector[columns:, where].astype(F32)
        own[...] = value.T
        wide[...] = jnp.zeros_like(wide)
        narrow[...] = jnp.zeros_like(narrow)

    @pl.when(step >= 0)
    def _():
        high, low = halves(coupling[...])
        where = pl.ds(pl.multiple_of(step * depth, depth), depth)
        wide[...] += dot(vector[:, where], high)
        narrow[...] += dot(vector[:columns, where], low)

    @pl.when(step == pl.num_programs(0) - 1)
    def _():
        gap[...] = first[...] - (wide[:columns, :] + wide[columns:, :] + narrow[...])


def leaf_back_top_kernel(size, place, path, coupling, tiles, out):
    @pl.when(pl.program_id(0) == 0)
    def _():
        out[...] = jnp.zeros_like(out)

    @pl.when(pl.program_id(0) >= 0)
    def _():
        out[...] += dot(path[...], masked(coupling[0], tiles[0], size))


def leaf_back_kernel(size, place, coupling, tiles, top, forward, inverse, *rest):
    blocks = rest[:GROUP]
    out, path, total = rest[GROUP:]
    step = pl.program_id(0)
    depth = coupling.shape[1]

    @pl.when(step == 0)
    def _():
        for at, block in enumerate(blocks):
            where = pl.ds(pl.multiple_of(chunk_of(at, place) * depth, depth), depth)
            path[:, where] = block[...]
        total[...] = top[...]

    @pl.when(step >= 0)
    def _():
        where = pl.ds(pl.multiple_of(step * depth, depth), depth)
        total[...] += dot(path[:, where], masked(coupling[0], tiles[0], size))

    @pl.when(step == pl.num_programs(0) - 1)
    def _():
        gap = forward[...] - total[...].T
        for at in range(gap.shape[0] // size):
            rows = slice(at * size, (at + 1) * size)
            block = triangular(inverse[rows, :], 0, 0).T
            out[rows, :] = jnp.dot(
                block, gap[rows, :], precision=PRECISE, preferred_element_type=F32
            )


def body(
    leaf_rhs,
    leaf_inverse,
    leaf_coupling,
    tile_mask,
    low_rhs,
    top_rhs,
    low_inverse,
    top_inverse,
    low_coupling,
):
    device_total = lax.axis_size("leaf") * lax.axis_size("sep")
    device = lax.axis_index("leaf") * lax.axis_size("sep") + lax.axis_index("sep")
    local_rows, columns = leaf_rhs.shape
    size = leaf_inverse.shape[1]
    sep_size = low_inverse.shape[1]
    low_count = low_inverse.shape[0]
    top_count = top_inverse.shape[0]
    chunk = sep_size // GROUP
    tiles = chunk // size
    across = local_rows // size
    low_far = list(range(GROUP, device_total // 2, GROUP))
    top_far = list(range(GROUP, device_total, GROUP))
    low_start = device % (device_total // 2) * low_count
    top_start = device * top_count
    place = jnp.stack([device % 2, device % GROUP // 2, low_start, top_start]).astype(jnp.int32)

    coded = (chunk + PAD, columns)
    step_block = pl.BlockSpec((1, *coded), lambda k, p: (k, 0, 0))
    sent_out = (step_block, jax.ShapeDtypeStruct((NEAR, *coded), I16))
    kept_out = [out_whole((chunk, columns), F32)] + [out_whole(coded, I16)] * (NEAR - 1)
    total = pltpu.VMEM((chunk, columns), F32)
    leaf_flops = 2 * sep_size * local_rows * columns
    leaf_moved = 2 * sep_size * local_rows

    def leaf_specs(level, where):
        return [
            pl.BlockSpec((1, chunk, local_rows), lambda k, p: (level, where(k, p), 0)),
            pl.BlockSpec((1, tiles, across), lambda k, p: (level, where(k, p), 0)),
        ]

    def parity(flip):
        return lambda k, p: chunk_at(k, p, flip)

    def straight(k, p):
        return k

    sent, forward_leaf, rounded_leaf = call(
        functools.partial(leaf_send_kernel, size),
        place,
        (NEAR,),
        [whole(leaf_rhs.shape), whole(leaf_inverse.shape), *leaf_specs(0, parity(1)), whole(low_rhs.shape)],
        [sent_out, out_whole(leaf_rhs.shape, F32), out_whole(leaf_rhs.shape, BF16)],
        [total],
        [leaf_rhs, leaf_inverse, leaf_coupling, tile_mask, low_rhs],
        leaf_flops // 2,
        leaf_moved // 2,
    )
    kept = call(
        functools.partial(leaf_keep_kernel, size),
        place,
        (NEAR,),
        [whole(rounded_leaf.shape), *leaf_specs(0, parity(0)), whole(low_rhs.shape), step_block],
        kept_out,
        [total],
        [rounded_leaf, leaf_coupling, tile_mask, low_rhs, swap(sent, 1)],
        leaf_flops // 2,
        leaf_moved // 2,
    )
    part = call(
        functools.partial(leaf_top_kernel, size),
        place,
        (GROUP,),
        [whole(rounded_leaf.shape), *leaf_specs(1, straight)],
        [
            (
                pl.BlockSpec((chunk, columns), lambda k, p: (k, 0)),
                jax.ShapeDtypeStruct((sep_size, columns), F32),
            )
        ],
        [],
        [rounded_leaf, leaf_coupling, tile_mask],
        leaf_flops,
        leaf_moved,
    )[0]
    first_input = reduce_and_gather(place, kept, low_far)
    first_rows, first_columns = factor_apply(place, low_inverse, first_input, 2)

    coupled_flops = 4 * sep_size * low_count * columns
    coupled_moved = 2 * sep_size * low_count

    def coupled_specs(flip):
        return [
            pl.BlockSpec((chunk, low_count), lambda k, p: (chunk_at(k, p, flip), 0)),
            pl.BlockSpec((chunk, columns), lambda k, p: (chunk_at(k, p, flip), 0)),
            whole(first_rows.shape),
            whole(top_rhs.shape),
        ]

    coupled_scratch = [pltpu.VMEM((low_count, 2 * columns), BF16), total]
    coupled_args = [low_coupling, part, first_rows, top_rhs]
    sent = call(
        coupled_send_kernel,
        place,
        (NEAR,),
        coupled_specs(1),
        [sent_out],
        coupled_scratch,
        coupled_args,
        coupled_flops,
        coupled_moved,
    )[0]
    kept = call(
        coupled_keep_kernel,
        place,
        (NEAR,),
        coupled_specs(0) + [step_block],
        kept_out,
        coupled_scratch,
        [*coupled_args, swap(sent, 1)],
        coupled_flops,
        coupled_moved,
    )
    top_input = reduce_and_gather(place, kept, top_far)
    _, forward_columns = factor_apply(place, top_inverse, top_input, 3)

    kept = back_apply(place, top_inverse, forward_columns, 3)
    solution_blocks = reduce_and_gather(place, kept, top_far)
    span = max(top_count, 128)
    depth = sep_size // NEAR
    gap, top_rounded, top_own = call(
        functools.partial(carry_kernel, span),
        place,
        (NEAR,),
        [pl.BlockSpec((depth, low_count), lambda k, p: (k, 0)), whole(first_columns.shape)]
        + [whole(b.shape) for b in solution_blocks],
        [
            out_whole((columns, low_count), F32),
            out_whole((columns, sep_size), BF16),
            out_whole((span, columns), F32),
        ],
        [
            pltpu.VMEM((2 * columns, sep_size), BF16),
            pltpu.VMEM((2 * columns, low_count), F32),
            pltpu.VMEM((columns, low_count), F32),
        ],
        [low_coupling, first_columns, *solution_blocks],
        2 * coupled_flops,
        2 * coupled_moved,
    )
    top_solution = lax.dynamic_slice_in_dim(top_own, top_start % span, top_count, 0)
    kept = back_apply(place, low_inverse, gap, 2)
    back_top = call(
        functools.partial(leaf_back_top_kernel, size),
        place,
        (GROUP,),
        [pl.BlockSpec((columns, chunk), lambda k, p: (0, k)), *leaf_specs(1, straight)],
        [out_whole((columns, local_rows), F32)],
        [],
        [top_rounded, leaf_coupling, tile_mask],
        leaf_flops,
        leaf_moved,
    )[0]
    path = reduce_and_gather(place, kept, low_far, True)
    interior = call(
        functools.partial(leaf_back_kernel, size),
        place,
        (GROUP,),
        [
            *leaf_specs(0, straight),
            whole(back_top.shape),
            whole(forward_leaf.shape),
            whole(leaf_inverse.shape),
        ]
        + [whole(b.shape) for b in path],
        [out_whole((local_rows, columns), F32)],
        [
            pltpu.VMEM((columns, sep_size), BF16),
            pltpu.VMEM((columns, local_rows), F32),
        ],
        [leaf_coupling, tile_mask, back_top, forward_leaf, leaf_inverse, *path],
        leaf_flops,
        leaf_moved,
    )[0]
    return interior, top_solution


def solution(mesh):
    return jax.shard_map(
        body,
        mesh=mesh,
        in_specs=(
            P(("leaf", "sep"), None),
            P(("leaf", "sep"), None),
            P(None, None, ("leaf", "sep")),
            P(None, None, ("leaf", "sep")),
            P(("leaf", "sep"), None),
            P(("leaf", "sep"), None),
            P(("leaf", "sep"), None),
            P(("leaf", "sep"), None),
            P(None, ("leaf", "sep")),
        ),
        out_specs=(P(("leaf", "sep"), None), P(("leaf", "sep"), None)),
        check_vma=False,
    )
```

```python
import functools

import jax
import jax.numpy as jnp
from jax import lax
from jax.experimental import pallas as pl
from jax.experimental.pallas import tpu as pltpu
from jax.sharding import PartitionSpec as P

PRECISE = lax.Precision.HIGHEST
F32 = jnp.float32
BF16 = jnp.bfloat16
I16 = jnp.int16
AXES = ("leaf", "sep")
NEAR = 8
GROUP = 2 * NEAR
PAD = 16
VMEM = 24 << 20


def swap(block, offset):
    count = lax.axis_size("leaf") * lax.axis_size("sep")
    return lax.ppermute(block, AXES, [(at, at ^ offset) for at in range(count)])


def exchange(blocks):
    count = lax.axis_size("leaf") * lax.axis_size("sep")
    groups = [
        [first + 2 * at + core for at in range(NEAR)]
        for first in range(0, count, GROUP)
        for core in range(2)
    ]
    return lax.all_to_all(blocks, AXES, 0, 0, axis_index_groups=groups)


def collect(block):
    count = lax.axis_size("leaf") * lax.axis_size("sep")
    groups = [
        [first + 2 * at + core for at in range(NEAR)]
        for first in range(0, count, GROUP)
        for core in range(2)
    ]
    return lax.all_gather(block, AXES, axis_index_groups=groups)


def encode(value):
    peak = jnp.maximum(jnp.max(jnp.abs(value), axis=0, keepdims=True), 1e-30)
    power = jnp.ceil(jnp.log2(peak))
    part = jnp.ceil(peak * jnp.exp2(14.0 - power))
    scale = 32767.0 / (part * jnp.exp2(power - 14.0))
    code = jnp.floor(value * scale + 0.5).astype(jnp.int32).astype(I16)
    row = lax.broadcasted_iota(jnp.int32, (PAD, value.shape[1]), 0)
    return code, jnp.where(row == 0, power, part).astype(jnp.int32).astype(I16)


def put(ref, coded):
    code, head = coded
    rows = code.shape[0]
    ref[:rows, :] = code
    ref[rows:, :] = head


def decode(block):
    rows = block.shape[0] - PAD
    head = block[rows:, :].astype(jnp.int32).astype(F32)
    scale = head[1:2, :] * jnp.exp2(head[0:1, :] - 14.0) * (1.0 / 32767.0)
    return block[:rows, :].astype(jnp.int32).astype(F32) * scale


def halves(value):
    high = value.astype(BF16)
    return high, (value - high.astype(F32)).astype(BF16)


def dot(left, right):
    return jnp.dot(left, right, preferred_element_type=F32)


def spread_tiles(tiles, level, width, size):
    across = tiles.shape[0]
    flags = tiles[:, level, :].astype(F32).T
    lane = lax.broadcasted_iota(jnp.int32, (flags.shape[0], width), 1) // size
    spread = jnp.zeros((flags.shape[0], width), F32)
    for at in range(across):
        spread = jnp.where(lane == at, flags[:, at : at + 1], spread)
    return spread


def masked(block, spread, chunk, size):
    width = block.shape[1]
    count = block.shape[0] // size
    flags = spread[pl.ds(pl.multiple_of(chunk * count, count), count), :]
    parts = []
    for at in range(count):
        row = jnp.broadcast_to(flags[at : at + 1, :], (16, width)).astype(BF16)
        tile = block[at * size : (at + 1) * size, :].reshape(size // 16, 16, width)
        parts.append((tile * row[None]).reshape(size, width))
    return jnp.concatenate(parts, 0)


def triangular(block, row_start, column_start):
    row = lax.broadcasted_iota(jnp.int32, block.shape, 0) + row_start
    column = lax.broadcasted_iota(jnp.int32, block.shape, 1) + column_start
    return jnp.where(row >= column, block, 0.0)


def with_rows(value, chunk, start, rhs):
    count = rhs.shape[0]
    parts = []
    for at in range(value.shape[0] // count):
        here = (start == chunk * value.shape[0] + at * count).astype(F32)
        parts.append(value[at * count : (at + 1) * count, :] + rhs[...] * here)
    return jnp.concatenate(parts, 0) if len(parts) > 1 else parts[0]


def call(kernel, place, steps, ins, outs, scratch, args, flops, moved):
    return pl.pallas_call(
        kernel,
        grid_spec=pltpu.PrefetchScalarGridSpec(
            num_scalar_prefetch=1,
            grid=(steps,),
            in_specs=ins,
            out_specs=[spec for spec, _ in outs],
            scratch_shapes=scratch,
        ),
        out_shape=[shape for _, shape in outs],
        compiler_params=pltpu.CompilerParams(vmem_limit_bytes=VMEM),
        cost_estimate=pl.CostEstimate(flops=flops, bytes_accessed=moved, transcendentals=0),
    )(place, *args)


def whole(shape):
    return pl.BlockSpec(shape, lambda *_: (0,) * len(shape))


def out_whole(shape, dtype):
    return whole(shape), jax.ShapeDtypeStruct(shape, dtype)


def in_steps(count, shape, dtype=None):
    spec = pl.BlockSpec((count, *shape), lambda k, p: (k,) + (0,) * len(shape))
    return spec if dtype is None else (spec, jax.ShapeDtypeStruct((NEAR, *shape), dtype))


def parity_of(place, flip):
    return place[0] ^ flip


def chunk_at(place, group, at, flip):
    return (pl.program_id(0) * group + at) * 2 + parity_of(place, flip)


def leaf_send_kernel(size, place, leaf_rhs, inverse_t, coupling, tiles, rhs, sent, forward, rounded, spread):
    group = coupling.shape[1]

    @pl.when(pl.program_id(0) == 0)
    def _():
        inverse = inverse_t[...].T
        for at in range(leaf_rhs.shape[0] // size):
            rows = slice(at * size, (at + 1) * size)
            block = triangular(inverse[rows, :], 0, 0)
            value = jnp.dot(block, leaf_rhs[rows, :], precision=PRECISE, preferred_element_type=F32)
            forward[rows, :] = value
            rounded[rows, :] = value.astype(BF16)
        spread[...] = spread_tiles(tiles, 0, coupling.shape[4], size)

    for at in range(group):
        chunk = chunk_at(place, group, at, 1)
        value = -dot(masked(coupling[0, at, 0], spread, chunk, size), rounded[...])
        put(sent.at[at], encode(with_rows(value, chunk, place[1], rhs)))


def leaf_keep_kernel(size, place, rounded, coupling, tiles, rhs, received, sent, spread):
    group = coupling.shape[1]

    @pl.when(pl.program_id(0) == 0)
    def _():
        spread[...] = spread_tiles(tiles, 0, coupling.shape[4], size)

    for at in range(group):
        chunk = chunk_at(place, group, at, 0)
        value = -dot(masked(coupling[0, at, 0], spread, chunk, size), rounded[...])
        put(sent.at[at], encode(with_rows(value, chunk, place[1], rhs) + decode(received[at])))


def leaf_top_kernel(size, place, rounded, coupling, tiles, part, spread):
    group, _, rows = coupling.shape[1:4]

    @pl.when(pl.program_id(0) == 0)
    def _():
        spread[...] = spread_tiles(tiles, 1, coupling.shape[4], size)

    for at in range(group):
        for core in range(2):
            chunk = (pl.program_id(0) * group + at) * 2 + core
            part[at, core] = dot(masked(coupling[0, at, core], spread, chunk, size), rounded[...])


def sum_kernel(final, place, *rest):
    blocks, out = rest[:-1], rest[-1]
    value = None
    for stack in blocks:
        for at in range(stack.shape[0]):
            term = decode(stack[at])
            value = term if value is None else value + term
    if final:
        value = value.astype(BF16)
        for at in range(out.shape[0]):
            out[at] = value
    else:
        coded = encode(value)
        for at in range(out.shape[0]):
            put(out.at[at], coded)


def summed(place, stacks, copies, final=False):
    _, rows, columns = stacks[0].shape
    shape = (copies, rows - PAD if final else rows, columns)
    return call(
        functools.partial(sum_kernel, final),
        place,
        1,
        [whole(s.shape) for s in stacks],
        [out_whole(shape, BF16 if final else I16)],
        [],
        stacks,
        rows * columns * 8,
        rows * columns * 20,
    )[0]


def reduce_and_gather(place, sent, far, direct, final=False):
    received = exchange(sent)
    copies = NEAR if direct else 1
    coded = summed(place, [received], 1 if far else copies, final and not far)
    if far:
        coded = summed(place, [coded] + [swap(coded, offset) for offset in far], copies, final)
    mine = exchange(coded) if direct else collect(coded[0])
    return mine, swap(mine, 1)


def factor_kernel(flip, start_at, group, place, *rest):
    factors, rest = rest[:group], rest[group:]
    if flip:
        blocks, before, rows_out, columns_out, wide, narrow = rest
    else:
        blocks, rows_out, wide, narrow = rest
    step = pl.program_id(0)
    count, depth = factors[0].shape
    columns = narrow.shape[1]
    start = place[start_at]

    @pl.when(step == 0)
    def _():
        wide[...] = jnp.zeros_like(wide)
        narrow[...] = jnp.zeros_like(narrow)

    for at in range(group):
        chunk = chunk_at(place, group, at, flip)

        @pl.when(chunk * depth < start + count)
        def _(at=at, chunk=chunk):
            high, low = halves(triangular(factors[at][...], start, chunk * depth))
            upper, lower = halves(decode(blocks[at]))
            wide[...] += dot(high, jnp.concatenate([upper, lower], 1))
            narrow[...] += dot(low, upper)

    @pl.when(step == pl.num_programs(0) - 1)
    def _():
        value = wide[:, :columns] + wide[:, columns:] + narrow[...]
        if flip:
            value = value + before[...]
            columns_out[...] = value.T
        rows_out[...] = value


def factor_apply(place, factor, stacks, start_at):
    count, size = factor.shape
    depth = size // GROUP
    columns = stacks[0].shape[2]
    group = 2
    result = ()
    for flip in range(2):
        outs = [out_whole((count, columns), F32)]
        if flip:
            outs.append(out_whole((columns, count), F32))
        result = call(
            functools.partial(factor_kernel, flip, start_at, group),
            place,
            NEAR // group,
            [
                pl.BlockSpec(
                    (count, depth),
                    lambda k, p, at=at, flip=flip: (0, (k * group + at) * 2 + parity_of(p, flip)),
                )
                for at in range(group)
            ]
            + [in_steps(group, stacks[0].shape[1:])]
            + [whole(r.shape) for r in result],
            outs,
            [pltpu.VMEM((count, 2 * columns), F32), pltpu.VMEM((count, columns), F32)],
            [factor] * group + [stacks[flip], *result],
            4 * count * size * columns,
            2 * count * size,
        )
    return result


def pack_rows(first, packed):
    columns = first.shape[1]

    @pl.when(pl.program_id(0) == 0)
    def _():
        high, low = halves(first[...])
        packed[:, :columns] = high
        packed[:, columns:] = low


def coupled_kernel(flip, place, coupling, part, first, rhs, *rest):
    if flip:
        sent, packed = rest
    else:
        received, sent, packed = rest
    group = coupling.shape[0]
    columns = first.shape[1]
    pack_rows(first, packed)
    for at in range(group):
        high, low = halves(coupling[at, 0])
        product = dot(high, packed[...])
        value = product[:, :columns] + product[:, columns:] + dot(low, packed[:, :columns])
        value = -(part[at, 0] + value)
        value = with_rows(value, chunk_at(place, group, at, flip), place[2], rhs)
        if not flip:
            value = value + decode(received[at])
        put(sent.at[at], encode(value))


def pack_columns(vector, packed):
    columns = vector.shape[0]

    @pl.when(pl.program_id(0) == 0)
    def _():
        high, low = halves(vector[...])
        packed[:columns, :] = high
        packed[columns:, :] = low


def back_kernel(flip, start_at, group, place, *rest):
    factors, rest = rest[:group], rest[group:]
    if flip:
        vector, sent, packed = rest
    else:
        vector, received, sent, packed = rest
    columns = vector.shape[0]
    pack_columns(vector, packed)
    for at in range(group):
        chunk = chunk_at(place, group, at, flip)
        depth = factors[at].shape[1]
        high, low = halves(triangular(factors[at][...], place[start_at], chunk * depth))
        product = dot(packed[...], high)
        value = product[:columns, :] + product[columns:, :] + dot(packed[:columns, :], low)
        if not flip:
            value = value + decode(received[at])
        put(sent.at[at], encode(value))


def back_apply(place, factor, vector, start_at):
    count, size = factor.shape
    columns = vector.shape[0]
    chunk = size // GROUP
    coded = (columns + PAD, chunk)
    group = 2
    sent = None
    for flip in (1, 0):
        sent = call(
            functools.partial(back_kernel, flip, start_at, group),
            place,
            NEAR // group,
            [
                pl.BlockSpec(
                    (count, chunk),
                    lambda k, p, at=at, flip=flip: (0, (k * group + at) * 2 + parity_of(p, flip)),
                )
                for at in range(group)
            ]
            + [whole(vector.shape)]
            + [in_steps(group, coded)] * (1 - flip),
            [in_steps(group, coded, I16)],
            [pltpu.VMEM((2 * columns, count), BF16)],
            [factor] * group + [vector] + ([] if flip else [swap(sent, 1)]),
            4 * count * size * columns,
            2 * count * size,
        )[0]
    return sent


def carry_kernel(flip, place, coupling, blocks, before, gap, rounded, wide, narrow):
    step = pl.program_id(0)
    group = coupling.shape[0]
    columns = before.shape[0]

    @pl.when(step == 0)
    def _():
        wide[...] = jnp.zeros_like(wide)
        narrow[...] = jnp.zeros_like(narrow)

    for at in range(group):

        @pl.when(step >= 0)
        def _(at=at):
            upper, lower = halves(decode(blocks[at]))
            rounded[at] = upper
            high, low = halves(coupling[at, 0])
            wide[...] += dot(jnp.concatenate([upper, lower], 0), high)
            narrow[...] += dot(upper, low)

    @pl.when(step == pl.num_programs(0) - 1)
    def _():
        gap[...] = before[...] - (wide[:columns, :] + wide[columns:, :] + narrow[...])


def own_kernel(place, mine, other, out):
    size = out.shape[0]
    here = (place[2] // size % 2 == place[0]).astype(F32)
    out[...] = (decode(mine[0]) * here + decode(other[0]) * (1.0 - here)).T


def leaf_back_top_kernel(size, place, mine, other, near_coupling, far_coupling, tiles, out, spread):
    step = pl.program_id(0)
    group = near_coupling.shape[1]

    @pl.when(step == 0)
    def _():
        spread[...] = spread_tiles(tiles, 1, near_coupling.shape[4], size)
        out[...] = jnp.zeros_like(out)

    @pl.when(step >= 0)
    def _():
        for flip, path, coupling in ((0, mine, near_coupling), (1, other, far_coupling)):
            for at in range(group):
                chunk = chunk_at(place, group, at, flip)
                out[...] += dot(path[at], masked(coupling[0, at, 0], spread, chunk, size))


def leaf_back_kernel(flip, size, place, coupling, tiles, path, before, *rest):
    if flip:
        forward, inverse_t, out, total, spread = rest
    else:
        out, total, spread = rest
    step = pl.program_id(0)
    group = coupling.shape[1]

    @pl.when(step == 0)
    def _():
        spread[...] = spread_tiles(tiles, 0, coupling.shape[4], size)
        total[...] = before[...]

    @pl.when(step >= 0)
    def _():
        for at in range(group):
            chunk = chunk_at(place, group, at, flip)
            total[...] += dot(path[at], masked(coupling[0, at, 0], spread, chunk, size))

    @pl.when(step == pl.num_programs(0) - 1)
    def _():
        if not flip:
            out[...] = total[...]
        else:
            gap = forward[...] - total[...].T
            inverse = inverse_t[...].T
            for at in range(gap.shape[0] // size):
                rows = slice(at * size, (at + 1) * size)
                block = triangular(inverse[rows, :], 0, 0).T
                out[rows, :] = jnp.dot(
                    block, gap[rows, :], precision=PRECISE, preferred_element_type=F32
                )


def body(
    leaf_rhs,
    leaf_inverse,
    leaf_coupling,
    tile_mask,
    low_rhs,
    top_rhs,
    low_inverse,
    top_inverse,
    low_coupling,
):
    device_total = lax.axis_size("leaf") * lax.axis_size("sep")
    device = lax.axis_index("leaf") * lax.axis_size("sep") + lax.axis_index("sep")
    local_rows, columns = leaf_rhs.shape
    size = leaf_inverse.shape[1]
    levels = leaf_coupling.shape[0]
    sep_size = low_inverse.shape[1]
    low_count = low_inverse.shape[0]
    top_count = top_inverse.shape[0]
    chunk = sep_size // GROUP
    low_far = list(range(GROUP, device_total // 2, GROUP))
    top_far = list(range(GROUP, device_total, GROUP))
    low_start = device % (device_total // 2) * low_count
    top_start = device * top_count
    place = jnp.stack([device % 2, low_start, top_start]).astype(jnp.int32)

    inverse_t = leaf_inverse.T
    tiles = jnp.transpose(tile_mask, (2, 0, 1))
    coupling = leaf_coupling.reshape(levels, NEAR, 2, chunk, local_rows)
    low_blocks = low_coupling.reshape(NEAR, 2, chunk, low_count)

    coded = (chunk + PAD, columns)
    back_coded = (columns + PAD, chunk)
    spread = pltpu.VMEM((sep_size // size, local_rows), F32)
    leaf_flops = 2 * sep_size * local_rows * columns
    leaf_moved = 2 * sep_size * local_rows

    def leaf_block(level, group, flip):
        return pl.BlockSpec(
            (1, group, 1, chunk, local_rows), lambda k, p: (level, k, parity_of(p, flip), 0, 0)
        )

    group = 4
    sent, forward_leaf, rounded_leaf = call(
        functools.partial(leaf_send_kernel, size),
        place,
        NEAR // group,
        [
            whole(leaf_rhs.shape),
            whole(inverse_t.shape),
            leaf_block(0, group, 1),
            whole(tiles.shape),
            whole(low_rhs.shape),
        ],
        [in_steps(group, coded, I16), out_whole(leaf_rhs.shape, F32), out_whole(leaf_rhs.shape, BF16)],
        [spread],
        [leaf_rhs, inverse_t, coupling, tiles, low_rhs],
        leaf_flops // 2,
        leaf_moved // 2,
    )
    sent = call(
        functools.partial(leaf_keep_kernel, size),
        place,
        NEAR // group,
        [
            whole(rounded_leaf.shape),
            leaf_block(0, group, 0),
            whole(tiles.shape),
            whole(low_rhs.shape),
            in_steps(group, coded),
        ],
        [in_steps(group, coded, I16)],
        [spread],
        [rounded_leaf, coupling, tiles, low_rhs, swap(sent, 1)],
        leaf_flops // 2,
        leaf_moved // 2,
    )[0]
    group = 2
    part = call(
        functools.partial(leaf_top_kernel, size),
        place,
        NEAR // group,
        [
            whole(rounded_leaf.shape),
            pl.BlockSpec((1, group, 2, chunk, local_rows), lambda k, p: (1, k, 0, 0, 0)),
            whole(tiles.shape),
        ],
        [in_steps(group, (2, chunk, columns), F32)],
        [spread],
        [rounded_leaf, coupling, tiles],
        leaf_flops,
        leaf_moved,
    )[0]
    first_input = reduce_and_gather(place, sent, low_far, False)
    first_rows, first_columns = factor_apply(place, low_inverse, first_input, 1)

    coupled_flops = 4 * sep_size * low_count * columns
    coupled_moved = 2 * sep_size * low_count
    sent = None
    for flip in (1, 0):
        sent = call(
            functools.partial(coupled_kernel, flip),
            place,
            NEAR // group,
            [
                pl.BlockSpec(
                    (group, 1, chunk, low_count),
                    lambda k, p, flip=flip: (k, parity_of(p, flip), 0, 0),
                ),
                pl.BlockSpec(
                    (group, 1, chunk, columns),
                    lambda k, p, flip=flip: (k, parity_of(p, flip), 0, 0),
                ),
                whole(first_rows.shape),
                whole(top_rhs.shape),
            ]
            + [in_steps(group, coded)] * (1 - flip),
            [in_steps(group, coded, I16)],
            [pltpu.VMEM((low_count, 2 * columns), BF16)],
            [low_blocks, part, first_rows, top_rhs] + ([] if flip else [swap(sent, 1)]),
            coupled_flops,
            coupled_moved,
        )[0]
    top_input = reduce_and_gather(place, sent, top_far, True)
    _, forward_columns = factor_apply(place, top_inverse, top_input, 2)

    sent = back_apply(place, top_inverse, forward_columns, 2)
    solution_blocks = reduce_and_gather(place, sent, top_far, True)
    gap, rounded = first_columns, []
    for flip in range(2):
        gap, near = call(
            functools.partial(carry_kernel, flip),
            place,
            NEAR // group,
            [
                pl.BlockSpec(
                    (group, 1, chunk, low_count),
                    lambda k, p, flip=flip: (k, parity_of(p, flip), 0, 0),
                ),
                in_steps(group, back_coded),
                whole(gap.shape),
            ],
            [out_whole(gap.shape, F32), in_steps(group, (columns, chunk), BF16)],
            [pltpu.VMEM((2 * columns, low_count), F32), pltpu.VMEM((columns, low_count), F32)],
            [low_blocks, solution_blocks[flip], gap],
            coupled_flops,
            coupled_moved,
        )
        rounded.append(near)
    top_own = call(
        own_kernel,
        place,
        1,
        [pl.BlockSpec((1, *back_coded), lambda k, p: (p[2] // chunk // 2, 0, 0))] * 2,
        [out_whole((chunk, columns), F32)],
        [],
        list(solution_blocks),
        chunk * columns,
        8 * chunk * columns,
    )[0]
    top_solution = lax.dynamic_slice_in_dim(top_own, top_start % chunk, top_count, 0)
    sent = back_apply(place, low_inverse, gap, 1)
    back_top = call(
        functools.partial(leaf_back_top_kernel, size),
        place,
        NEAR // group,
        [in_steps(group, (columns, chunk))] * 2
        + [leaf_block(1, group, 0), leaf_block(1, group, 1), whole(tiles.shape)],
        [out_whole((columns, local_rows), F32)],
        [spread],
        [*rounded, coupling, coupling, tiles],
        leaf_flops,
        leaf_moved,
    )[0]
    path = reduce_and_gather(place, sent, low_far, False, True)
    group = 4
    total = pltpu.VMEM((columns, local_rows), F32)
    result = back_top
    for flip in range(2):
        last = [forward_leaf, inverse_t] if flip else []
        result = call(
            functools.partial(leaf_back_kernel, flip, size),
            place,
            NEAR // group,
            [
                leaf_block(0, group, flip),
                whole(tiles.shape),
                in_steps(group, (columns, chunk)),
                whole(back_top.shape),
            ]
            + [whole(a.shape) for a in last],
            [out_whole((local_rows, columns) if flip else (columns, local_rows), F32)],
            [total, spread],
            [coupling, tiles, path[flip], result, *last],
            leaf_flops // 2,
            leaf_moved // 2,
        )[0]
    return result, top_solution


def solution(mesh):
    return jax.shard_map(
        body,
        mesh=mesh,
        in_specs=(
            P(("leaf", "sep"), None),
            P(("leaf", "sep"), None),
            P(None, None, ("leaf", "sep")),
            P(None, None, ("leaf", "sep")),
            P(("leaf", "sep"), None),
            P(("leaf", "sep"), None),
            P(("leaf", "sep"), None),
            P(("leaf", "sep"), None),
            P(None, ("leaf", "sep")),
        ),
        out_specs=(P(("leaf", "sep"), None), P(("leaf", "sep"), None)),
        check_vma=False,
    )
```

```python
import functools

import jax
import jax.numpy as jnp
from jax import lax
from jax.experimental import pallas as pl
from jax.experimental.pallas import tpu as pltpu
from jax.sharding import PartitionSpec as P

PRECISE = lax.Precision.HIGHEST
F32 = jnp.float32
BF16 = jnp.bfloat16
I16 = jnp.int16
AXES = ("leaf", "sep")
NEAR = 8
GROUP = 2 * NEAR
BATCHES = ((4, 4), (0, 4))
PIECES = ((0, 1), (6, 2), (4, 2), (1, 3))
PAD = 16
VMEM = 24 << 20


def swap(block, offset):
    count = lax.axis_size("leaf") * lax.axis_size("sep")
    return lax.ppermute(block, AXES, [(at, at ^ offset) for at in range(count)])


def encode(value):
    peak = jnp.maximum(jnp.max(jnp.abs(value), axis=0, keepdims=True), 1e-30)
    power = jnp.ceil(jnp.log2(peak))
    part = jnp.ceil(peak * jnp.exp2(14.0 - power))
    scale = 32767.0 / (part * jnp.exp2(power - 14.0))
    code = jnp.floor(value * scale + 0.5).astype(jnp.int32).astype(I16)
    row = lax.broadcasted_iota(jnp.int32, (PAD, value.shape[1]), 0)
    return code, jnp.where(row == 0, power, part).astype(jnp.int32).astype(I16)


def put(ref, coded):
    code, head = coded
    rows = code.shape[0]
    ref[:rows, :] = code
    ref[rows:, :] = head


def decode(block):
    rows = block.shape[0] - PAD
    head = block[rows:, :].astype(jnp.int32).astype(F32)
    scale = head[1:2, :] * jnp.exp2(head[0:1, :] - 14.0) * (1.0 / 32767.0)
    return block[:rows, :].astype(jnp.int32).astype(F32) * scale


def halves(value):
    high = value.astype(BF16)
    return high, (value - high.astype(F32)).astype(BF16)


def dot(left, right):
    return jnp.dot(left, right, preferred_element_type=F32)


def spread_tiles(tiles, level, width, size):
    across = tiles.shape[0]
    flags = tiles[:, level, :].astype(F32).T
    lane = lax.broadcasted_iota(jnp.int32, (flags.shape[0], width), 1) // size
    spread = jnp.zeros((flags.shape[0], width), F32)
    for at in range(across):
        spread = jnp.where(lane == at, flags[:, at : at + 1], spread)
    return spread


def masked(block, spread, chunk, size):
    width = block.shape[1]
    count = block.shape[0] // size
    flags = spread[pl.ds(pl.multiple_of(chunk * count, count), count), :]
    parts = []
    for at in range(count):
        row = jnp.broadcast_to(flags[at : at + 1, :], (16, width)).astype(BF16)
        tile = block[at * size : (at + 1) * size, :].reshape(size // 16, 16, width)
        parts.append((tile * row[None]).reshape(size, width))
    return jnp.concatenate(parts, 0)


def triangular(block, row_start, column_start):
    row = lax.broadcasted_iota(jnp.int32, block.shape, 0) + row_start
    column = lax.broadcasted_iota(jnp.int32, block.shape, 1) + column_start
    return jnp.where(row >= column, block, 0.0)


def with_rows(value, chunk, start, rhs):
    count = rhs.shape[0]
    parts = []
    for at in range(value.shape[0] // count):
        here = (start == chunk * value.shape[0] + at * count).astype(F32)
        parts.append(value[at * count : (at + 1) * count, :] + rhs[...] * here)
    return jnp.concatenate(parts, 0) if len(parts) > 1 else parts[0]


def call(kernel, place, steps, ins, outs, scratch, args, flops, moved):
    return pl.pallas_call(
        kernel,
        grid_spec=pltpu.PrefetchScalarGridSpec(
            num_scalar_prefetch=1,
            grid=(steps,),
            in_specs=ins,
            out_specs=[spec for spec, _ in outs],
            scratch_shapes=scratch,
        ),
        out_shape=[shape for _, shape in outs],
        compiler_params=pltpu.CompilerParams(vmem_limit_bytes=VMEM),
        cost_estimate=pl.CostEstimate(flops=flops, bytes_accessed=moved, transcendentals=0),
    )(place, *args)


def whole(shape):
    return pl.BlockSpec(shape, lambda *_: (0,) * len(shape))


def out_whole(shape, dtype):
    return whole(shape), jax.ShapeDtypeStruct(shape, dtype)


def in_steps(count, shape, dtype=None, entries=0):
    spec = pl.BlockSpec((count, *shape), lambda k, p: (k,) + (0,) * len(shape))
    return spec if dtype is None else (spec, jax.ShapeDtypeStruct((entries, *shape), dtype))


def at_rest(array):
    return pltpu.with_memory_space_constraint(array, pltpu.HBM)


def chunk_at(step, place, flip):
    return ((place[1] ^ step) << 1) | (place[0] ^ flip)


def steps_of(first, at, per):
    return first + pl.program_id(0) * per + at


def over(shape, index):
    def spec(first, at, per, flip):
        return pl.BlockSpec(shape, lambda k, p: index(chunk_at(first + k * per + at, p, flip)))

    return spec


def emit(first, per, at, outs, value):
    coded = encode(value)
    for step in range(len(outs) // per):
        where = step * per + at

        @pl.when(pl.program_id(0) == step)
        def _(where=where):
            if first + where == 0:
                outs[where][...] = value
            else:
                put(outs[where], coded)


def reduced(place, kernel, specs, args, shape, scratch, flops, moved):
    coded = (shape[0] + PAD, shape[1])
    per = 2
    received = {}
    for first, count in BATCHES:
        outs = call(
            functools.partial(kernel, 1, first, per),
            place,
            count // per,
            specs(first, per, 1),
            [in_steps(per, coded, I16, count)],
            scratch,
            args(1),
            flops,
            moved,
        )
        received[first] = swap(outs[0], 1)
    kept = [None] * NEAR
    for first, count in BATCHES:
        kept[first : first + count] = call(
            functools.partial(kernel, 0, first, per),
            place,
            count // per,
            specs(first, per, 0) + [in_steps(per, coded)],
            [
                out_whole(shape, F32) if at == 0 else out_whole(coded, I16)
                for at in range(first, first + count)
            ],
            scratch,
            args(0) + [received[first]],
            flops,
            moved,
        )
    return kept


def leaf_kernel(size, place, leaf_rhs, inverse_t, forward, rounded):
    inverse = inverse_t[...].T
    for at in range(leaf_rhs.shape[0] // size):
        rows = slice(at * size, (at + 1) * size)
        block = triangular(inverse[rows, :], 0, 0)
        value = jnp.dot(block, leaf_rhs[rows, :], precision=PRECISE, preferred_element_type=F32)
        forward[rows, :] = value
        rounded[rows, :] = value.astype(BF16)


def leaf_low_kernel(size, flip, first, per, place, *rest):
    blocks, (rounded, tiles, rhs), rest = rest[:per], rest[per : per + 3], rest[per + 3 :]
    spread = rest[-1]

    @pl.when(pl.program_id(0) == 0)
    def _():
        spread[...] = spread_tiles(tiles, 0, spread.shape[1], size)

    for at in range(per):
        chunk = chunk_at(steps_of(first, at, per), place, flip)
        value = -dot(masked(blocks[at][0, 0], spread, chunk, size), rounded[...])
        value = with_rows(value, chunk, place[2], rhs)
        if flip:
            put(rest[0].at[at], encode(value))
        else:
            emit(first, per, at, rest[1:-1], value + decode(rest[0][at]))


def leaf_top_kernel(size, place, rounded, coupling, tiles, part, spread):
    group = coupling.shape[1]

    @pl.when(pl.program_id(0) == 0)
    def _():
        spread[...] = spread_tiles(tiles, 1, spread.shape[1], size)

    for at in range(group):
        chunk = pl.program_id(0) * group + at
        part[at] = dot(masked(coupling[0, at], spread, chunk, size), rounded[...])


def sum_kernel(final, waits, place, own, *rest):
    blocks, out = rest[: len(rest) - 1 - waits], rest[-1]
    value = own[...] if own.dtype == F32 else decode(own[...])
    for block in blocks:
        value = value + decode(block[...])
    if final:
        out[...] = value.astype(BF16)
    else:
        put(out, encode(value))


def summed(place, own, received, final, before=()):
    rows, columns = received[0].shape
    return call(
        functools.partial(sum_kernel, final, len(before)),
        place,
        1,
        [whole(own.shape)]
        + [whole(r.shape) for r in received]
        + [pl.BlockSpec(memory_space=pl.ANY) for _ in before],
        [out_whole((rows - PAD if final else rows, columns), BF16 if final else I16)],
        [],
        [own, *received, *before],
        rows * columns * 8,
        rows * columns * 20,
    )[0]


def reduce_and_gather(place, kept, far, final=False, before=()):
    received = [swap(kept[at], at << 1) for at in range(NEAR - 1, 0, -1)]
    coded = summed(place, kept[0], received, final and not far, before)
    if far:
        coded = summed(place, coded, [swap(coded, offset) for offset in far], final)
    mine = [coded] + [None] * (NEAR - 1)
    for at in range(NEAR - 1, 0, -1):
        mine[at] = swap(coded, at << 1)
    return [(block, swap(block, 1)) for block in mine]


def pieces(place, kernel, spec, args, chunks, outs, scratch, before, flops, moved):
    stacks = []
    for number, (first, count) in enumerate(PIECES):
        last = number == len(PIECES) - 1
        blocks = [block for pair in chunks[first : first + count] for block in pair]
        more = args(last)
        result = call(
            functools.partial(kernel, first, count, last),
            place,
            count,
            [spec(first, 0, 1, flip) for flip in range(2)]
            + [whole(b.shape) for b in blocks]
            + [whole(b.shape) for b in before]
            + [whole(a.shape) for a in more[2:]],
            outs(count, last),
            scratch,
            more[:2] + blocks + before + more[2:],
            flops * count // NEAR,
            moved * count // NEAR,
        )
        keep = len(before) if before else 1
        before, stacks = list(result[:keep]), stacks + list(result[keep:])
    return before, stacks


def in_turn(count, blocks, work):
    for step in range(count):

        @pl.when(pl.program_id(0) == step)
        def _(step=step):
            for flip in range(2):
                work(step, flip, blocks[2 * step + flip])


def factor_kernel(start_at, first, count, last, place, near, far, *rest):
    blocks, rest = rest[: 2 * count], rest[2 * count :]
    before, rest = (rest[0], rest[1:]) if first else (None, rest)
    out, wide, narrow = rest[0], rest[-2], rest[-1]
    rows, depth = near.shape
    columns = narrow.shape[1]
    start = place[start_at]

    @pl.when(pl.program_id(0) == 0)
    def _():
        wide[...] = jnp.zeros_like(wide)
        narrow[...] = jnp.zeros_like(narrow)

    def work(step, flip, block):
        chunk = chunk_at(first + step, place, flip)

        @pl.when(chunk * depth < start + rows)
        def _():
            high, low = halves(triangular((near, far)[flip][...], start, chunk * depth))
            upper, lower = halves(decode(block[...]))
            wide[...] += dot(high, jnp.concatenate([upper, lower], 1))
            narrow[...] += dot(low, upper)

    in_turn(count, blocks, work)

    @pl.when(pl.program_id(0) == count - 1)
    def _():
        value = wide[:, :columns] + wide[:, columns:] + narrow[...]
        if before is not None:
            value = value + before[...]
        out[...] = value
        if last:
            rest[1][...] = value.T


def factor_apply(place, factor, chunks, start_at):
    count, size = factor.shape
    depth = size // GROUP
    columns = chunks[0][0].shape[1]
    held = at_rest(factor)

    def outs(_, last):
        return [out_whole((count, columns), F32)] + [out_whole((columns, count), F32)] * last

    rows, turned = pieces(
        place,
        functools.partial(factor_kernel, start_at),
        over((count, depth), lambda chunk: (0, chunk)),
        lambda last: [held, held],
        chunks,
        outs,
        [pltpu.VMEM((count, 2 * columns), F32), pltpu.VMEM((count, columns), F32)],
        [],
        8 * count * size * columns,
        4 * count * size,
    )
    return rows[0], turned[0]


def coupled_kernel(flip, first, per, place, *rest):
    couplings, parts, rest = rest[:per], rest[per : 2 * per], rest[2 * per :]
    rows, rhs, packed = rest[0], rest[1], rest[-1]
    columns = rows.shape[1]

    @pl.when(pl.program_id(0) == 0)
    def _():
        high, low = halves(rows[...])
        packed[:, :columns] = high
        packed[:, columns:] = low

    for at in range(per):
        chunk = chunk_at(steps_of(first, at, per), place, flip)
        high, low = halves(couplings[at][0])
        product = dot(high, packed[...])
        value = product[:, :columns] + product[:, columns:] + dot(low, packed[:, :columns])
        value = with_rows(-(parts[at][0] + value), chunk, place[3], rhs)
        if flip:
            put(rest[2].at[at], encode(value))
        else:
            emit(first, per, at, rest[3:-1], value + decode(rest[2][at]))


def back_kernel(start_at, flip, first, per, place, *rest):
    factors, vector, rest = rest[:per], rest[per], rest[per + 1 :]
    packed = rest[-1]
    columns = vector.shape[0]

    @pl.when(pl.program_id(0) == 0)
    def _():
        high, low = halves(vector[...])
        packed[:columns, :] = high
        packed[columns:, :] = low

    for at in range(per):
        chunk = chunk_at(steps_of(first, at, per), place, flip)
        depth = factors[at].shape[1]
        high, low = halves(triangular(factors[at][...], place[start_at], chunk * depth))
        product = dot(packed[...], high)
        value = product[:columns, :] + product[columns:, :] + dot(packed[:columns, :], low)
        if flip:
            put(rest[0].at[at], encode(value))
        else:
            emit(first, per, at, rest[1:-1], value + decode(rest[0][at]))


def back_apply(place, factor, vector, start_at):
    count, size = factor.shape
    columns = vector.shape[0]
    chunk = size // GROUP
    block = over((count, chunk), lambda c: (0, c))

    def specs(first, per, flip):
        return [block(first, at, per, flip) for at in range(per)] + [whole(vector.shape)]

    return reduced(
        place,
        functools.partial(back_kernel, start_at),
        specs,
        lambda flip: [at_rest(factor)] * 2 + [vector],
        (columns, chunk),
        [pltpu.VMEM((2 * columns, count), BF16)],
        2 * count * size * columns,
        count * size,
    )


def carry_kernel(first, count, last, place, near, far, *rest):
    blocks, rest = rest[: 2 * count], rest[2 * count :]
    before, own_before, gap, own, rounded, wide, narrow = rest
    columns = before.shape[0]

    @pl.when(pl.program_id(0) == 0)
    def _():
        wide[...] = jnp.zeros_like(wide)
        narrow[...] = jnp.zeros_like(narrow)
        own[...] = own_before[...]

    def work(step, flip, block):
        value = decode(block[...])
        upper, lower = halves(value)
        rounded[0, flip] = upper
        high, low = halves((near, far)[flip][0])
        wide[...] += dot(jnp.concatenate([upper, lower], 0), high)
        narrow[...] += dot(upper, low)

        @pl.when(chunk_at(first + step, place, flip) == place[3] // value.shape[1])
        def _():
            own[...] = value

    in_turn(count, blocks, work)

    @pl.when(pl.program_id(0) == count - 1)
    def _():
        gap[...] = before[...] - (wide[:columns, :] + wide[columns:, :] + narrow[...])


def leaf_back_top_kernel(size, place, near, far, tiles, *rest):
    stacks, out, spread = rest[:-2], rest[-2], rest[-1]

    @pl.when(pl.program_id(0) == 0)
    def _():
        spread[...] = spread_tiles(tiles, 1, spread.shape[1], size)
        out[...] = jnp.zeros_like(out)

    for (first, count), stack in zip(PIECES, stacks):
        for at in range(count):

            @pl.when(pl.program_id(0) == first + at)
            def _(step=first + at, at=at, stack=stack):
                for flip in range(2):
                    chunk = chunk_at(step, place, flip)
                    block = masked((near, far)[flip][0, 0], spread, chunk, size)
                    out[...] += dot(stack[at, flip], block)


def leaf_back_kernel(size, first, count, last, place, near, far, *rest):
    blocks, rest = rest[: 2 * count], rest[2 * count :]
    before, tiles = rest[:2]
    out, total, spread = rest[-3:]

    @pl.when(pl.program_id(0) == 0)
    def _():
        spread[...] = spread_tiles(tiles, 0, spread.shape[1], size)
        total[...] = before[...]

    def work(step, flip, block):
        chunk = chunk_at(first + step, place, flip)
        total[...] += dot(block[...], masked((near, far)[flip][0, 0], spread, chunk, size))

    in_turn(count, blocks, work)

    @pl.when(pl.program_id(0) == count - 1)
    def _():
        if not last:
            out[...] = total[...]
        else:
            forward, inverse_t = rest[2:4]
            gap = forward[...] - total[...].T
            inverse = inverse_t[...].T
            for at in range(gap.shape[0] // size):
                rows = slice(at * size, (at + 1) * size)
                block = triangular(inverse[rows, :], 0, 0).T
                out[rows, :] = jnp.dot(
                    block, gap[rows, :], precision=PRECISE, preferred_element_type=F32
                )


def body(
    leaf_rhs,
    leaf_inverse,
    leaf_coupling,
    tile_mask,
    low_rhs,
    top_rhs,
    low_inverse,
    top_inverse,
    low_coupling,
):
    device_total = lax.axis_size("leaf") * lax.axis_size("sep")
    device = lax.axis_index("leaf") * lax.axis_size("sep") + lax.axis_index("sep")
    local_rows, columns = leaf_rhs.shape
    size = leaf_inverse.shape[1]
    levels = leaf_coupling.shape[0]
    sep_size = low_inverse.shape[1]
    low_count = low_inverse.shape[0]
    top_count = top_inverse.shape[0]
    chunk = sep_size // GROUP
    low_far = list(range(GROUP, device_total // 2, GROUP))
    top_far = list(range(GROUP, device_total, GROUP))
    low_start = device % (device_total // 2) * low_count
    top_start = device * top_count
    place = jnp.stack([device % 2, device % GROUP // 2, low_start, top_start]).astype(jnp.int32)

    inverse_t = at_rest(leaf_inverse.T)
    tiles = at_rest(jnp.transpose(tile_mask, (2, 0, 1)))
    coupling = at_rest(leaf_coupling.reshape(levels, GROUP, chunk, local_rows))
    low_blocks = at_rest(low_coupling.reshape(GROUP, chunk, low_count))
    low_rhs, top_rhs = at_rest(low_rhs), at_rest(top_rhs)

    spread = pltpu.VMEM((sep_size // size, local_rows), F32)
    leaf_flops = 2 * sep_size * local_rows * columns
    leaf_moved = 2 * sep_size * local_rows
    leaf_low = over((1, 1, chunk, local_rows), lambda c: (0, c, 0, 0))
    leaf_top = over((1, 1, chunk, local_rows), lambda c: (1, c, 0, 0))

    forward_leaf, rounded_leaf = call(
        functools.partial(leaf_kernel, size),
        place,
        1,
        [whole(leaf_rhs.shape), whole(inverse_t.shape)],
        [out_whole(leaf_rhs.shape, F32), out_whole(leaf_rhs.shape, BF16)],
        [],
        [at_rest(leaf_rhs), inverse_t],
        2 * local_rows * size * columns,
        8 * local_rows * columns,
    )

    def leaf_specs(first, per, flip):
        return [leaf_low(first, at, per, flip) for at in range(per)] + [
            whole(rounded_leaf.shape),
            whole(tiles.shape),
            whole(low_rhs.shape),
        ]

    kept = reduced(
        place,
        functools.partial(leaf_low_kernel, size),
        leaf_specs,
        lambda flip: [coupling] * 2 + [rounded_leaf, tiles, low_rhs],
        (chunk, columns),
        [spread],
        leaf_flops // 4,
        leaf_moved // 4,
    )
    group = 4
    part = call(
        functools.partial(leaf_top_kernel, size),
        place,
        GROUP // group,
        [
            whole(rounded_leaf.shape),
            pl.BlockSpec((1, group, chunk, local_rows), lambda k, p: (1, k, 0, 0)),
            whole(tiles.shape),
        ],
        [in_steps(group, (chunk, columns), F32, GROUP)],
        [spread],
        [rounded_leaf, coupling, tiles],
        leaf_flops,
        leaf_moved,
    )[0]
    first_input = reduce_and_gather(place, kept, low_far, before=[part])
    first_rows, first_columns = factor_apply(place, low_inverse, first_input, 2)

    coupled_flops = 8 * sep_size * low_count * columns
    coupled_moved = 4 * sep_size * low_count
    low_block = over((1, chunk, low_count), lambda c: (c, 0, 0))
    part_block = over((1, chunk, columns), lambda c: (c, 0, 0))

    def coupled_specs(first, per, flip):
        return (
            [low_block(first, at, per, flip) for at in range(per)]
            + [part_block(first, at, per, flip) for at in range(per)]
            + [whole(first_rows.shape), whole(top_rhs.shape)]
        )

    kept = reduced(
        place,
        coupled_kernel,
        coupled_specs,
        lambda flip: [low_blocks] * 2 + [part] * 2 + [first_rows, top_rhs],
        (chunk, columns),
        [pltpu.VMEM((low_count, 2 * columns), BF16)],
        coupled_flops // 4,
        coupled_moved // 4,
    )
    top_input = reduce_and_gather(place, kept, top_far)
    _, forward_columns = factor_apply(place, top_inverse, top_input, 3)

    kept = back_apply(place, top_inverse, forward_columns, 3)
    solution_blocks = reduce_and_gather(place, kept, top_far)
    turned = (columns, chunk)
    (gap, own), rounded = pieces(
        place,
        carry_kernel,
        low_block,
        lambda last: [low_blocks] * 2,
        solution_blocks,
        lambda count, last: [
            out_whole(first_columns.shape, F32),
            out_whole(turned, F32),
            (
                pl.BlockSpec((1, 2, *turned), lambda k, p: (k, 0, 0, 0)),
                jax.ShapeDtypeStruct((count, 2, *turned), BF16),
            ),
        ],
        [pltpu.VMEM((2 * columns, low_count), F32), pltpu.VMEM((columns, low_count), F32)],
        [first_columns, jnp.zeros(turned, F32)],
        coupled_flops,
        coupled_moved,
    )
    top_solution = lax.dynamic_slice_in_dim(own, top_start % chunk, top_count, 1).T
    kept = back_apply(place, low_inverse, gap, 2)
    back_top = call(
        functools.partial(leaf_back_top_kernel, size),
        place,
        NEAR,
        [leaf_top(0, 0, 1, flip) for flip in range(2)]
        + [whole(tiles.shape)]
        + [whole(r.shape) for r in rounded],
        [out_whole((columns, local_rows), F32)],
        [spread],
        [coupling, coupling, tiles, *rounded],
        leaf_flops,
        leaf_moved,
    )[0]
    path = reduce_and_gather(place, kept, low_far, True, [back_top])
    (interior,), _ = pieces(
        place,
        functools.partial(leaf_back_kernel, size),
        leaf_low,
        lambda last: [coupling, coupling, tiles] + [forward_leaf, inverse_t] * last,
        path,
        lambda count, last: [
            out_whole((local_rows, columns) if last else (columns, local_rows), F32)
        ],
        [pltpu.VMEM((columns, local_rows), F32), spread],
        [back_top],
        leaf_flops,
        leaf_moved,
    )
    return interior, top_solution


def solution(mesh):
    return jax.shard_map(
        body,
        mesh=mesh,
        in_specs=(
            P(("leaf", "sep"), None),
            P(("leaf", "sep"), None),
            P(None, None, ("leaf", "sep")),
            P(None, None, ("leaf", "sep")),
            P(("leaf", "sep"), None),
            P(("leaf", "sep"), None),
            P(("leaf", "sep"), None),
            P(("leaf", "sep"), None),
            P(None, ("leaf", "sep")),
        ),
        out_specs=(P(("leaf", "sep"), None), P(("leaf", "sep"), None)),
        check_vma=False,
    )
```

```python
import functools

import jax
import jax.numpy as jnp
from jax import lax
from jax.experimental import pallas as pl
from jax.experimental.pallas import tpu as pltpu
from jax.sharding import PartitionSpec as P

PRECISE = lax.Precision.HIGHEST
F32 = jnp.float32
BF16 = jnp.bfloat16
I16 = jnp.int16
AXES = ("leaf", "sep")
NEAR = 8
GROUP = 2 * NEAR
BATCHES = ((4, 4), (0, 4))
PAD = 16
VMEM = 24 << 20


def swap(block, offset):
    count = lax.axis_size("leaf") * lax.axis_size("sep")
    return lax.ppermute(block, AXES, [(at, at ^ offset) for at in range(count)])


def encode(value):
    peak = jnp.maximum(jnp.max(jnp.abs(value), axis=0, keepdims=True), 1e-30)
    power = jnp.ceil(jnp.log2(peak))
    part = jnp.ceil(peak * jnp.exp2(14.0 - power))
    scale = 32767.0 / (part * jnp.exp2(power - 14.0))
    code = jnp.floor(value * scale + 0.5).astype(jnp.int32).astype(I16)
    row = lax.broadcasted_iota(jnp.int32, (PAD, value.shape[1]), 0)
    return code, jnp.where(row == 0, power, part).astype(jnp.int32).astype(I16)


def put(ref, coded):
    code, head = coded
    rows = code.shape[0]
    ref[:rows, :] = code
    ref[rows:, :] = head


def decode(block):
    rows = block.shape[0] - PAD
    head = block[rows:, :].astype(jnp.int32).astype(F32)
    scale = head[1:2, :] * jnp.exp2(head[0:1, :] - 14.0) * (1.0 / 32767.0)
    return block[:rows, :].astype(jnp.int32).astype(F32) * scale


def halves(value):
    high = value.astype(BF16)
    return high, (value - high.astype(F32)).astype(BF16)


def dot(left, right):
    return jnp.dot(left, right, preferred_element_type=F32)


def spread_tiles(tiles, level, width, size):
    across = tiles.shape[0]
    flags = tiles[:, level, :].astype(F32).T
    lane = lax.broadcasted_iota(jnp.int32, (flags.shape[0], width), 1) // size
    spread = jnp.zeros((flags.shape[0], width), F32)
    for at in range(across):
        spread = jnp.where(lane == at, flags[:, at : at + 1], spread)
    return spread


def masked(block, spread, chunk, size):
    width = block.shape[1]
    count = block.shape[0] // size
    flags = spread[0, pl.ds(pl.multiple_of(chunk * count, count), count), :]
    parts = []
    for at in range(count):
        row = jnp.broadcast_to(flags[at : at + 1, :], (16, width)).astype(BF16)
        tile = block[at * size : (at + 1) * size, :].reshape(size // 16, 16, width)
        parts.append((tile * row[None]).reshape(size, width))
    return jnp.concatenate(parts, 0)


def triangular(block, row_start, column_start):
    row = lax.broadcasted_iota(jnp.int32, block.shape, 0) + row_start
    column = lax.broadcasted_iota(jnp.int32, block.shape, 1) + column_start
    return jnp.where(row >= column, block, 0.0)


def with_rows(value, chunk, start, rhs):
    count = rhs.shape[0]
    parts = []
    for at in range(value.shape[0] // count):
        here = (start == chunk * value.shape[0] + at * count).astype(F32)
        parts.append(value[at * count : (at + 1) * count, :] + rhs[...] * here)
    return jnp.concatenate(parts, 0) if len(parts) > 1 else parts[0]


def call(kernel, place, steps, ins, outs, scratch, args, flops, moved):
    return pl.pallas_call(
        kernel,
        grid_spec=pltpu.PrefetchScalarGridSpec(
            num_scalar_prefetch=1,
            grid=(steps,),
            in_specs=ins,
            out_specs=[spec for spec, _ in outs],
            scratch_shapes=scratch,
        ),
        out_shape=[shape for _, shape in outs],
        compiler_params=pltpu.CompilerParams(vmem_limit_bytes=VMEM),
        cost_estimate=pl.CostEstimate(flops=flops, bytes_accessed=moved, transcendentals=0),
    )(place, *args)


def whole(shape):
    return pl.BlockSpec(shape, lambda *_: (0,) * len(shape))


def out_whole(shape, dtype):
    return whole(shape), jax.ShapeDtypeStruct(shape, dtype)


def in_steps(count, shape, dtype=None, entries=0):
    spec = pl.BlockSpec((count, *shape), lambda k, p: (k,) + (0,) * len(shape))
    return spec if dtype is None else (spec, jax.ShapeDtypeStruct((entries, *shape), dtype))


def at_rest(array):
    return pltpu.with_memory_space_constraint(array, pltpu.HBM)


def chunk_at(step, place, flip):
    return ((place[1] ^ step) << 1) | (place[0] ^ flip)


def steps_of(first, at, per):
    return first + pl.program_id(0) * per + at


def over(shape, index):
    def spec(first, at, per, flip):
        return pl.BlockSpec(shape, lambda k, p: index(chunk_at(first + k * per + at, p, flip)))

    return spec


def emit(first, per, at, outs, value):
    coded = encode(value)
    for step in range(len(outs) // per):
        where = step * per + at

        @pl.when(pl.program_id(0) == step)
        def _(where=where):
            if first + where == 0:
                outs[where][...] = value
            else:
                put(outs[where], coded)


def reduced(place, kernel, specs, args, shape, scratch, flops, moved, per, received=None):
    coded = (shape[0] + PAD, shape[1])
    if received is None:
        sent = call(
            functools.partial(kernel, 1, 0, per),
            place,
            NEAR // per,
            specs(0, per, 1),
            [in_steps(per, coded, I16, NEAR)],
            scratch,
            args,
            flops // 2,
            moved // 2,
        )
        received = swap(sent[0], 1)
    kept = [None] * NEAR
    for first, count in BATCHES:
        kept[first : first + count] = call(
            functools.partial(kernel, 0, first, per),
            place,
            count // per,
            specs(first, per, 0)
            + [
                pl.BlockSpec(
                    (per, *coded), lambda k, p, first=first: (first // per + k, 0, 0)
                )
            ],
            [
                out_whole(shape, F32) if at == 0 else out_whole(coded, I16)
                for at in range(first, first + count)
            ],
            scratch,
            [*args, received],
            flops // 4,
            moved // 4,
        )
    return kept


def leaf_low_value(size, chunk, place, block, spread, rounded, rhs):
    value = -dot(masked(block[0, 0], spread, chunk, size), rounded[...])
    return with_rows(value, chunk, place[2], rhs)


def leaf_send_kernel(size, per, place, *rest):
    blocks, (leaf_rhs, inverse_t, tiles, rhs) = rest[:per], rest[per : per + 4]
    sent, forward, rounded, spread = rest[per + 4 :]

    @pl.when(pl.program_id(0) == 0)
    def _():
        inverse = inverse_t[...].T
        for at in range(leaf_rhs.shape[0] // size):
            rows = slice(at * size, (at + 1) * size)
            block = triangular(inverse[rows, :], 0, 0)
            value = jnp.dot(block, leaf_rhs[rows, :], precision=PRECISE, preferred_element_type=F32)
            forward[rows, :] = value
            rounded[rows, :] = value.astype(BF16)
        for level in range(spread.shape[0]):
            spread[level] = spread_tiles(tiles, level, spread.shape[2], size)

    for at in range(per):
        chunk = chunk_at(steps_of(0, at, per), place, 1)
        value = leaf_low_value(size, chunk, place, blocks[at], spread, rounded, rhs)
        put(sent.at[at], encode(value))


def leaf_keep_kernel(size, flip, first, per, place, *rest):
    blocks, (spread, rounded, rhs, received) = rest[:per], rest[per : per + 4]
    for at in range(per):
        chunk = chunk_at(steps_of(first, at, per), place, flip)
        value = leaf_low_value(size, chunk, place, blocks[at], spread, rounded, rhs)
        emit(first, per, at, rest[per + 4 :], value + decode(received[at]))


def leaf_top_kernel(size, place, spread, rounded, coupling, part):
    group = coupling.shape[1]
    for at in range(group):
        chunk = pl.program_id(0) * group + at
        part[at] = dot(masked(coupling[0, at], spread, chunk, size), rounded[...])


def sum_kernel(final, waits, place, own, *rest):
    blocks, out = rest[: len(rest) - 1 - waits], rest[-1]
    value = own[...] if own.dtype == F32 else decode(own[...])
    for block in blocks:
        value = value + decode(block[...])
    if final:
        out[...] = value.astype(BF16)
    else:
        put(out, encode(value))


def summed(place, own, received, final, before=()):
    rows, columns = received[0].shape
    return call(
        functools.partial(sum_kernel, final, len(before)),
        place,
        1,
        [whole(own.shape)]
        + [whole(r.shape) for r in received]
        + [pl.BlockSpec(memory_space=pl.ANY) for _ in before],
        [out_whole((rows - PAD if final else rows, columns), BF16 if final else I16)],
        [],
        [own, *received, *before],
        rows * columns * 8,
        rows * columns * 20,
    )[0]


def reduce_and_gather(place, kept, far, final=False, before=()):
    received = [swap(kept[at], at << 1) for at in range(NEAR - 1, 0, -1)]
    coded = summed(place, kept[0], received, final and not far, before)
    if far:
        coded = summed(place, coded, [swap(coded, offset) for offset in far], final)
    mine = [coded] + [None] * (NEAR - 1)
    for at in range(NEAR - 1, 0, -1):
        mine[at] = swap(coded, at << 1)
    mine = jnp.stack(mine)
    return mine, swap(mine, 1)


def factor_kernel(start_at, flip, per, place, *rest):
    factors, stack, rest = rest[:per], rest[per], rest[per + 1 :]
    before, rest = (rest[0], rest[1:]) if flip else (None, rest)
    out, wide, narrow = rest[0], rest[-2], rest[-1]
    depth = factors[0].shape[1]
    columns = narrow.shape[1]

    @pl.when(pl.program_id(0) == 0)
    def _():
        wide[...] = jnp.zeros_like(wide)
        narrow[...] = jnp.zeros_like(narrow)

    @pl.when(pl.program_id(0) >= 0)
    def _():
        highs, lows, uppers, lowers = [], [], [], []
        for at in range(per):
            chunk = chunk_at(steps_of(0, at, per), place, flip)
            high, low = halves(triangular(factors[at][...], place[start_at], chunk * depth))
            upper, lower = halves(decode(stack[at]))
            highs, lows = highs + [high], lows + [low]
            uppers, lowers = uppers + [upper], lowers + [lower]
        upper = jnp.concatenate(uppers, 0)
        both = jnp.concatenate([upper, jnp.concatenate(lowers, 0)], 1)
        wide[...] += dot(jnp.concatenate(highs, 1), both)
        narrow[...] += dot(jnp.concatenate(lows, 1), upper)

    @pl.when(pl.program_id(0) == pl.num_programs(0) - 1)
    def _():
        value = wide[:, :columns] + wide[:, columns:] + narrow[...]
        if flip:
            value = value + before[...]
            rest[1][...] = value.T
        out[...] = value


def factor_apply(place, factor, stacks, start_at):
    count, size = factor.shape
    depth = size // GROUP
    columns = stacks[0].shape[2]
    per = 2
    block = over((count, depth), lambda chunk: (0, chunk))
    result = ()
    for flip in range(2):
        result = call(
            functools.partial(factor_kernel, start_at, flip, per),
            place,
            NEAR // per,
            [block(0, at, per, flip) for at in range(per)]
            + [in_steps(per, stacks[flip].shape[1:])]
            + [whole(r.shape) for r in result],
            [out_whole((count, columns), F32)] + [out_whole((columns, count), F32)] * flip,
            [pltpu.VMEM((count, 2 * columns), F32), pltpu.VMEM((count, columns), F32)],
            [at_rest(factor)] * per + [stacks[flip], *result],
            4 * count * size * columns,
            2 * count * size,
        )
    return result


def coupled_kernel(flip, first, per, place, *rest):
    couplings, parts, rest = rest[:per], rest[per : 2 * per], rest[2 * per :]
    rows, rhs, packed = rest[0], rest[1], rest[-1]
    columns = rows.shape[1]

    @pl.when(pl.program_id(0) == 0)
    def _():
        high, low = halves(rows[...])
        packed[:, :columns] = high
        packed[:, columns:] = low

    for at in range(per):
        chunk = chunk_at(steps_of(first, at, per), place, flip)
        high, low = halves(couplings[at][0])
        product = dot(high, packed[...])
        value = product[:, :columns] + product[:, columns:] + dot(low, packed[:, :columns])
        value = with_rows(-(parts[at][0] + value), chunk, place[3], rhs)
        if flip:
            put(rest[2].at[at], encode(value))
        else:
            emit(first, per, at, rest[3:-1], value + decode(rest[2][at]))


def back_kernel(start_at, flip, first, per, place, *rest):
    factors, vector, rest = rest[:per], rest[per], rest[per + 1 :]
    packed = rest[-1]
    columns = vector.shape[0]

    @pl.when(pl.program_id(0) == 0)
    def _():
        high, low = halves(vector[...])
        packed[:columns, :] = high
        packed[columns:, :] = low

    for at in range(per):
        chunk = chunk_at(steps_of(first, at, per), place, flip)
        depth = factors[at].shape[1]
        high, low = halves(triangular(factors[at][...], place[start_at], chunk * depth))
        product = dot(packed[...], high)
        value = product[:columns, :] + product[columns:, :] + dot(packed[:columns, :], low)
        if flip:
            put(rest[0].at[at], encode(value))
        else:
            emit(first, per, at, rest[1:-1], value + decode(rest[0][at]))


def back_apply(place, factor, vector, start_at):
    count, size = factor.shape
    columns = vector.shape[0]
    chunk = size // GROUP
    block = over((count, chunk), lambda c: (0, c))
    per = 2

    def specs(first, per, flip):
        return [block(first, at, per, flip) for at in range(per)] + [whole(vector.shape)]

    return reduced(
        place,
        functools.partial(back_kernel, start_at),
        specs,
        [at_rest(factor)] * per + [vector],
        (columns, chunk),
        [pltpu.VMEM((2 * columns, count), BF16)],
        8 * count * size * columns,
        4 * count * size,
        per,
    )


def carry_kernel(flip, per, place, *rest):
    couplings, (stack, before, gap, rounded, wide, narrow) = rest[:per], rest[per:]
    columns = before.shape[0]

    @pl.when(pl.program_id(0) == 0)
    def _():
        wide[...] = jnp.zeros_like(wide)
        narrow[...] = jnp.zeros_like(narrow)

    @pl.when(pl.program_id(0) >= 0)
    def _():
        highs, lows, uppers, lowers = [], [], [], []
        for at in range(per):
            high, low = halves(couplings[at][0])
            upper, lower = halves(decode(stack[at]))
            rounded[at] = upper
            highs, lows = highs + [high], lows + [low]
            uppers, lowers = uppers + [upper], lowers + [lower]
        upper = jnp.concatenate(uppers, 1)
        both = jnp.concatenate([upper, jnp.concatenate(lowers, 1)], 0)
        wide[...] += dot(both, jnp.concatenate(highs, 0))
        narrow[...] += dot(upper, jnp.concatenate(lows, 0))

    @pl.when(pl.program_id(0) == pl.num_programs(0) - 1)
    def _():
        gap[...] = before[...] - (wide[:columns, :] + wide[columns:, :] + narrow[...])


def own_kernel(place, mine, other, out):
    chunk = place[3] // out.shape[0]
    here = (chunk % 2 == place[0]).astype(F32)
    out[...] = (decode(mine[0]) * here + decode(other[0]) * (1.0 - here)).T


def leaf_product(size, flip, per, place, blocks, spread, path):
    left, right = [], []
    for at in range(per):
        chunk = chunk_at(steps_of(0, at, per), place, flip)
        left.append(path[at])
        right.append(masked(blocks[at][0, 0], spread, chunk, size))
    return dot(jnp.concatenate(left, 1), jnp.concatenate(right, 0))


def leaf_back_top_kernel(size, per, place, *rest):
    near, far, (spread, mine, other, out) = rest[:per], rest[per : 2 * per], rest[2 * per :]

    @pl.when(pl.program_id(0) == 0)
    def _():
        out[...] = jnp.zeros_like(out)

    @pl.when(pl.program_id(0) >= 0)
    def _():
        out[...] += leaf_product(size, 0, per, place, near, spread, mine)
        out[...] += leaf_product(size, 1, per, place, far, spread, other)


def leaf_back_kernel(size, flip, per, place, *rest):
    blocks, (spread, path, before), rest = rest[:per], rest[per : per + 3], rest[per + 3 :]
    out, total = rest[-2:]

    @pl.when(pl.program_id(0) == 0)
    def _():
        total[...] = before[...]

    @pl.when(pl.program_id(0) >= 0)
    def _():
        total[...] += leaf_product(size, flip, per, place, blocks, spread, path)

    @pl.when(pl.program_id(0) == pl.num_programs(0) - 1)
    def _():
        if not flip:
            out[...] = total[...]
        else:
            forward, inverse_t = rest[:2]
            gap = forward[...] - total[...].T
            inverse = inverse_t[...].T
            for at in range(gap.shape[0] // size):
                rows = slice(at * size, (at + 1) * size)
                block = triangular(inverse[rows, :], 0, 0).T
                out[rows, :] = jnp.dot(
                    block, gap[rows, :], precision=PRECISE, preferred_element_type=F32
                )


def body(
    leaf_rhs,
    leaf_inverse,
    leaf_coupling,
    tile_mask,
    low_rhs,
    top_rhs,
    low_inverse,
    top_inverse,
    low_coupling,
):
    device_total = lax.axis_size("leaf") * lax.axis_size("sep")
    device = lax.axis_index("leaf") * lax.axis_size("sep") + lax.axis_index("sep")
    local_rows, columns = leaf_rhs.shape
    size = leaf_inverse.shape[1]
    levels = leaf_coupling.shape[0]
    sep_size = low_inverse.shape[1]
    low_count = low_inverse.shape[0]
    top_count = top_inverse.shape[0]
    chunk = sep_size // GROUP
    low_far = list(range(GROUP, device_total // 2, GROUP))
    top_far = list(range(GROUP, device_total, GROUP))
    low_start = device % (device_total // 2) * low_count
    top_start = device * top_count
    place = jnp.stack([device % 2, device % GROUP // 2, low_start, top_start]).astype(jnp.int32)

    inverse_t = at_rest(leaf_inverse.T)
    tiles = at_rest(jnp.transpose(tile_mask, (2, 0, 1)))
    coupling = at_rest(leaf_coupling.reshape(levels, GROUP, chunk, local_rows))
    low_blocks = at_rest(low_coupling.reshape(GROUP, chunk, low_count))
    low_rhs, top_rhs = at_rest(low_rhs), at_rest(top_rhs)

    leaf_flops = 2 * sep_size * local_rows * columns
    leaf_moved = 2 * sep_size * local_rows
    leaf_low = over((1, 1, chunk, local_rows), lambda c: (0, c, 0, 0))
    leaf_top = over((1, 1, chunk, local_rows), lambda c: (1, c, 0, 0))
    spread_shape = (levels, sep_size // size, local_rows)

    def spread_of(level):
        return pl.BlockSpec((1, *spread_shape[1:]), lambda k, p: (level, 0, 0))

    per = 4
    coded = (chunk + PAD, columns)
    sent, forward_leaf, rounded_leaf, spread = call(
        functools.partial(leaf_send_kernel, size, per),
        place,
        NEAR // per,
        [leaf_low(0, at, per, 1) for at in range(per)]
        + [whole(a.shape) for a in (leaf_rhs, inverse_t, tiles, low_rhs)],
        [
            in_steps(per, coded, I16, NEAR),
            out_whole(leaf_rhs.shape, F32),
            out_whole(leaf_rhs.shape, BF16),
            out_whole(spread_shape, F32),
        ],
        [],
        [coupling] * per + [at_rest(leaf_rhs), inverse_t, tiles, low_rhs],
        leaf_flops // 2,
        leaf_moved // 2,
    )

    def leaf_specs(first, per, flip):
        return [leaf_low(first, at, per, flip) for at in range(per)] + [
            spread_of(0),
            whole(rounded_leaf.shape),
            whole(low_rhs.shape),
        ]

    kept = reduced(
        place,
        functools.partial(leaf_keep_kernel, size),
        leaf_specs,
        [coupling] * per + [spread, rounded_leaf, low_rhs],
        (chunk, columns),
        [],
        leaf_flops,
        leaf_moved,
        per,
        swap(sent, 1),
    )
    part = call(
        functools.partial(leaf_top_kernel, size),
        place,
        GROUP // per,
        [
            spread_of(1),
            whole(rounded_leaf.shape),
            pl.BlockSpec((1, per, chunk, local_rows), lambda k, p: (1, k, 0, 0)),
        ],
        [in_steps(per, (chunk, columns), F32, GROUP)],
        [],
        [spread, rounded_leaf, coupling],
        leaf_flops,
        leaf_moved,
    )[0]
    first_input = reduce_and_gather(place, kept, low_far, before=[part])
    first_rows, first_columns = factor_apply(place, low_inverse, first_input, 2)

    coupled_flops = 8 * sep_size * low_count * columns
    coupled_moved = 4 * sep_size * low_count
    low_block = over((1, chunk, low_count), lambda c: (c, 0, 0))
    part_block = over((1, chunk, columns), lambda c: (c, 0, 0))
    per = 2

    def coupled_specs(first, per, flip):
        return (
            [low_block(first, at, per, flip) for at in range(per)]
            + [part_block(first, at, per, flip) for at in range(per)]
            + [whole(first_rows.shape), whole(top_rhs.shape)]
        )

    kept = reduced(
        place,
        coupled_kernel,
        coupled_specs,
        [low_blocks] * per + [part] * per + [first_rows, top_rhs],
        (chunk, columns),
        [pltpu.VMEM((low_count, 2 * columns), BF16)],
        coupled_flops,
        coupled_moved,
        per,
    )
    top_input = reduce_and_gather(place, kept, top_far)
    _, forward_columns = factor_apply(place, top_inverse, top_input, 3)

    kept = back_apply(place, top_inverse, forward_columns, 3)
    solution_blocks = reduce_and_gather(place, kept, top_far)
    turned = (columns, chunk)
    gap, rounded = first_columns, []
    for flip in range(2):
        gap, near = call(
            functools.partial(carry_kernel, flip, per),
            place,
            NEAR // per,
            [low_block(0, at, per, flip) for at in range(per)]
            + [in_steps(per, solution_blocks[flip].shape[1:]), whole(gap.shape)],
            [out_whole(gap.shape, F32), in_steps(per, turned, BF16, NEAR)],
            [pltpu.VMEM((2 * columns, low_count), F32), pltpu.VMEM((columns, low_count), F32)],
            [low_blocks] * per + [solution_blocks[flip], gap],
            coupled_flops // 2,
            coupled_moved // 2,
        )
        rounded.append(near)
    top_own = call(
        own_kernel,
        place,
        1,
        [
            pl.BlockSpec(
                (1, *s.shape[1:]), lambda k, p: ((p[3] // chunk // 2) ^ p[1], 0, 0)
            )
            for s in solution_blocks
        ],
        [out_whole((chunk, columns), F32)],
        [],
        list(solution_blocks),
        chunk * columns,
        8 * chunk * columns,
    )[0]
    top_solution = lax.dynamic_slice_in_dim(top_own, top_start % chunk, top_count, 0)
    kept = back_apply(place, low_inverse, gap, 2)
    back_top = call(
        functools.partial(leaf_back_top_kernel, size, per),
        place,
        NEAR // per,
        [leaf_top(0, at, per, flip) for flip in range(2) for at in range(per)]
        + [spread_of(1)]
        + [in_steps(per, turned)] * 2,
        [out_whole((columns, local_rows), F32)],
        [],
        [coupling] * (2 * per) + [spread, *rounded],
        leaf_flops,
        leaf_moved,
    )[0]
    path = reduce_and_gather(place, kept, low_far, True, [back_top, top_own])
    per = 4
    result = back_top
    for flip in range(2):
        last = [forward_leaf, inverse_t] if flip else []
        result = call(
            functools.partial(leaf_back_kernel, size, flip, per),
            place,
            NEAR // per,
            [leaf_low(0, at, per, flip) for at in range(per)]
            + [spread_of(0), in_steps(per, turned), whole(result.shape)]
            + [whole(a.shape) for a in last],
            [out_whole((local_rows, columns) if flip else (columns, local_rows), F32)],
            [pltpu.VMEM((columns, local_rows), F32)],
            [coupling] * per + [spread, path[flip], result, *last],
            leaf_flops // 2,
            leaf_moved // 2,
        )[0]
    return result, top_solution


def solution(mesh):
    return jax.shard_map(
        body,
        mesh=mesh,
        in_specs=(
            P(("leaf", "sep"), None),
            P(("leaf", "sep"), None),
            P(None, None, ("leaf", "sep")),
            P(None, None, ("leaf", "sep")),
            P(("leaf", "sep"), None),
            P(("leaf", "sep"), None),
            P(("leaf", "sep"), None),
            P(("leaf", "sep"), None),
            P(None, ("leaf", "sep")),
        ),
        out_specs=(P(("leaf", "sep"), None), P(("leaf", "sep"), None)),
        check_vma=False,
    )
```

```python
import functools

import jax
import jax.numpy as jnp
from jax import lax
from jax.experimental import pallas as pl
from jax.experimental.pallas import tpu as pltpu
from jax.sharding import PartitionSpec as P

PRECISE = lax.Precision.HIGHEST
F32 = jnp.float32
BF16 = jnp.bfloat16
I16 = jnp.int16
AXES = ("leaf", "sep")
NEAR = 8
GROUP = 2 * NEAR
BATCHES = ((4, 4), (0, 4))
PAD = 16
VMEM = 24 << 20


def swap(block, offset):
    count = lax.axis_size("leaf") * lax.axis_size("sep")
    return lax.ppermute(block, AXES, [(at, at ^ offset) for at in range(count)])


def encode(value):
    peak = jnp.maximum(jnp.max(jnp.abs(value), axis=0, keepdims=True), 1e-30)
    power = jnp.ceil(jnp.log2(peak))
    part = jnp.ceil(peak * jnp.exp2(14.0 - power))
    scale = 32767.0 / (part * jnp.exp2(power - 14.0))
    code = jnp.floor(value * scale + 0.5).astype(jnp.int32).astype(I16)
    row = lax.broadcasted_iota(jnp.int32, (PAD, value.shape[1]), 0)
    return code, jnp.where(row == 0, power, part).astype(jnp.int32).astype(I16)


def put(ref, coded):
    code, head = coded
    rows = code.shape[0]
    ref[:rows, :] = code
    ref[rows:, :] = head


def decode(block):
    rows = block.shape[0] - PAD
    head = block[rows:, :].astype(jnp.int32).astype(F32)
    scale = head[1:2, :] * jnp.exp2(head[0:1, :] - 14.0) * (1.0 / 32767.0)
    return block[:rows, :].astype(jnp.int32).astype(F32) * scale


def halves(value):
    high = value.astype(BF16)
    return high, (value - high.astype(F32)).astype(BF16)


def dot(left, right):
    return jnp.dot(left, right, preferred_element_type=F32)


def spread_tiles(tiles, level, width, size):
    across = tiles.shape[0]
    flags = tiles[:, level, :].astype(F32).T
    lane = lax.broadcasted_iota(jnp.int32, (flags.shape[0], width), 1) // size
    spread = jnp.zeros((flags.shape[0], width), F32)
    for at in range(across):
        spread = jnp.where(lane == at, flags[:, at : at + 1], spread)
    return spread


def masked(block, spread, chunk, size):
    width = block.shape[1]
    count = block.shape[0] // size
    flags = spread[0, pl.ds(pl.multiple_of(chunk * count, count), count), :]
    parts = []
    for at in range(count):
        row = jnp.broadcast_to(flags[at : at + 1, :], (16, width)).astype(BF16)
        tile = block[at * size : (at + 1) * size, :].reshape(size // 16, 16, width)
        parts.append((tile * row[None]).reshape(size, width))
    return jnp.concatenate(parts, 0)


def triangular(block, row_start, column_start):
    row = lax.broadcasted_iota(jnp.int32, block.shape, 0) + row_start
    column = lax.broadcasted_iota(jnp.int32, block.shape, 1) + column_start
    return jnp.where(row >= column, block, 0.0)


def with_rows(value, chunk, start, rhs):
    count = rhs.shape[0]
    parts = []
    for at in range(value.shape[0] // count):
        here = (start == chunk * value.shape[0] + at * count).astype(F32)
        parts.append(value[at * count : (at + 1) * count, :] + rhs[...] * here)
    return jnp.concatenate(parts, 0) if len(parts) > 1 else parts[0]


def call(kernel, place, steps, ins, outs, scratch, args, flops, moved):
    return pl.pallas_call(
        kernel,
        grid_spec=pltpu.PrefetchScalarGridSpec(
            num_scalar_prefetch=1,
            grid=(steps,),
            in_specs=ins,
            out_specs=[spec for spec, _ in outs],
            scratch_shapes=scratch,
        ),
        out_shape=[shape for _, shape in outs],
        compiler_params=pltpu.CompilerParams(vmem_limit_bytes=VMEM),
        cost_estimate=pl.CostEstimate(flops=flops, bytes_accessed=moved, transcendentals=0),
    )(place, *args)


def whole(shape):
    return pl.BlockSpec(shape, lambda *_: (0,) * len(shape))


def out_whole(shape, dtype):
    return whole(shape), jax.ShapeDtypeStruct(shape, dtype)


def in_steps(count, shape, dtype=None, entries=0):
    spec = pl.BlockSpec((count, *shape), lambda k, p: (k,) + (0,) * len(shape))
    return spec if dtype is None else (spec, jax.ShapeDtypeStruct((entries, *shape), dtype))


def at_rest(array):
    return pltpu.with_memory_space_constraint(array, pltpu.HBM)


def chunk_at(step, place, flip):
    return ((place[1] ^ step) << 1) | (place[0] ^ flip)


def steps_of(first, at, per):
    return first + pl.program_id(0) * per + at


def arrival(entry):
    return (NEAR - entry) & (NEAR - 1)


def over(shape, index):
    def spec(first, at, per, flip):
        return pl.BlockSpec(shape, lambda k, p: index(chunk_at(first + k * per + at, p, flip)))

    return spec


def over_arrived(shape, index):
    def spec(at, per, flip):
        return pl.BlockSpec(shape, lambda k, p: index(chunk_at(arrival(k * per + at), p, flip)))

    return spec


def arrived(at, per, place, flip):
    return chunk_at(arrival(pl.program_id(0) * per + at), place, flip)


def emit(first, per, at, outs, value):
    coded = encode(value)
    for step in range(len(outs) // per):
        where = step * per + at

        @pl.when(pl.program_id(0) == step)
        def _(where=where):
            if first + where == 0:
                outs[where][...] = value
            else:
                put(outs[where], coded)


def reduced(place, kernel, specs, args, shape, scratch, flops, moved, per, received=None, batches=BATCHES):
    coded = (shape[0] + PAD, shape[1])
    if received is None:
        sent = call(
            functools.partial(kernel, 1, 0, per),
            place,
            NEAR // per,
            specs(0, per, 1),
            [in_steps(per, coded, I16, NEAR)],
            scratch,
            args,
            flops // 2,
            moved // 2,
        )
        received = swap(sent[0], 1)
    kept = [None] * NEAR
    for first, count in batches:
        kept[first : first + count] = call(
            functools.partial(kernel, 0, first, per),
            place,
            count // per,
            specs(first, per, 0)
            + [
                pl.BlockSpec(
                    (per, *coded), lambda k, p, first=first: (first // per + k, 0, 0)
                )
            ],
            [
                out_whole(shape, F32) if at == 0 else out_whole(coded, I16)
                for at in range(first, first + count)
            ],
            scratch,
            [*args, received],
            flops * count // GROUP,
            moved * count // GROUP,
        )
    return kept


def leaf_low_value(size, chunk, place, block, spread, rounded, rhs):
    value = -dot(masked(block[0, 0], spread, chunk, size), rounded[...])
    return with_rows(value, chunk, place[2], rhs)


def leaf_send_kernel(size, per, place, *rest):
    blocks, (leaf_rhs, inverse_t, tiles, rhs) = rest[:per], rest[per : per + 4]
    sent, forward, rounded, spread = rest[per + 4 :]

    @pl.when(pl.program_id(0) == 0)
    def _():
        inverse = inverse_t[...].T
        for at in range(leaf_rhs.shape[0] // size):
            rows = slice(at * size, (at + 1) * size)
            block = triangular(inverse[rows, :], 0, 0)
            value = jnp.dot(block, leaf_rhs[rows, :], precision=PRECISE, preferred_element_type=F32)
            forward[rows, :] = value
            rounded[rows, :] = value.astype(BF16)
        for level in range(spread.shape[0]):
            spread[level] = spread_tiles(tiles, level, spread.shape[2], size)

    values = []
    for at in range(per):
        chunk = chunk_at(steps_of(0, at, per), place, 1)
        values.append(leaf_low_value(size, chunk, place, blocks[at], spread, rounded, rhs))
    for at in range(per):
        put(sent.at[at], encode(values[at]))


def leaf_keep_kernel(size, flip, first, per, place, *rest):
    blocks, (spread, rounded, rhs, received) = rest[:per], rest[per : per + 4]
    values = []
    for at in range(per):
        chunk = chunk_at(steps_of(first, at, per), place, flip)
        values.append(leaf_low_value(size, chunk, place, blocks[at], spread, rounded, rhs))
    for at in range(per):
        emit(first, per, at, rest[per + 4 :], values[at] + decode(received[at]))


def leaf_top_kernel(size, place, spread, rounded, coupling, part):
    group = coupling.shape[1]
    for at in range(group):
        chunk = pl.program_id(0) * group + at
        part[at] = dot(masked(coupling[0, at], spread, chunk, size), rounded[...])


def sum_kernel(final, waits, place, own, *rest):
    blocks, out = rest[: len(rest) - 1 - waits], rest[-1]
    value = own[...] if own.dtype == F32 else decode(own[...])
    for block in blocks:
        value = value + decode(block[...])
    if final:
        out[...] = value.astype(BF16)
    else:
        put(out, encode(value))


def summed(place, own, received, final, before=()):
    rows, columns = received[0].shape
    return call(
        functools.partial(sum_kernel, final, len(before)),
        place,
        1,
        [whole(own.shape)]
        + [whole(r.shape) for r in received]
        + [pl.BlockSpec(memory_space=pl.ANY) for _ in before],
        [out_whole((rows - PAD if final else rows, columns), BF16 if final else I16)],
        [],
        [own, *received, *before],
        rows * columns * 8,
        rows * columns * 20,
    )[0]


def reduce_and_gather(place, kept, far, final=False, before=()):
    received = [swap(kept[at], at << 1) for at in range(NEAR - 1, 0, -1)]
    coded = summed(place, kept[0], received, final and not far, before)
    if far:
        coded = summed(place, coded, [swap(coded, offset) for offset in far], final)
    mine = [coded] + [swap(coded, arrival(entry) << 1) for entry in range(1, NEAR)]
    mine = jnp.stack(mine)
    return mine, swap(mine, 1)


def factor_kernel(start_at, flip, per, place, *rest):
    factors, stack, rest = rest[:per], rest[per], rest[per + 1 :]
    before, rest = (rest[0], rest[1:]) if flip else (None, rest)
    out, wide, narrow = rest[0], rest[-2], rest[-1]
    depth = factors[0].shape[1]
    columns = narrow.shape[1]

    @pl.when(pl.program_id(0) == 0)
    def _():
        wide[...] = jnp.zeros_like(wide)
        narrow[...] = jnp.zeros_like(narrow)

    start = place[start_at]
    rows = factors[0].shape[0]
    chunks = [arrived(at, per, place, flip) for at in range(per)]
    below = functools.reduce(
        jnp.logical_and, [(chunk + 1) * depth <= start + 1 for chunk in chunks]
    )

    def add(wanted, cut):
        highs, lows, uppers, lowers = [], [], [], []
        for at in wanted:
            block = factors[at][...]
            high, low = halves(triangular(block, start, chunks[at] * depth) if cut else block)
            upper, lower = halves(decode(stack[at]))
            highs, lows = highs + [high], lows + [low]
            uppers, lowers = uppers + [upper], lowers + [lower]
        upper = jnp.concatenate(uppers, 0)
        both = jnp.concatenate([upper, jnp.concatenate(lowers, 0)], 1)
        wide[...] += dot(jnp.concatenate(highs, 1), both)
        narrow[...] += dot(jnp.concatenate(lows, 1), upper)

    @pl.when(below)
    def _():
        add(range(per), False)

    for at in range(per):

        @pl.when(jnp.logical_not(below) & (chunks[at] * depth < start + rows))
        def _(at=at):
            add([at], True)

    @pl.when(pl.program_id(0) == pl.num_programs(0) - 1)
    def _():
        value = wide[:, :columns] + wide[:, columns:] + narrow[...]
        if flip:
            value = value + before[...]
            rest[1][...] = value.T
        out[...] = value


def factor_apply(place, factor, stacks, start_at):
    count, size = factor.shape
    depth = size // GROUP
    columns = stacks[0].shape[2]
    per = 2
    block = over_arrived((count, depth), lambda chunk: (0, chunk))
    result = ()
    for flip in range(2):
        result = call(
            functools.partial(factor_kernel, start_at, flip, per),
            place,
            NEAR // per,
            [block(at, per, flip) for at in range(per)]
            + [in_steps(per, stacks[flip].shape[1:])]
            + [whole(r.shape) for r in result],
            [out_whole((count, columns), F32)] + [out_whole((columns, count), F32)] * flip,
            [pltpu.VMEM((count, 2 * columns), F32), pltpu.VMEM((count, columns), F32)],
            [at_rest(factor)] * per + [stacks[flip], *result],
            4 * count * size * columns,
            2 * count * size,
        )
    return result


def coupled_kernel(flip, first, per, place, *rest):
    couplings, parts, rest = rest[:per], rest[per : 2 * per], rest[2 * per :]
    rows, rhs, packed = rest[0], rest[1], rest[-1]
    columns = rows.shape[1]

    @pl.when(pl.program_id(0) == 0)
    def _():
        high, low = halves(rows[...])
        packed[:, :columns] = high
        packed[:, columns:] = low

    values = []
    for at in range(per):
        chunk = chunk_at(steps_of(first, at, per), place, flip)
        high, low = halves(couplings[at][0])
        product = dot(high, packed[...])
        value = product[:, :columns] + product[:, columns:] + dot(low, packed[:, :columns])
        values.append(with_rows(-(parts[at][0] + value), chunk, place[3], rhs))
    for at in range(per):
        if flip:
            put(rest[2].at[at], encode(values[at]))
        else:
            emit(first, per, at, rest[3:-1], values[at] + decode(rest[2][at]))


def back_kernel(start_at, flip, first, per, place, *rest):
    factors, vector, rest = rest[:per], rest[per], rest[per + 1 :]
    packed = rest[-1]
    columns = vector.shape[0]

    @pl.when(pl.program_id(0) == 0)
    def _():
        high, low = halves(vector[...])
        packed[:columns, :] = high
        packed[columns:, :] = low

    rows, depth = factors[0].shape
    start = place[start_at]
    chunks = [chunk_at(steps_of(first, at, per), place, flip) for at in range(per)]
    below = functools.reduce(
        jnp.logical_and, [(chunk + 1) * depth <= start + 1 for chunk in chunks]
    )
    above = functools.reduce(jnp.logical_and, [chunk * depth >= start + rows for chunk in chunks])

    def finish(values):
        for at in range(per):
            if flip:
                put(rest[0].at[at], encode(values[at]))
            else:
                emit(first, per, at, rest[1:-1], values[at] + decode(rest[0][at]))

    def products(cut):
        values = []
        for at in range(per):
            block = factors[at][...]
            high, low = halves(triangular(block, start, chunks[at] * depth) if cut else block)
            product = dot(packed[...], high)
            values.append(
                product[:columns, :] + product[columns:, :] + dot(packed[:columns, :], low)
            )
        return values

    @pl.when(below)
    def _():
        finish(products(False))

    @pl.when(above)
    def _():
        finish([jnp.zeros((columns, depth), F32)] * per)

    @pl.when(jnp.logical_not(below | above))
    def _():
        finish(products(True))


def back_apply(place, factor, vector, start_at):
    count, size = factor.shape
    columns = vector.shape[0]
    chunk = size // GROUP
    block = over((count, chunk), lambda c: (0, c))
    per = 2

    def specs(first, per, flip):
        return [block(first, at, per, flip) for at in range(per)] + [whole(vector.shape)]

    return reduced(
        place,
        functools.partial(back_kernel, start_at),
        specs,
        [at_rest(factor)] * per + [vector],
        (columns, chunk),
        [pltpu.VMEM((2 * columns, count), BF16)],
        8 * count * size * columns,
        4 * count * size,
        per,
    )


def carry_kernel(flip, per, place, *rest):
    couplings, (stack, before, gap, rounded, wide, narrow) = rest[:per], rest[per:]
    columns = before.shape[0]

    @pl.when(pl.program_id(0) == 0)
    def _():
        wide[...] = jnp.zeros_like(wide)
        narrow[...] = jnp.zeros_like(narrow)

    @pl.when(pl.program_id(0) >= 0)
    def _():
        highs, lows, uppers, lowers = [], [], [], []
        for at in range(per):
            high, low = halves(couplings[at][0])
            upper, lower = halves(decode(stack[at]))
            rounded[at] = upper
            highs, lows = highs + [high], lows + [low]
            uppers, lowers = uppers + [upper], lowers + [lower]
        upper = jnp.concatenate(uppers, 1)
        both = jnp.concatenate([upper, jnp.concatenate(lowers, 1)], 0)
        wide[...] += dot(both, jnp.concatenate(highs, 0))
        narrow[...] += dot(upper, jnp.concatenate(lows, 0))

    @pl.when(pl.program_id(0) == pl.num_programs(0) - 1)
    def _():
        gap[...] = before[...] - (wide[:columns, :] + wide[columns:, :] + narrow[...])


def own_kernel(place, mine, other, out):
    chunk = place[3] // out.shape[0]
    here = (chunk % 2 == place[0]).astype(F32)
    out[...] = (decode(mine[0]) * here + decode(other[0]) * (1.0 - here)).T


def leaf_product(size, flip, per, place, blocks, spread, path):
    left, right = [], []
    for at in range(per):
        chunk = arrived(at, per, place, flip)
        left.append(path[at])
        right.append(masked(blocks[at][0, 0], spread, chunk, size))
    return dot(jnp.concatenate(left, 1), jnp.concatenate(right, 0))


def leaf_back_top_kernel(size, per, place, *rest):
    near, far, (spread, mine, other, out) = rest[:per], rest[per : 2 * per], rest[2 * per :]

    @pl.when(pl.program_id(0) == 0)
    def _():
        out[...] = jnp.zeros_like(out)

    @pl.when(pl.program_id(0) >= 0)
    def _():
        out[...] += leaf_product(size, 0, per, place, near, spread, mine)
        out[...] += leaf_product(size, 1, per, place, far, spread, other)


def leaf_back_kernel(size, flip, per, place, *rest):
    blocks, (spread, path, before), rest = rest[:per], rest[per : per + 3], rest[per + 3 :]
    out, total = rest[-2:]

    @pl.when(pl.program_id(0) == 0)
    def _():
        total[...] = before[...]

    @pl.when(pl.program_id(0) >= 0)
    def _():
        total[...] += leaf_product(size, flip, per, place, blocks, spread, path)

    @pl.when(pl.program_id(0) == pl.num_programs(0) - 1)
    def _():
        if not flip:
            out[...] = total[...]
        else:
            forward, inverse_t = rest[:2]
            gap = forward[...] - total[...].T
            inverse = inverse_t[...].T
            for at in range(gap.shape[0] // size):
                rows = slice(at * size, (at + 1) * size)
                block = triangular(inverse[rows, :], 0, 0).T
                out[rows, :] = jnp.dot(
                    block, gap[rows, :], precision=PRECISE, preferred_element_type=F32
                )


def body(
    leaf_rhs,
    leaf_inverse,
    leaf_coupling,
    tile_mask,
    low_rhs,
    top_rhs,
    low_inverse,
    top_inverse,
    low_coupling,
):
    device_total = lax.axis_size("leaf") * lax.axis_size("sep")
    device = lax.axis_index("leaf") * lax.axis_size("sep") + lax.axis_index("sep")
    local_rows, columns = leaf_rhs.shape
    size = leaf_inverse.shape[1]
    levels = leaf_coupling.shape[0]
    sep_size = low_inverse.shape[1]
    low_count = low_inverse.shape[0]
    top_count = top_inverse.shape[0]
    chunk = sep_size // GROUP
    low_far = list(range(GROUP, device_total // 2, GROUP))
    top_far = list(range(GROUP, device_total, GROUP))
    low_start = device % (device_total // 2) * low_count
    top_start = device * top_count
    place = jnp.stack([device % 2, device % GROUP // 2, low_start, top_start]).astype(jnp.int32)

    inverse_t = at_rest(leaf_inverse.T)
    tiles = at_rest(jnp.transpose(tile_mask, (2, 0, 1)))
    coupling = at_rest(leaf_coupling.reshape(levels, GROUP, chunk, local_rows))
    low_blocks = at_rest(low_coupling.reshape(GROUP, chunk, low_count))
    low_rhs, top_rhs = at_rest(low_rhs), at_rest(top_rhs)

    leaf_flops = 2 * sep_size * local_rows * columns
    leaf_moved = 2 * sep_size * local_rows
    leaf_low = over((1, 1, chunk, local_rows), lambda c: (0, c, 0, 0))
    leaf_top = over_arrived((1, 1, chunk, local_rows), lambda c: (1, c, 0, 0))
    leaf_arrived = over_arrived((1, 1, chunk, local_rows), lambda c: (0, c, 0, 0))
    spread_shape = (levels, sep_size // size, local_rows)

    def spread_of(level):
        return pl.BlockSpec((1, *spread_shape[1:]), lambda k, p: (level, 0, 0))

    per = 4
    coded = (chunk + PAD, columns)
    sent, forward_leaf, rounded_leaf, spread = call(
        functools.partial(leaf_send_kernel, size, per),
        place,
        NEAR // per,
        [leaf_low(0, at, per, 1) for at in range(per)]
        + [whole(a.shape) for a in (leaf_rhs, inverse_t, tiles, low_rhs)],
        [
            in_steps(per, coded, I16, NEAR),
            out_whole(leaf_rhs.shape, F32),
            out_whole(leaf_rhs.shape, BF16),
            out_whole(spread_shape, F32),
        ],
        [],
        [coupling] * per + [at_rest(leaf_rhs), inverse_t, tiles, low_rhs],
        leaf_flops // 2,
        leaf_moved // 2,
    )

    def leaf_specs(first, per, flip):
        return [leaf_low(first, at, per, flip) for at in range(per)] + [
            spread_of(0),
            whole(rounded_leaf.shape),
            whole(low_rhs.shape),
        ]

    kept = reduced(
        place,
        functools.partial(leaf_keep_kernel, size),
        leaf_specs,
        [coupling] * per + [spread, rounded_leaf, low_rhs],
        (chunk, columns),
        [],
        leaf_flops,
        leaf_moved,
        per,
        swap(sent, 1),
        ((0, NEAR),),
    )
    part = call(
        functools.partial(leaf_top_kernel, size),
        place,
        GROUP // per,
        [
            spread_of(1),
            whole(rounded_leaf.shape),
            pl.BlockSpec((1, per, chunk, local_rows), lambda k, p: (1, k, 0, 0)),
        ],
        [in_steps(per, (chunk, columns), F32, GROUP)],
        [],
        [spread, rounded_leaf, coupling],
        leaf_flops,
        leaf_moved,
    )[0]
    first_input = reduce_and_gather(place, kept, low_far, before=[part])
    first_rows, first_columns = factor_apply(place, low_inverse, first_input, 2)

    coupled_flops = 8 * sep_size * low_count * columns
    coupled_moved = 4 * sep_size * low_count
    low_block = over((1, chunk, low_count), lambda c: (c, 0, 0))
    low_arrived = over_arrived((1, chunk, low_count), lambda c: (c, 0, 0))
    part_block = over((1, chunk, columns), lambda c: (c, 0, 0))
    per = 2

    def coupled_specs(first, per, flip):
        return (
            [low_block(first, at, per, flip) for at in range(per)]
            + [part_block(first, at, per, flip) for at in range(per)]
            + [whole(first_rows.shape), whole(top_rhs.shape)]
        )

    kept = reduced(
        place,
        coupled_kernel,
        coupled_specs,
        [low_blocks] * per + [part] * per + [first_rows, top_rhs],
        (chunk, columns),
        [pltpu.VMEM((low_count, 2 * columns), BF16)],
        coupled_flops,
        coupled_moved,
        per,
    )
    top_input = reduce_and_gather(place, kept, top_far)
    _, forward_columns = factor_apply(place, top_inverse, top_input, 3)

    kept = back_apply(place, top_inverse, forward_columns, 3)
    solution_blocks = reduce_and_gather(place, kept, top_far)
    turned = (columns, chunk)
    gap, rounded = first_columns, []
    for flip in range(2):
        gap, near = call(
            functools.partial(carry_kernel, flip, per),
            place,
            NEAR // per,
            [low_arrived(at, per, flip) for at in range(per)]
            + [in_steps(per, solution_blocks[flip].shape[1:]), whole(gap.shape)],
            [out_whole(gap.shape, F32), in_steps(per, turned, BF16, NEAR)],
            [pltpu.VMEM((2 * columns, low_count), F32), pltpu.VMEM((columns, low_count), F32)],
            [low_blocks] * per + [solution_blocks[flip], gap],
            coupled_flops // 2,
            coupled_moved // 2,
        )
        rounded.append(near)
    top_own = call(
        own_kernel,
        place,
        1,
        [
            pl.BlockSpec(
                (1, *s.shape[1:]), lambda k, p: (arrival((p[3] // chunk // 2) ^ p[1]), 0, 0)
            )
            for s in solution_blocks
        ],
        [out_whole((chunk, columns), F32)],
        [],
        list(solution_blocks),
        chunk * columns,
        8 * chunk * columns,
    )[0]
    top_solution = lax.dynamic_slice_in_dim(top_own, top_start % chunk, top_count, 0)
    kept = back_apply(place, low_inverse, gap, 2)
    back_top = call(
        functools.partial(leaf_back_top_kernel, size, per),
        place,
        NEAR // per,
        [leaf_top(at, per, flip) for flip in range(2) for at in range(per)]
        + [spread_of(1)]
        + [in_steps(per, turned)] * 2,
        [out_whole((columns, local_rows), F32)],
        [],
        [coupling] * (2 * per) + [spread, *rounded],
        leaf_flops,
        leaf_moved,
    )[0]
    path = reduce_and_gather(place, kept, low_far, True, [back_top, top_own])
    per = 4
    result = back_top
    for flip in range(2):
        last = [forward_leaf, inverse_t] if flip else []
        result = call(
            functools.partial(leaf_back_kernel, size, flip, per),
            place,
            NEAR // per,
            [leaf_arrived(at, per, flip) for at in range(per)]
            + [spread_of(0), in_steps(per, turned), whole(result.shape)]
            + [whole(a.shape) for a in last],
            [out_whole((local_rows, columns) if flip else (columns, local_rows), F32)],
            [pltpu.VMEM((columns, local_rows), F32)],
            [coupling] * per + [spread, path[flip], result, *last],
            leaf_flops // 2,
            leaf_moved // 2,
        )[0]
    return result, top_solution


def solution(mesh):
    return jax.shard_map(
        body,
        mesh=mesh,
        in_specs=(
            P(("leaf", "sep"), None),
            P(("leaf", "sep"), None),
            P(None, None, ("leaf", "sep")),
            P(None, None, ("leaf", "sep")),
            P(("leaf", "sep"), None),
            P(("leaf", "sep"), None),
            P(("leaf", "sep"), None),
            P(("leaf", "sep"), None),
            P(None, ("leaf", "sep")),
        ),
        out_specs=(P(("leaf", "sep"), None), P(("leaf", "sep"), None)),
        check_vma=False,
    )
```

```python
import functools

import jax
import jax.numpy as jnp
from jax import lax
from jax.experimental import pallas as pl
from jax.experimental.pallas import tpu as pltpu
from jax.sharding import PartitionSpec as P

PRECISE = lax.Precision.HIGHEST
F32 = jnp.float32
BF16 = jnp.bfloat16
I16 = jnp.int16
AXES = ("leaf", "sep")
NEAR = 8
GROUP = 2 * NEAR
BATCHES = ((4, 4), (0, 4))
PAD = 16
VMEM = 12 << 20


def swap(block, offset):
    count = lax.axis_size("leaf") * lax.axis_size("sep")
    return lax.ppermute(block, AXES, [(at, at ^ offset) for at in range(count)])


def encode(value):
    peak = jnp.maximum(jnp.max(jnp.abs(value), axis=0, keepdims=True), 1e-30)
    power = jnp.ceil(jnp.log2(peak))
    part = jnp.ceil(peak * jnp.exp2(14.0 - power))
    scale = 32767.0 / (part * jnp.exp2(power - 14.0))
    code = jnp.floor(value * scale + 0.5).astype(jnp.int32).astype(I16)
    row = lax.broadcasted_iota(jnp.int32, (PAD, value.shape[1]), 0)
    return code, jnp.where(row == 0, power, part).astype(jnp.int32).astype(I16)


def put(ref, coded):
    code, head = coded
    rows = code.shape[0]
    ref[:rows, :] = code
    ref[rows:, :] = head


def decode(block):
    rows = block.shape[0] - PAD
    head = block[rows:, :].astype(jnp.int32).astype(F32)
    scale = head[1:2, :] * jnp.exp2(head[0:1, :] - 14.0) * (1.0 / 32767.0)
    return block[:rows, :].astype(jnp.int32).astype(F32) * scale


def halves(value):
    high = value.astype(BF16)
    return high, (value - high.astype(F32)).astype(BF16)


def dot(left, right):
    return jnp.dot(left, right, preferred_element_type=F32)


def spread_tiles(tiles, level, width, size):
    across = tiles.shape[0]
    flags = tiles[:, level, :].astype(F32).T
    lane = lax.broadcasted_iota(jnp.int32, (flags.shape[0], width), 1) // size
    spread = jnp.zeros((flags.shape[0], width), F32)
    for at in range(across):
        spread = jnp.where(lane == at, flags[:, at : at + 1], spread)
    return spread


def masked(block, spread, chunk, size):
    width = block.shape[1]
    count = block.shape[0] // size
    flags = spread[0, pl.ds(pl.multiple_of(chunk * count, count), count), :]
    parts = []
    for at in range(count):
        row = jnp.broadcast_to(flags[at : at + 1, :], (16, width)).astype(BF16)
        tile = block[at * size : (at + 1) * size, :].reshape(size // 16, 16, width)
        parts.append((tile * row[None]).reshape(size, width))
    return jnp.concatenate(parts, 0)


def triangular(block, row_start, column_start):
    row = lax.broadcasted_iota(jnp.int32, block.shape, 0) + row_start
    column = lax.broadcasted_iota(jnp.int32, block.shape, 1) + column_start
    return jnp.where(row >= column, block, 0.0)


def with_rows(value, chunk, start, rhs):
    count = rhs.shape[0]
    parts = []
    for at in range(value.shape[0] // count):
        here = (start == chunk * value.shape[0] + at * count).astype(F32)
        parts.append(value[at * count : (at + 1) * count, :] + rhs[...] * here)
    return jnp.concatenate(parts, 0) if len(parts) > 1 else parts[0]


def call(kernel, place, steps, ins, outs, scratch, args, flops, moved):
    return pl.pallas_call(
        kernel,
        grid_spec=pltpu.PrefetchScalarGridSpec(
            num_scalar_prefetch=1,
            grid=(steps,),
            in_specs=ins,
            out_specs=[spec for spec, _ in outs],
            scratch_shapes=scratch,
        ),
        out_shape=[shape for _, shape in outs],
        compiler_params=pltpu.CompilerParams(vmem_limit_bytes=VMEM),
        cost_estimate=pl.CostEstimate(flops=flops, bytes_accessed=moved, transcendentals=0),
    )(place, *args)


def whole(shape):
    return pl.BlockSpec(shape, lambda *_: (0,) * len(shape))


def out_whole(shape, dtype):
    return whole(shape), jax.ShapeDtypeStruct(shape, dtype)


def in_steps(count, shape, dtype=None, entries=0):
    spec = pl.BlockSpec((count, *shape), lambda k, p: (k,) + (0,) * len(shape))
    return spec if dtype is None else (spec, jax.ShapeDtypeStruct((entries, *shape), dtype))


def at_rest(array):
    return pltpu.with_memory_space_constraint(array, pltpu.HBM)


def chunk_at(step, place, flip):
    return ((place[1] ^ step) << 1) | (place[0] ^ flip)


def steps_of(first, at, per):
    return first + pl.program_id(0) * per + at


def arrival(entry):
    return (NEAR - entry) & (NEAR - 1)


def over(shape, index):
    def spec(first, at, per, flip):
        return pl.BlockSpec(shape, lambda k, p: index(chunk_at(first + k * per + at, p, flip)))

    return spec


def over_arrived(shape, index):
    def spec(at, per, flip):
        return pl.BlockSpec(shape, lambda k, p: index(chunk_at(arrival(k * per + at), p, flip)))

    return spec


def arrived(at, per, place, flip):
    return chunk_at(arrival(pl.program_id(0) * per + at), place, flip)


def emit(first, per, at, outs, value):
    coded = encode(value)
    for step in range(len(outs) // per):
        where = step * per + at

        @pl.when(pl.program_id(0) == step)
        def _(where=where):
            if first + where == 0:
                outs[where][...] = value
            else:
                put(outs[where], coded)


def reduced(place, kernel, specs, args, shape, scratch, flops, moved, per, received=None, batches=BATCHES):
    coded = (shape[0] + PAD, shape[1])
    if received is None:
        sent = call(
            functools.partial(kernel, 1, 0, per),
            place,
            NEAR // per,
            specs(0, per, 1),
            [in_steps(per, coded, I16, NEAR)],
            scratch,
            args,
            flops // 2,
            moved // 2,
        )
        received = swap(sent[0], 1)
    kept = [None] * NEAR
    for first, count in batches:
        kept[first : first + count] = call(
            functools.partial(kernel, 0, first, per),
            place,
            count // per,
            specs(first, per, 0)
            + [
                pl.BlockSpec(
                    (per, *coded), lambda k, p, first=first: (first // per + k, 0, 0)
                )
            ],
            [
                out_whole(shape, F32) if at == 0 else out_whole(coded, I16)
                for at in range(first, first + count)
            ],
            scratch,
            [*args, received],
            flops * count // GROUP,
            moved * count // GROUP,
        )
    return kept


def leaf_low_value(size, chunk, place, block, spread, rounded, rhs):
    value = -dot(masked(block[0, 0], spread, chunk, size), rounded[...])
    return with_rows(value, chunk, place[2], rhs)


def leaf_send_kernel(size, per, place, *rest):
    blocks, (leaf_rhs, inverse_t, tiles, rhs) = rest[:per], rest[per : per + 4]
    sent, forward, rounded, spread = rest[per + 4 :]

    @pl.when(pl.program_id(0) == 0)
    def _():
        inverse = inverse_t[...].T
        for at in range(leaf_rhs.shape[0] // size):
            rows = slice(at * size, (at + 1) * size)
            block = triangular(inverse[rows, :], 0, 0)
            value = jnp.dot(block, leaf_rhs[rows, :], precision=PRECISE, preferred_element_type=F32)
            forward[rows, :] = value
            rounded[rows, :] = value.astype(BF16)
        for level in range(spread.shape[0]):
            spread[level] = spread_tiles(tiles, level, spread.shape[2], size)

    values = []
    for at in range(per):
        chunk = chunk_at(steps_of(0, at, per), place, 1)
        values.append(leaf_low_value(size, chunk, place, blocks[at], spread, rounded, rhs))
    for at in range(per):
        put(sent.at[at], encode(values[at]))


def leaf_keep_kernel(size, flip, first, per, place, *rest):
    blocks, (spread, rounded, rhs, received) = rest[:per], rest[per : per + 4]
    values = []
    for at in range(per):
        chunk = chunk_at(steps_of(first, at, per), place, flip)
        values.append(leaf_low_value(size, chunk, place, blocks[at], spread, rounded, rhs))
    for at in range(per):
        emit(first, per, at, rest[per + 4 :], values[at] + decode(received[at]))


def leaf_top_kernel(size, place, spread, rounded, coupling, part):
    group = coupling.shape[1]
    for at in range(group):
        chunk = pl.program_id(0) * group + at
        part[at] = dot(masked(coupling[0, at], spread, chunk, size), rounded[...])


def sum_kernel(final, waits, place, own, *rest):
    blocks, out = rest[: len(rest) - 1 - waits], rest[-1]
    value = own[...] if own.dtype == F32 else decode(own[...])
    for block in blocks:
        value = value + decode(block[...])
    if final:
        out[...] = value.astype(BF16)
    else:
        put(out, encode(value))


def summed(place, own, received, final, before=()):
    rows, columns = received[0].shape
    return call(
        functools.partial(sum_kernel, final, len(before)),
        place,
        1,
        [whole(own.shape)]
        + [whole(r.shape) for r in received]
        + [pl.BlockSpec(memory_space=pl.ANY) for _ in before],
        [out_whole((rows - PAD if final else rows, columns), BF16 if final else I16)],
        [],
        [own, *received, *before],
        rows * columns * 8,
        rows * columns * 20,
    )[0]


def reduce_and_gather(place, kept, far, final=False, before=()):
    received = [swap(kept[at], at << 1) for at in range(NEAR - 1, 0, -1)]
    coded = summed(place, kept[0], received, final and not far, before)
    if far:
        coded = summed(place, coded, [swap(coded, offset) for offset in far], final)
    mine = [coded] + [swap(coded, arrival(entry) << 1) for entry in range(1, NEAR)]
    mine = jnp.stack(mine)
    return mine, swap(mine, 1)


def factor_kernel(start_at, flip, per, place, *rest):
    factors, stack, rest = rest[:per], rest[per], rest[per + 1 :]
    before, rest = (rest[0], rest[1:]) if flip else (None, rest)
    out, wide, narrow = rest[0], rest[-2], rest[-1]
    depth = factors[0].shape[1]
    columns = narrow.shape[1]

    @pl.when(pl.program_id(0) == 0)
    def _():
        wide[...] = jnp.zeros_like(wide)
        narrow[...] = jnp.zeros_like(narrow)

    start = place[start_at]
    rows = factors[0].shape[0]
    chunks = [arrived(at, per, place, flip) for at in range(per)]
    below = functools.reduce(
        jnp.logical_and, [(chunk + 1) * depth <= start + 1 for chunk in chunks]
    )

    def add(wanted, cut):
        highs, lows, uppers, lowers = [], [], [], []
        for at in wanted:
            block = factors[at][...]
            high, low = halves(triangular(block, start, chunks[at] * depth) if cut else block)
            upper, lower = halves(decode(stack[at]))
            highs, lows = highs + [high], lows + [low]
            uppers, lowers = uppers + [upper], lowers + [lower]
        upper = jnp.concatenate(uppers, 0)
        both = jnp.concatenate([upper, jnp.concatenate(lowers, 0)], 1)
        wide[...] += dot(jnp.concatenate(highs, 1), both)
        narrow[...] += dot(jnp.concatenate(lows, 1), upper)

    @pl.when(below)
    def _():
        add(range(per), False)

    for at in range(per):

        @pl.when(jnp.logical_not(below) & (chunks[at] * depth < start + rows))
        def _(at=at):
            add([at], True)

    @pl.when(pl.program_id(0) == pl.num_programs(0) - 1)
    def _():
        value = wide[:, :columns] + wide[:, columns:] + narrow[...]
        if flip:
            value = value + before[...]
            rest[1][...] = value.T
        out[...] = value


def factor_apply(place, factor, stacks, start_at):
    count, size = factor.shape
    depth = size // GROUP
    columns = stacks[0].shape[2]
    per = 2
    block = over_arrived((count, depth), lambda chunk: (0, chunk))
    result = ()
    for flip in range(2):
        result = call(
            functools.partial(factor_kernel, start_at, flip, per),
            place,
            NEAR // per,
            [block(at, per, flip) for at in range(per)]
            + [in_steps(per, stacks[flip].shape[1:])]
            + [whole(r.shape) for r in result],
            [out_whole((count, columns), F32)] + [out_whole((columns, count), F32)] * flip,
            [pltpu.VMEM((count, 2 * columns), F32), pltpu.VMEM((count, columns), F32)],
            [factor] * per + [stacks[flip], *result],
            4 * count * size * columns,
            2 * count * size,
        )
    return result


def coupled_kernel(flip, first, per, place, *rest):
    couplings, parts, rest = rest[:per], rest[per : 2 * per], rest[2 * per :]
    rows, rhs, packed = rest[0], rest[1], rest[-1]
    columns = rows.shape[1]

    @pl.when(pl.program_id(0) == 0)
    def _():
        high, low = halves(rows[...])
        packed[:, :columns] = high
        packed[:, columns:] = low

    values = []
    for at in range(per):
        chunk = chunk_at(steps_of(first, at, per), place, flip)
        high, low = halves(couplings[at][0])
        product = dot(high, packed[...])
        value = product[:, :columns] + product[:, columns:] + dot(low, packed[:, :columns])
        values.append(with_rows(-(parts[at][0] + value), chunk, place[3], rhs))
    for at in range(per):
        if flip:
            put(rest[2].at[at], encode(values[at]))
        else:
            emit(first, per, at, rest[3:-1], values[at] + decode(rest[2][at]))


def back_kernel(start_at, flip, first, per, place, *rest):
    factors, vector, rest = rest[:per], rest[per], rest[per + 1 :]
    packed = rest[-1]
    columns = vector.shape[0]

    @pl.when(pl.program_id(0) == 0)
    def _():
        high, low = halves(vector[...])
        packed[:columns, :] = high
        packed[columns:, :] = low

    rows, depth = factors[0].shape
    start = place[start_at]
    chunks = [chunk_at(steps_of(first, at, per), place, flip) for at in range(per)]
    below = functools.reduce(
        jnp.logical_and, [(chunk + 1) * depth <= start + 1 for chunk in chunks]
    )
    above = functools.reduce(jnp.logical_and, [chunk * depth >= start + rows for chunk in chunks])

    def finish(values):
        for at in range(per):
            if flip:
                put(rest[0].at[at], encode(values[at]))
            else:
                emit(first, per, at, rest[1:-1], values[at] + decode(rest[0][at]))

    def products(cut):
        values = []
        for at in range(per):
            block = factors[at][...]
            high, low = halves(triangular(block, start, chunks[at] * depth) if cut else block)
            product = dot(packed[...], high)
            values.append(
                product[:columns, :] + product[columns:, :] + dot(packed[:columns, :], low)
            )
        return values

    @pl.when(below)
    def _():
        finish(products(False))

    @pl.when(above)
    def _():
        finish([jnp.zeros((columns, depth), F32)] * per)

    @pl.when(jnp.logical_not(below | above))
    def _():
        finish(products(True))


def back_apply(place, factor, vector, start_at):
    count, size = factor.shape
    columns = vector.shape[0]
    chunk = size // GROUP
    block = over((count, chunk), lambda c: (0, c))
    per = 2

    def specs(first, per, flip):
        return [block(first, at, per, flip) for at in range(per)] + [whole(vector.shape)]

    return reduced(
        place,
        functools.partial(back_kernel, start_at),
        specs,
        [factor] * per + [vector],
        (columns, chunk),
        [pltpu.VMEM((2 * columns, count), BF16)],
        8 * count * size * columns,
        4 * count * size,
        per,
    )


def carry_kernel(flip, per, place, *rest):
    couplings, (stack, before, gap, rounded, wide, narrow) = rest[:per], rest[per:]
    columns = before.shape[0]

    @pl.when(pl.program_id(0) == 0)
    def _():
        wide[...] = jnp.zeros_like(wide)
        narrow[...] = jnp.zeros_like(narrow)

    @pl.when(pl.program_id(0) >= 0)
    def _():
        highs, lows, uppers, lowers = [], [], [], []
        for at in range(per):
            high, low = halves(couplings[at][0])
            upper, lower = halves(decode(stack[at]))
            rounded[at] = upper
            highs, lows = highs + [high], lows + [low]
            uppers, lowers = uppers + [upper], lowers + [lower]
        upper = jnp.concatenate(uppers, 1)
        both = jnp.concatenate([upper, jnp.concatenate(lowers, 1)], 0)
        wide[...] += dot(both, jnp.concatenate(highs, 0))
        narrow[...] += dot(upper, jnp.concatenate(lows, 0))

    @pl.when(pl.program_id(0) == pl.num_programs(0) - 1)
    def _():
        gap[...] = before[...] - (wide[:columns, :] + wide[columns:, :] + narrow[...])


def own_kernel(place, mine, other, out):
    chunk = place[3] // out.shape[0]
    here = (chunk % 2 == place[0]).astype(F32)
    out[...] = (decode(mine[0]) * here + decode(other[0]) * (1.0 - here)).T


def leaf_product(size, flip, per, place, blocks, spread, path):
    left, right = [], []
    for at in range(per):
        chunk = arrived(at, per, place, flip)
        left.append(path[at])
        right.append(masked(blocks[at][0, 0], spread, chunk, size))
    return dot(jnp.concatenate(left, 1), jnp.concatenate(right, 0))


def leaf_back_top_kernel(size, per, place, *rest):
    near, far, (spread, mine, other, out) = rest[:per], rest[per : 2 * per], rest[2 * per :]

    @pl.when(pl.program_id(0) == 0)
    def _():
        out[...] = jnp.zeros_like(out)

    @pl.when(pl.program_id(0) >= 0)
    def _():
        out[...] += leaf_product(size, 0, per, place, near, spread, mine)
        out[...] += leaf_product(size, 1, per, place, far, spread, other)


def leaf_back_kernel(size, flip, per, place, *rest):
    blocks, (spread, path, before), rest = rest[:per], rest[per : per + 3], rest[per + 3 :]
    out, total = rest[-2:]

    @pl.when(pl.program_id(0) == 0)
    def _():
        total[...] = before[...]

    @pl.when(pl.program_id(0) >= 0)
    def _():
        total[...] += leaf_product(size, flip, per, place, blocks, spread, path)

    @pl.when(pl.program_id(0) == pl.num_programs(0) - 1)
    def _():
        if not flip:
            out[...] = total[...]
        else:
            forward, inverse_t = rest[:2]
            gap = forward[...] - total[...].T
            inverse = inverse_t[...].T
            for at in range(gap.shape[0] // size):
                rows = slice(at * size, (at + 1) * size)
                block = triangular(inverse[rows, :], 0, 0).T
                out[rows, :] = jnp.dot(
                    block, gap[rows, :], precision=PRECISE, preferred_element_type=F32
                )


def body(
    leaf_rhs,
    leaf_inverse,
    leaf_coupling,
    tile_mask,
    low_rhs,
    top_rhs,
    low_inverse,
    top_inverse,
    low_coupling,
):
    device_total = lax.axis_size("leaf") * lax.axis_size("sep")
    device = lax.axis_index("leaf") * lax.axis_size("sep") + lax.axis_index("sep")
    local_rows, columns = leaf_rhs.shape
    size = leaf_inverse.shape[1]
    levels = leaf_coupling.shape[0]
    sep_size = low_inverse.shape[1]
    low_count = low_inverse.shape[0]
    top_count = top_inverse.shape[0]
    chunk = sep_size // GROUP
    low_far = list(range(GROUP, device_total // 2, GROUP))
    top_far = list(range(GROUP, device_total, GROUP))
    low_start = device % (device_total // 2) * low_count
    top_start = device * top_count
    place = jnp.stack([device % 2, device % GROUP // 2, low_start, top_start]).astype(jnp.int32)

    inverse_t = at_rest(leaf_inverse.T)
    tiles = at_rest(jnp.transpose(tile_mask, (2, 0, 1)))
    coupling = at_rest(leaf_coupling.reshape(levels, GROUP, chunk, local_rows))
    low_blocks = low_coupling.reshape(GROUP, chunk, low_count)
    low_rhs, top_rhs = at_rest(low_rhs), at_rest(top_rhs)

    leaf_flops = 2 * sep_size * local_rows * columns
    leaf_moved = 2 * sep_size * local_rows
    leaf_low = over((1, 1, chunk, local_rows), lambda c: (0, c, 0, 0))
    leaf_top = over_arrived((1, 1, chunk, local_rows), lambda c: (1, c, 0, 0))
    leaf_arrived = over_arrived((1, 1, chunk, local_rows), lambda c: (0, c, 0, 0))
    spread_shape = (levels, sep_size // size, local_rows)

    def spread_of(level):
        return pl.BlockSpec((1, *spread_shape[1:]), lambda k, p: (level, 0, 0))

    per = 4
    coded = (chunk + PAD, columns)
    sent, forward_leaf, rounded_leaf, spread = call(
        functools.partial(leaf_send_kernel, size, per),
        place,
        NEAR // per,
        [leaf_low(0, at, per, 1) for at in range(per)]
        + [whole(a.shape) for a in (leaf_rhs, inverse_t, tiles, low_rhs)],
        [
            in_steps(per, coded, I16, NEAR),
            out_whole(leaf_rhs.shape, F32),
            out_whole(leaf_rhs.shape, BF16),
            out_whole(spread_shape, F32),
        ],
        [],
        [coupling] * per + [at_rest(leaf_rhs), inverse_t, tiles, low_rhs],
        leaf_flops // 2,
        leaf_moved // 2,
    )

    def leaf_specs(first, per, flip):
        return [leaf_low(first, at, per, flip) for at in range(per)] + [
            spread_of(0),
            whole(rounded_leaf.shape),
            whole(low_rhs.shape),
        ]

    kept = reduced(
        place,
        functools.partial(leaf_keep_kernel, size),
        leaf_specs,
        [coupling] * per + [spread, rounded_leaf, low_rhs],
        (chunk, columns),
        [],
        leaf_flops,
        leaf_moved,
        per,
        swap(sent, 1),
        ((0, NEAR),),
    )
    part = call(
        functools.partial(leaf_top_kernel, size),
        place,
        GROUP // per,
        [
            spread_of(1),
            whole(rounded_leaf.shape),
            pl.BlockSpec((1, per, chunk, local_rows), lambda k, p: (1, k, 0, 0)),
        ],
        [in_steps(per, (chunk, columns), F32, GROUP)],
        [],
        [spread, rounded_leaf, coupling],
        leaf_flops,
        leaf_moved,
    )[0]
    first_input = reduce_and_gather(place, kept, low_far, before=[part])
    first_rows, first_columns = factor_apply(place, low_inverse, first_input, 2)

    coupled_flops = 8 * sep_size * low_count * columns
    coupled_moved = 4 * sep_size * low_count
    low_block = over((1, chunk, low_count), lambda c: (c, 0, 0))
    low_arrived = over_arrived((1, chunk, low_count), lambda c: (c, 0, 0))
    part_block = over((1, chunk, columns), lambda c: (c, 0, 0))
    per = 2

    def coupled_specs(first, per, flip):
        return (
            [low_block(first, at, per, flip) for at in range(per)]
            + [part_block(first, at, per, flip) for at in range(per)]
            + [whole(first_rows.shape), whole(top_rhs.shape)]
        )

    kept = reduced(
        place,
        coupled_kernel,
        coupled_specs,
        [low_blocks] * per + [part] * per + [first_rows, top_rhs],
        (chunk, columns),
        [pltpu.VMEM((low_count, 2 * columns), BF16)],
        coupled_flops,
        coupled_moved,
        per,
    )
    top_input = reduce_and_gather(place, kept, top_far)
    _, forward_columns = factor_apply(place, top_inverse, top_input, 3)

    kept = back_apply(place, top_inverse, forward_columns, 3)
    solution_blocks = reduce_and_gather(place, kept, top_far)
    turned = (columns, chunk)
    gap, rounded = first_columns, []
    for flip in range(2):
        gap, near = call(
            functools.partial(carry_kernel, flip, per),
            place,
            NEAR // per,
            [low_arrived(at, per, flip) for at in range(per)]
            + [in_steps(per, solution_blocks[flip].shape[1:]), whole(gap.shape)],
            [out_whole(gap.shape, F32), in_steps(per, turned, BF16, NEAR)],
            [pltpu.VMEM((2 * columns, low_count), F32), pltpu.VMEM((columns, low_count), F32)],
            [low_blocks] * per + [solution_blocks[flip], gap],
            coupled_flops // 2,
            coupled_moved // 2,
        )
        rounded.append(near)
    top_own = call(
        own_kernel,
        place,
        1,
        [
            pl.BlockSpec(
                (1, *s.shape[1:]), lambda k, p: (arrival((p[3] // chunk // 2) ^ p[1]), 0, 0)
            )
            for s in solution_blocks
        ],
        [out_whole((chunk, columns), F32)],
        [],
        list(solution_blocks),
        chunk * columns,
        8 * chunk * columns,
    )[0]
    top_solution = lax.dynamic_slice_in_dim(top_own, top_start % chunk, top_count, 0)
    kept = back_apply(place, low_inverse, gap, 2)
    back_top = call(
        functools.partial(leaf_back_top_kernel, size, per),
        place,
        NEAR // per,
        [leaf_top(at, per, flip) for flip in range(2) for at in range(per)]
        + [spread_of(1)]
        + [in_steps(per, turned)] * 2,
        [out_whole((columns, local_rows), F32)],
        [],
        [coupling] * (2 * per) + [spread, *rounded],
        leaf_flops,
        leaf_moved,
    )[0]
    path = reduce_and_gather(place, kept, low_far, True, [back_top, top_own])
    per = 4
    result = back_top
    for flip in range(2):
        last = [forward_leaf, inverse_t] if flip else []
        result = call(
            functools.partial(leaf_back_kernel, size, flip, per),
            place,
            NEAR // per,
            [leaf_arrived(at, per, flip) for at in range(per)]
            + [spread_of(0), in_steps(per, turned), whole(result.shape)]
            + [whole(a.shape) for a in last],
            [out_whole((local_rows, columns) if flip else (columns, local_rows), F32)],
            [pltpu.VMEM((columns, local_rows), F32)],
            [coupling] * per + [spread, path[flip], result, *last],
            leaf_flops // 2,
            leaf_moved // 2,
        )[0]
    return result, top_solution


def solution(mesh):
    return jax.shard_map(
        body,
        mesh=mesh,
        in_specs=(
            P(("leaf", "sep"), None),
            P(("leaf", "sep"), None),
            P(None, None, ("leaf", "sep")),
            P(None, None, ("leaf", "sep")),
            P(("leaf", "sep"), None),
            P(("leaf", "sep"), None),
            P(("leaf", "sep"), None),
            P(("leaf", "sep"), None),
            P(None, ("leaf", "sep")),
        ),
        out_specs=(P(("leaf", "sep"), None), P(("leaf", "sep"), None)),
        check_vma=False,
    )
```

```python
import functools

import jax
import jax.numpy as jnp
from jax import lax
from jax.experimental import pallas as pl
from jax.experimental.pallas import tpu as pltpu
from jax.sharding import PartitionSpec as P

PRECISE = lax.Precision.HIGHEST
F32 = jnp.float32
BF16 = jnp.bfloat16
I16 = jnp.int16
AXES = ("leaf", "sep")
NEAR = 8
GROUP = 2 * NEAR
BATCHES = ((4, 4), (0, 4))
PAD = 16
VMEM = 8 << 20


def swap(block, offset):
    count = lax.axis_size("leaf") * lax.axis_size("sep")
    return lax.ppermute(block, AXES, [(at, at ^ offset) for at in range(count)])


def encode(value):
    peak = jnp.maximum(jnp.max(jnp.abs(value), axis=0, keepdims=True), 1e-30)
    power = jnp.ceil(jnp.log2(peak))
    part = jnp.ceil(peak * jnp.exp2(14.0 - power))
    scale = 32767.0 / (part * jnp.exp2(power - 14.0))
    code = jnp.floor(value * scale + 0.5).astype(jnp.int32).astype(I16)
    row = lax.broadcasted_iota(jnp.int32, (PAD, value.shape[1]), 0)
    return code, jnp.where(row == 0, power, part).astype(jnp.int32).astype(I16)


def put(ref, coded):
    code, head = coded
    rows = code.shape[0]
    ref[:rows, :] = code
    ref[rows:, :] = head


def decode(block):
    rows = block.shape[0] - PAD
    head = block[rows:, :].astype(jnp.int32).astype(F32)
    scale = head[1:2, :] * jnp.exp2(head[0:1, :] - 14.0) * (1.0 / 32767.0)
    return block[:rows, :].astype(jnp.int32).astype(F32) * scale


def halves(value):
    high = value.astype(BF16)
    return high, (value - high.astype(F32)).astype(BF16)


def dot(left, right):
    return jnp.dot(left, right, preferred_element_type=F32)


def spread_tiles(tiles, level, width, size):
    across = tiles.shape[0]
    flags = tiles[:, level, :].astype(F32).T
    lane = lax.broadcasted_iota(jnp.int32, (flags.shape[0], width), 1) // size
    spread = jnp.zeros((flags.shape[0], width), F32)
    for at in range(across):
        spread = jnp.where(lane == at, flags[:, at : at + 1], spread)
    return spread


def masked(block, spread, chunk, size):
    width = block.shape[1]
    count = block.shape[0] // size
    flags = spread[0, pl.ds(pl.multiple_of(chunk * count, count), count), :]
    parts = []
    for at in range(count):
        row = jnp.broadcast_to(flags[at : at + 1, :], (16, width)).astype(BF16)
        tile = block[at * size : (at + 1) * size, :].reshape(size // 16, 16, width)
        parts.append((tile * row[None]).reshape(size, width))
    return jnp.concatenate(parts, 0)


def triangular(block, row_start, column_start):
    row = lax.broadcasted_iota(jnp.int32, block.shape, 0) + row_start
    column = lax.broadcasted_iota(jnp.int32, block.shape, 1) + column_start
    return jnp.where(row >= column, block, 0.0)


def with_rows(value, chunk, start, rhs):
    count = rhs.shape[0]
    parts = []
    for at in range(value.shape[0] // count):
        here = (start == chunk * value.shape[0] + at * count).astype(F32)
        parts.append(value[at * count : (at + 1) * count, :] + rhs[...] * here)
    return jnp.concatenate(parts, 0) if len(parts) > 1 else parts[0]


def call(kernel, place, steps, ins, outs, scratch, args, flops, moved):
    return pl.pallas_call(
        kernel,
        grid_spec=pltpu.PrefetchScalarGridSpec(
            num_scalar_prefetch=1,
            grid=(steps,),
            in_specs=ins,
            out_specs=[spec for spec, _ in outs],
            scratch_shapes=scratch,
        ),
        out_shape=[shape for _, shape in outs],
        compiler_params=pltpu.CompilerParams(vmem_limit_bytes=VMEM),
        cost_estimate=pl.CostEstimate(flops=flops, bytes_accessed=moved, transcendentals=0),
    )(place, *args)


def held_call(kernel, place, outs, scratch, args, flops, moved, before=()):
    return pl.pallas_call(
        kernel,
        in_specs=[pl.BlockSpec(memory_space=pltpu.SMEM)]
        + [pl.BlockSpec(memory_space=pltpu.VMEM) for _ in args]
        + [pl.BlockSpec(memory_space=pl.ANY) for _ in before],
        out_specs=[pl.BlockSpec(memory_space=pltpu.VMEM) for _ in outs],
        out_shape=[jax.ShapeDtypeStruct(shape, dtype) for shape, dtype in outs],
        scratch_shapes=scratch,
        compiler_params=pltpu.CompilerParams(vmem_limit_bytes=VMEM),
        cost_estimate=pl.CostEstimate(flops=flops, bytes_accessed=moved, transcendentals=0),
    )(place, *args, *before)


def whole(shape):
    return pl.BlockSpec(shape, lambda *_: (0,) * len(shape))


def out_whole(shape, dtype):
    return whole(shape), jax.ShapeDtypeStruct(shape, dtype)


def in_steps(count, shape, dtype=None, entries=0):
    spec = pl.BlockSpec((count, *shape), lambda k, p: (k,) + (0,) * len(shape))
    return spec if dtype is None else (spec, jax.ShapeDtypeStruct((entries, *shape), dtype))


def at_rest(array):
    return pltpu.with_memory_space_constraint(array, pltpu.HBM)


def chunk_at(step, place, flip):
    return ((place[1] ^ step) << 1) | (place[0] ^ flip)


def steps_of(first, at, per):
    return first + pl.program_id(0) * per + at


def arrival(entry):
    return (NEAR - entry) & (NEAR - 1)


def over(shape, index):
    def spec(first, at, per, flip):
        return pl.BlockSpec(shape, lambda k, p: index(chunk_at(first + k * per + at, p, flip)))

    return spec


def over_arrived(shape, index):
    def spec(at, per, flip):
        return pl.BlockSpec(shape, lambda k, p: index(chunk_at(arrival(k * per + at), p, flip)))

    return spec


def columns_of(factor, chunk, depth):
    return factor[:, pl.ds(pl.multiple_of(chunk * depth, depth), depth)]


def all_of(conditions):
    return functools.reduce(jnp.logical_and, conditions)


def arrived(at, per, place, flip):
    return chunk_at(arrival(pl.program_id(0) * per + at), place, flip)


def emit(first, per, at, outs, value):
    coded = encode(value)
    for step in range(len(outs) // per):
        where = step * per + at

        @pl.when(pl.program_id(0) == step)
        def _(where=where):
            if first + where == 0:
                outs[where][...] = value
            else:
                put(outs[where], coded)


def reduced(place, kernel, specs, args, shape, scratch, flops, moved, per, received=None, batches=BATCHES):
    coded = (shape[0] + PAD, shape[1])
    if received is None:
        sent = call(
            functools.partial(kernel, 1, 0, per),
            place,
            NEAR // per,
            specs(0, per, 1),
            [in_steps(per, coded, I16, NEAR)],
            scratch,
            args,
            flops // 2,
            moved // 2,
        )
        received = swap(sent[0], 1)
    kept = [None] * NEAR
    for first, count in batches:
        kept[first : first + count] = call(
            functools.partial(kernel, 0, first, per),
            place,
            count // per,
            specs(first, per, 0)
            + [
                pl.BlockSpec(
                    (per, *coded), lambda k, p, first=first: (first // per + k, 0, 0)
                )
            ],
            [
                out_whole(shape, F32) if at == 0 else out_whole(coded, I16)
                for at in range(first, first + count)
            ],
            scratch,
            [*args, received],
            flops * count // GROUP,
            moved * count // GROUP,
        )
    return kept


def reduced_held(place, kernel, args, shape, scratch, flops, moved):
    coded = (shape[0] + PAD, shape[1])
    sent = held_call(
        functools.partial(kernel, 1, 0, NEAR),
        place,
        [((NEAR, *coded), I16)],
        scratch,
        args,
        flops // 2,
        moved // 2,
    )
    received = swap(sent[0], 1)
    kept = [None] * NEAR
    for first, count in BATCHES:
        kept[first : first + count] = held_call(
            functools.partial(kernel, 0, first, count),
            place,
            [(shape, F32) if at == 0 else (coded, I16) for at in range(first, first + count)],
            scratch,
            [*args, received],
            flops * count // GROUP,
            moved * count // GROUP,
        )
    return kept


def in_pairs(flip, first, count, values, sent, received, outs):
    def pair(begin):
        both = values([begin, begin + 1])
        for at in range(2):
            if flip:
                put(sent.at[begin + at], encode(both[at]))
            else:
                value = both[at] + decode(received[begin + at])
                if begin + at == 0:
                    outs[0][...] = value
                else:
                    put(outs[begin + at - first], encode(value))

    if flip:
        pl.loop(0, count // 2)(lambda number: pair(2 * number))
    else:
        for begin in range(first, first + count, 2):
            pair(begin)


def leaf_low_value(size, chunk, place, block, spread, rounded, rhs):
    value = -dot(masked(block[0, 0], spread, chunk, size), rounded[...])
    return with_rows(value, chunk, place[2], rhs)


def leaf_send_kernel(size, per, place, *rest):
    blocks, (leaf_rhs, inverse_t, tiles, rhs) = rest[:per], rest[per : per + 4]
    sent, forward, rounded, spread = rest[per + 4 :]

    @pl.when(pl.program_id(0) == 0)
    def _():
        inverse = inverse_t[...].T
        for at in range(leaf_rhs.shape[0] // size):
            rows = slice(at * size, (at + 1) * size)
            block = triangular(inverse[rows, :], 0, 0)
            value = jnp.dot(block, leaf_rhs[rows, :], precision=PRECISE, preferred_element_type=F32)
            forward[rows, :] = value
            rounded[rows, :] = value.astype(BF16)
        for level in range(spread.shape[0]):
            spread[level] = spread_tiles(tiles, level, spread.shape[2], size)

    values = []
    for at in range(per):
        chunk = chunk_at(steps_of(0, at, per), place, 1)
        values.append(leaf_low_value(size, chunk, place, blocks[at], spread, rounded, rhs))
    for at in range(per):
        put(sent.at[at], encode(values[at]))


def leaf_keep_kernel(size, flip, first, per, place, *rest):
    blocks, (spread, rounded, rhs, received) = rest[:per], rest[per : per + 4]
    values = []
    for at in range(per):
        chunk = chunk_at(steps_of(first, at, per), place, flip)
        values.append(leaf_low_value(size, chunk, place, blocks[at], spread, rounded, rhs))
    for at in range(per):
        emit(first, per, at, rest[per + 4 :], values[at] + decode(received[at]))


def leaf_top_kernel(size, place, spread, rounded, coupling, part):
    group = coupling.shape[1]
    for at in range(group):
        chunk = pl.program_id(0) * group + at
        part[at] = dot(masked(coupling[0, at], spread, chunk, size), rounded[...])


def sum_kernel(final, waits, place, own, *rest):
    blocks, out = rest[: len(rest) - 1 - waits], rest[-1]
    value = own[...] if own.dtype == F32 else decode(own[...])
    for block in blocks:
        value = value + decode(block[...])
    if final:
        out[...] = value.astype(BF16)
    else:
        put(out, encode(value))


def summed(place, own, received, final, before=()):
    rows, columns = received[0].shape
    return held_call(
        functools.partial(sum_kernel, final, len(before)),
        place,
        [((rows - PAD if final else rows, columns), BF16 if final else I16)],
        [],
        [own, *received],
        rows * columns * 8,
        rows * columns * 20,
        before,
    )[0]


def reduce_and_gather(place, kept, far, final=False, before=()):
    received = [swap(kept[at], at << 1) for at in range(NEAR - 1, 0, -1)]
    coded = summed(place, kept[0], received, final and not far, before)
    if far:
        coded = summed(place, coded, [swap(coded, offset) for offset in far], final)
    mine = [coded] + [swap(coded, arrival(entry) << 1) for entry in range(1, NEAR)]
    mine = jnp.stack(mine)
    return mine, swap(mine, 1)


def factor_kernel(start_at, flip, place, factor, stack, *rest):
    before, rest = (rest[0], rest[1:]) if flip else (None, rest)
    out, wide, narrow = rest[0], rest[-2], rest[-1]
    rows, size = factor.shape
    depth = size // GROUP
    columns = narrow.shape[1]
    start = place[start_at]
    wide[...] = jnp.zeros_like(wide)
    narrow[...] = jnp.zeros_like(narrow)

    @pl.loop(0, NEAR // 2)
    def _(number):
        entries = [2 * number, 2 * number + 1]
        chunks = [chunk_at(arrival(entry), place, flip) for entry in entries]
        below = all_of([(chunk + 1) * depth <= start + 1 for chunk in chunks])

        def add(wanted, cut):
            highs, lows, uppers, lowers = [], [], [], []
            for at in wanted:
                block = columns_of(factor, chunks[at], depth)
                high, low = halves(triangular(block, start, chunks[at] * depth) if cut else block)
                upper, lower = halves(decode(stack[entries[at]]))
                highs, lows = highs + [high], lows + [low]
                uppers, lowers = uppers + [upper], lowers + [lower]
            upper = jnp.concatenate(uppers, 0)
            both = jnp.concatenate([upper, jnp.concatenate(lowers, 0)], 1)
            wide[...] += dot(jnp.concatenate(highs, 1), both)
            narrow[...] += dot(jnp.concatenate(lows, 1), upper)

        @pl.when(below)
        def _():
            add(range(2), False)

        for at in range(2):

            @pl.when(jnp.logical_not(below) & (chunks[at] * depth < start + rows))
            def _(at=at):
                add([at], True)

    value = wide[:, :columns] + wide[:, columns:] + narrow[...]
    if flip:
        value = value + before[...]
        rest[1][...] = value.T
    out[...] = value


def factor_apply(place, factor, stacks, start_at):
    count, size = factor.shape
    columns = stacks[0].shape[2]
    result = ()
    for flip in range(2):
        result = held_call(
            functools.partial(factor_kernel, start_at, flip),
            place,
            [((count, columns), F32)] + [((columns, count), F32)] * flip,
            [pltpu.VMEM((count, 2 * columns), F32), pltpu.VMEM((count, columns), F32)],
            [factor, stacks[flip], *result],
            4 * count * size * columns,
            2 * count * size,
        )
    return result


def coupled_kernel(flip, first, count, place, coupling, part, rows, rhs, *rest):
    packed = rest[-1]
    columns = rows.shape[1]
    high, low = halves(rows[...])
    packed[:, :columns] = high
    packed[:, columns:] = low

    def values(steps):
        result = []
        for step in steps:
            chunk = chunk_at(step, place, flip)
            high, low = halves(coupling[chunk])
            product = dot(high, packed[...])
            value = product[:, :columns] + product[:, columns:] + dot(low, packed[:, :columns])
            result.append(with_rows(-(part[chunk] + value), chunk, place[3], rhs))
        return result

    in_pairs(flip, first, count, values, rest[0], rest[0], rest[1:-1])


def back_kernel(start_at, flip, first, count, place, factor, vector, *rest):
    packed, total = rest[-2:]
    columns = vector.shape[0]
    rows, size = factor.shape
    depth = size // GROUP
    start = place[start_at]
    high, low = halves(vector[...])
    packed[:columns, :] = high
    packed[columns:, :] = low

    def values(steps):
        chunks = [chunk_at(step, place, flip) for step in steps]
        below = all_of([(chunk + 1) * depth <= start + 1 for chunk in chunks])
        above = all_of([chunk * depth >= start + rows for chunk in chunks])

        def products(cut):
            for at, chunk in enumerate(chunks):
                block = columns_of(factor, chunk, depth)
                high, low = halves(triangular(block, start, chunk * depth) if cut else block)
                product = dot(packed[...], high)
                total[at] = (
                    product[:columns, :] + product[columns:, :] + dot(packed[:columns, :], low)
                )

        @pl.when(below)
        def _():
            products(False)

        @pl.when(above)
        def _():
            total[...] = jnp.zeros_like(total)

        @pl.when(jnp.logical_not(below | above))
        def _():
            products(True)

        return [total[at] for at in range(len(chunks))]

    in_pairs(flip, first, count, values, rest[0], rest[0], rest[1:-2])


def back_apply(place, factor, vector, start_at):
    count, size = factor.shape
    columns = vector.shape[0]
    chunk = size // GROUP
    return reduced_held(
        place,
        functools.partial(back_kernel, start_at),
        [factor, vector],
        (columns, chunk),
        [pltpu.VMEM((2 * columns, count), BF16), pltpu.VMEM((2, columns, chunk), F32)],
        8 * count * size * columns,
        4 * count * size,
    )


def carry_kernel(flip, place, coupling, stack, before, gap, rounded, wide, narrow):
    columns = before.shape[0]
    wide[...] = jnp.zeros_like(wide)
    narrow[...] = jnp.zeros_like(narrow)

    @pl.loop(0, NEAR // 2)
    def _(number):
        @pl.when(number >= 0)
        def _():
            highs, lows, uppers, lowers = [], [], [], []
            for at in range(2):
                entry = 2 * number + at
                high, low = halves(coupling[chunk_at(arrival(entry), place, flip)])
                upper, lower = halves(decode(stack[entry]))
                rounded[entry] = upper
                highs, lows = highs + [high], lows + [low]
                uppers, lowers = uppers + [upper], lowers + [lower]
            upper = jnp.concatenate(uppers, 1)
            both = jnp.concatenate([upper, jnp.concatenate(lowers, 1)], 0)
            wide[...] += dot(both, jnp.concatenate(highs, 0))
            narrow[...] += dot(upper, jnp.concatenate(lows, 0))

    gap[...] = before[...] - (wide[:columns, :] + wide[columns:, :] + narrow[...])


def own_kernel(place, mine, other, out):
    chunk = place[3] // out.shape[0]
    here = (chunk % 2 == place[0]).astype(F32)
    out[...] = (decode(mine[0]) * here + decode(other[0]) * (1.0 - here)).T


def leaf_product(size, flip, per, place, blocks, spread, path):
    left, right = [], []
    for at in range(per):
        chunk = arrived(at, per, place, flip)
        left.append(path[at])
        right.append(masked(blocks[at][0, 0], spread, chunk, size))
    return dot(jnp.concatenate(left, 1), jnp.concatenate(right, 0))


def leaf_back_top_kernel(size, per, place, *rest):
    near, far, (spread, mine, other, out) = rest[:per], rest[per : 2 * per], rest[2 * per :]

    @pl.when(pl.program_id(0) == 0)
    def _():
        out[...] = jnp.zeros_like(out)

    @pl.when(pl.program_id(0) >= 0)
    def _():
        out[...] += leaf_product(size, 0, per, place, near, spread, mine)
        out[...] += leaf_product(size, 1, per, place, far, spread, other)


def leaf_back_kernel(size, flip, per, place, *rest):
    blocks, (spread, path, before), rest = rest[:per], rest[per : per + 3], rest[per + 3 :]
    out, total = rest[-2:]

    @pl.when(pl.program_id(0) == 0)
    def _():
        total[...] = before[...]

    @pl.when(pl.program_id(0) >= 0)
    def _():
        total[...] += leaf_product(size, flip, per, place, blocks, spread, path)

    @pl.when(pl.program_id(0) == pl.num_programs(0) - 1)
    def _():
        if not flip:
            out[...] = total[...]
        else:
            forward, inverse_t = rest[:2]
            gap = forward[...] - total[...].T
            inverse = inverse_t[...].T
            for at in range(gap.shape[0] // size):
                rows = slice(at * size, (at + 1) * size)
                block = triangular(inverse[rows, :], 0, 0).T
                out[rows, :] = jnp.dot(
                    block, gap[rows, :], precision=PRECISE, preferred_element_type=F32
                )


def body(
    leaf_rhs,
    leaf_inverse,
    leaf_coupling,
    tile_mask,
    low_rhs,
    top_rhs,
    low_inverse,
    top_inverse,
    low_coupling,
):
    device_total = lax.axis_size("leaf") * lax.axis_size("sep")
    device = lax.axis_index("leaf") * lax.axis_size("sep") + lax.axis_index("sep")
    local_rows, columns = leaf_rhs.shape
    size = leaf_inverse.shape[1]
    levels = leaf_coupling.shape[0]
    sep_size = low_inverse.shape[1]
    low_count = low_inverse.shape[0]
    top_count = top_inverse.shape[0]
    chunk = sep_size // GROUP
    low_far = list(range(GROUP, device_total // 2, GROUP))
    top_far = list(range(GROUP, device_total, GROUP))
    low_start = device % (device_total // 2) * low_count
    top_start = device * top_count
    place = jnp.stack([device % 2, device % GROUP // 2, low_start, top_start]).astype(jnp.int32)

    inverse_t = at_rest(leaf_inverse.T)
    tiles = at_rest(jnp.transpose(tile_mask, (2, 0, 1)))
    coupling = at_rest(leaf_coupling.reshape(levels, GROUP, chunk, local_rows))
    low_blocks = low_coupling.reshape(GROUP, chunk, low_count)
    low_rhs = at_rest(low_rhs)

    leaf_flops = 2 * sep_size * local_rows * columns
    leaf_moved = 2 * sep_size * local_rows
    leaf_low = over((1, 1, chunk, local_rows), lambda c: (0, c, 0, 0))
    leaf_top = over_arrived((1, 1, chunk, local_rows), lambda c: (1, c, 0, 0))
    leaf_arrived = over_arrived((1, 1, chunk, local_rows), lambda c: (0, c, 0, 0))
    spread_shape = (levels, sep_size // size, local_rows)

    def spread_of(level):
        return pl.BlockSpec((1, *spread_shape[1:]), lambda k, p: (level, 0, 0))

    per = 4
    coded = (chunk + PAD, columns)
    sent, forward_leaf, rounded_leaf, spread = call(
        functools.partial(leaf_send_kernel, size, per),
        place,
        NEAR // per,
        [leaf_low(0, at, per, 1) for at in range(per)]
        + [whole(a.shape) for a in (leaf_rhs, inverse_t, tiles, low_rhs)],
        [
            in_steps(per, coded, I16, NEAR),
            out_whole(leaf_rhs.shape, F32),
            out_whole(leaf_rhs.shape, BF16),
            out_whole(spread_shape, F32),
        ],
        [],
        [coupling] * per + [at_rest(leaf_rhs), inverse_t, tiles, low_rhs],
        leaf_flops // 2,
        leaf_moved // 2,
    )

    def leaf_specs(first, per, flip):
        return [leaf_low(first, at, per, flip) for at in range(per)] + [
            spread_of(0),
            whole(rounded_leaf.shape),
            whole(low_rhs.shape),
        ]

    kept = reduced(
        place,
        functools.partial(leaf_keep_kernel, size),
        leaf_specs,
        [coupling] * per + [spread, rounded_leaf, low_rhs],
        (chunk, columns),
        [],
        leaf_flops,
        leaf_moved,
        per,
        swap(sent, 1),
        ((0, NEAR),),
    )
    part = call(
        functools.partial(leaf_top_kernel, size),
        place,
        GROUP // per,
        [
            spread_of(1),
            whole(rounded_leaf.shape),
            pl.BlockSpec((1, per, chunk, local_rows), lambda k, p: (1, k, 0, 0)),
        ],
        [in_steps(per, (chunk, columns), F32, GROUP)],
        [],
        [spread, rounded_leaf, coupling],
        leaf_flops,
        leaf_moved,
    )[0]
    first_input = reduce_and_gather(place, kept, low_far, before=[part])
    first_rows, first_columns = factor_apply(place, low_inverse, first_input, 2)

    coupled_flops = 8 * sep_size * low_count * columns
    coupled_moved = 4 * sep_size * low_count
    kept = reduced_held(
        place,
        coupled_kernel,
        [low_blocks, part, first_rows, top_rhs],
        (chunk, columns),
        [pltpu.VMEM((low_count, 2 * columns), BF16)],
        coupled_flops,
        coupled_moved,
    )
    top_input = reduce_and_gather(place, kept, top_far)
    _, forward_columns = factor_apply(place, top_inverse, top_input, 3)

    kept = back_apply(place, top_inverse, forward_columns, 3)
    solution_blocks = reduce_and_gather(place, kept, top_far)
    turned = (columns, chunk)
    gap, rounded = first_columns, []
    for flip in range(2):
        gap, near = held_call(
            functools.partial(carry_kernel, flip),
            place,
            [(gap.shape, F32), ((NEAR, *turned), BF16)],
            [pltpu.VMEM((2 * columns, low_count), F32), pltpu.VMEM((columns, low_count), F32)],
            [low_blocks, solution_blocks[flip], gap],
            coupled_flops // 2,
            coupled_moved // 2,
        )
        rounded.append(near)
    top_own = call(
        own_kernel,
        place,
        1,
        [
            pl.BlockSpec(
                (1, *s.shape[1:]), lambda k, p: (arrival((p[3] // chunk // 2) ^ p[1]), 0, 0)
            )
            for s in solution_blocks
        ],
        [out_whole((chunk, columns), F32)],
        [],
        list(solution_blocks),
        chunk * columns,
        8 * chunk * columns,
    )[0]
    top_solution = lax.dynamic_slice_in_dim(top_own, top_start % chunk, top_count, 0)
    kept = back_apply(place, low_inverse, gap, 2)
    per = 2
    back_top = call(
        functools.partial(leaf_back_top_kernel, size, per),
        place,
        NEAR // per,
        [leaf_top(at, per, flip) for flip in range(2) for at in range(per)]
        + [spread_of(1)]
        + [in_steps(per, turned)] * 2,
        [out_whole((columns, local_rows), F32)],
        [],
        [coupling] * (2 * per) + [spread, *rounded],
        leaf_flops,
        leaf_moved,
    )[0]
    path = reduce_and_gather(place, kept, low_far, True, [back_top, top_own])
    per = 4
    result = back_top
    for flip in range(2):
        last = [forward_leaf, inverse_t] if flip else []
        result = call(
            functools.partial(leaf_back_kernel, size, flip, per),
            place,
            NEAR // per,
            [leaf_arrived(at, per, flip) for at in range(per)]
            + [spread_of(0), in_steps(per, turned), whole(result.shape)]
            + [whole(a.shape) for a in last],
            [out_whole((local_rows, columns) if flip else (columns, local_rows), F32)],
            [pltpu.VMEM((columns, local_rows), F32)],
            [coupling] * per + [spread, path[flip], result, *last],
            leaf_flops // 2,
            leaf_moved // 2,
        )[0]
    return result, top_solution


def solution(mesh):
    return jax.shard_map(
        body,
        mesh=mesh,
        in_specs=(
            P(("leaf", "sep"), None),
            P(("leaf", "sep"), None),
            P(None, None, ("leaf", "sep")),
            P(None, None, ("leaf", "sep")),
            P(("leaf", "sep"), None),
            P(("leaf", "sep"), None),
            P(("leaf", "sep"), None),
            P(("leaf", "sep"), None),
            P(None, ("leaf", "sep")),
        ),
        out_specs=(P(("leaf", "sep"), None), P(("leaf", "sep"), None)),
        check_vma=False,
    )
```

```python
import functools

import jax
import jax.numpy as jnp
from jax import lax
from jax.experimental import pallas as pl
from jax.experimental.pallas import tpu as pltpu
from jax.sharding import PartitionSpec as P

PRECISE = lax.Precision.HIGHEST
F32 = jnp.float32
BF16 = jnp.bfloat16
I16 = jnp.int16
AXES = ("leaf", "sep")
NEAR = 8
GROUP = 2 * NEAR
BATCHES = ((0, 4), (4, 4))
SENDING = 0x01246537
ARRIVING = 0x12465370
PLACE_OF = 0x14352670
PAD = 16
VMEM = 8 << 20


def swap(block, offset):
    count = lax.axis_size("leaf") * lax.axis_size("sep")
    return lax.ppermute(block, AXES, [(at, at ^ offset) for at in range(count)])


def encode(value):
    peak = jnp.maximum(jnp.max(jnp.abs(value), axis=0, keepdims=True), 1e-30)
    power = jnp.ceil(jnp.log2(peak))
    part = jnp.ceil(peak * jnp.exp2(14.0 - power))
    scale = 32767.0 / (part * jnp.exp2(power - 14.0))
    code = jnp.floor(value * scale + 0.5).astype(jnp.int32).astype(I16)
    row = lax.broadcasted_iota(jnp.int32, (PAD, value.shape[1]), 0)
    return code, jnp.where(row == 0, power, part).astype(jnp.int32).astype(I16)


def put(ref, coded):
    code, head = coded
    rows = code.shape[0]
    ref[:rows, :] = code
    ref[rows:, :] = head


def decode(block):
    rows = block.shape[0] - PAD
    head = block[rows:, :].astype(jnp.int32).astype(F32)
    scale = head[1:2, :] * jnp.exp2(head[0:1, :] - 14.0) * (1.0 / 32767.0)
    return block[:rows, :].astype(jnp.int32).astype(F32) * scale


def halves(value):
    high = value.astype(BF16)
    return high, (value - high.astype(F32)).astype(BF16)


def dot(left, right):
    return jnp.dot(left, right, preferred_element_type=F32)


def spread_tiles(tiles, level, width, size):
    across = tiles.shape[0]
    flags = tiles[:, level, :].astype(F32).T
    lane = lax.broadcasted_iota(jnp.int32, (flags.shape[0], width), 1) // size
    spread = jnp.zeros((flags.shape[0], width), F32)
    for at in range(across):
        spread = jnp.where(lane == at, flags[:, at : at + 1], spread)
    return spread


def masked(block, spread, chunk, size):
    width = block.shape[1]
    count = block.shape[0] // size
    flags = spread[0, pl.ds(pl.multiple_of(chunk * count, count), count), :]
    parts = []
    for at in range(count):
        row = jnp.broadcast_to(flags[at : at + 1, :], (16, width)).astype(BF16)
        tile = block[at * size : (at + 1) * size, :].reshape(size // 16, 16, width)
        parts.append((tile * row[None]).reshape(size, width))
    return jnp.concatenate(parts, 0)


def triangular(block, row_start, column_start):
    row = lax.broadcasted_iota(jnp.int32, block.shape, 0) + row_start
    column = lax.broadcasted_iota(jnp.int32, block.shape, 1) + column_start
    return jnp.where(row >= column, block, 0.0)


def with_rows(value, chunk, start, rhs):
    count = rhs.shape[0]
    parts = []
    for at in range(value.shape[0] // count):
        here = (start == chunk * value.shape[0] + at * count).astype(F32)
        parts.append(value[at * count : (at + 1) * count, :] + rhs[...] * here)
    return jnp.concatenate(parts, 0) if len(parts) > 1 else parts[0]


def call(kernel, place, steps, ins, outs, scratch, args, flops, moved):
    return pl.pallas_call(
        kernel,
        grid_spec=pltpu.PrefetchScalarGridSpec(
            num_scalar_prefetch=1,
            grid=(steps,),
            in_specs=ins,
            out_specs=[spec for spec, _ in outs],
            scratch_shapes=scratch,
        ),
        out_shape=[shape for _, shape in outs],
        compiler_params=pltpu.CompilerParams(vmem_limit_bytes=VMEM),
        cost_estimate=pl.CostEstimate(flops=flops, bytes_accessed=moved, transcendentals=0),
    )(place, *args)


def held_call(kernel, place, outs, scratch, args, flops, moved, before=()):
    return pl.pallas_call(
        kernel,
        in_specs=[pl.BlockSpec(memory_space=pltpu.SMEM)]
        + [pl.BlockSpec(memory_space=pltpu.VMEM) for _ in args]
        + [pl.BlockSpec(memory_space=pl.ANY) for _ in before],
        out_specs=[pl.BlockSpec(memory_space=pltpu.VMEM) for _ in outs],
        out_shape=[jax.ShapeDtypeStruct(shape, dtype) for shape, dtype in outs],
        scratch_shapes=scratch,
        compiler_params=pltpu.CompilerParams(vmem_limit_bytes=VMEM),
        cost_estimate=pl.CostEstimate(flops=flops, bytes_accessed=moved, transcendentals=0),
    )(place, *args, *before)


def whole(shape):
    return pl.BlockSpec(shape, lambda *_: (0,) * len(shape))


def out_whole(shape, dtype):
    return whole(shape), jax.ShapeDtypeStruct(shape, dtype)


def in_steps(count, shape, dtype=None, entries=0):
    spec = pl.BlockSpec((count, *shape), lambda k, p: (k,) + (0,) * len(shape))
    return spec if dtype is None else (spec, jax.ShapeDtypeStruct((entries, *shape), dtype))


def at_rest(array):
    return pltpu.with_memory_space_constraint(array, pltpu.HBM)


def chunk_at(step, place, flip):
    return ((place[1] ^ step) << 1) | (place[0] ^ flip)


def digit(table, at):
    return (table >> (4 * at)) & (NEAR - 1)


def over(shape, index):
    def spec(at, per, flip):
        return pl.BlockSpec(
            shape, lambda k, p: index(chunk_at(digit(SENDING, k * per + at), p, flip))
        )

    return spec


def columns_of(factor, chunk, depth):
    return factor[:, pl.ds(pl.multiple_of(chunk * depth, depth), depth)]


def all_of(conditions):
    return functools.reduce(jnp.logical_and, conditions)


def reduced_held(place, kernel, args, shape, scratch, flops, moved, received=None):
    coded = (shape[0] + PAD, shape[1])
    batches = BATCHES if received is None else ((0, NEAR),)
    arrivals = [received]
    if received is None:
        arrivals = []
        for first, count in batches:
            sent = held_call(
                functools.partial(kernel, 1, first, count),
                place,
                [((count, *coded), I16)],
                scratch,
                args,
                flops * count // GROUP,
                moved * count // GROUP,
            )
            arrivals.append(swap(sent[0], 1))
    kept = [None] * NEAR
    for (first, count), arrival in zip(batches, arrivals):
        steps = [digit(SENDING, at) for at in range(first, first + count)]
        outs = held_call(
            functools.partial(kernel, 0, first, count),
            place,
            [(coded, I16) if step else (shape, F32) for step in steps],
            scratch,
            [*args, arrival],
            flops * count // GROUP,
            moved * count // GROUP,
        )
        for step, out in zip(steps, outs):
            kept[step] = out
    return kept


def in_pairs(flip, first, count, values, sent, received, outs):
    for begin in range(0, count, 2):
        steps = [digit(SENDING, first + begin + at) for at in range(2)]
        both = values(steps)
        for at, step in enumerate(steps):
            if flip:
                put(sent.at[begin + at], encode(both[at]))
            else:
                value = both[at] + decode(received[begin + at])
                if step == 0:
                    outs[begin + at][...] = value
                else:
                    put(outs[begin + at], encode(value))


def leaf_low_value(size, chunk, place, block, spread, rounded, rhs):
    value = -dot(masked(block, spread, chunk, size), rounded[...])
    return with_rows(value, chunk, place[2], rhs)


def leaf_send_kernel(size, per, place, *rest):
    blocks, (leaf_rhs, inverse_t, tiles, rhs) = rest[:per], rest[per : per + 4]
    sent, forward, rounded, spread = rest[per + 4 :]

    @pl.when(pl.program_id(0) == 0)
    def _():
        inverse = inverse_t[...].T
        for at in range(leaf_rhs.shape[0] // size):
            rows = slice(at * size, (at + 1) * size)
            block = triangular(inverse[rows, :], 0, 0)
            value = jnp.dot(block, leaf_rhs[rows, :], precision=PRECISE, preferred_element_type=F32)
            forward[rows, :] = value
            rounded[rows, :] = value.astype(BF16)
        for level in range(spread.shape[0]):
            spread[level] = spread_tiles(tiles, level, spread.shape[2], size)

    values = []
    for at in range(per):
        chunk = chunk_at(digit(SENDING, pl.program_id(0) * per + at), place, 1)
        values.append(leaf_low_value(size, chunk, place, blocks[at][0, 0], spread, rounded, rhs))
    for at in range(per):
        put(sent.at[at], encode(values[at]))


def leaf_keep_kernel(size, flip, first, count, place, coupling, spread, rounded, rhs, received, *outs):
    def values(steps):
        chunks = [chunk_at(step, place, flip) for step in steps]
        return [
            leaf_low_value(size, chunk, place, coupling[0, chunk], spread, rounded, rhs)
            for chunk in chunks
        ]

    in_pairs(flip, first, count, values, None, received, outs)


def leaf_top_kernel(size, place, spread, rounded, coupling, part):
    group = coupling.shape[1]
    for at in range(group):
        chunk = pl.program_id(0) * group + at
        part[at] = dot(masked(coupling[0, at], spread, chunk, size), rounded[...])


def sum_kernel(final, waits, place, own, *rest):
    blocks, out = rest[: len(rest) - 1 - waits], rest[-1]
    value = own[...] if own.dtype == F32 else decode(own[...])
    for block in blocks:
        value = value + decode(block[...])
    if final:
        out[...] = value.astype(BF16)
    else:
        put(out, encode(value))


def summed(place, own, received, final, before=()):
    rows, columns = received[0].shape
    return held_call(
        functools.partial(sum_kernel, final, len(before)),
        place,
        [((rows - PAD if final else rows, columns), BF16 if final else I16)],
        [],
        [own, *received],
        rows * columns * 8,
        rows * columns * 20,
        before,
    )[0]


def reduce_and_gather(place, kept, far, final=False, before=()):
    received = [swap(kept[at], at << 1) for at in (digit(ARRIVING, n) for n in range(1, NEAR))]
    coded = summed(place, kept[0], received, final and not far, before)
    if far:
        coded = summed(place, coded, [swap(coded, offset) for offset in far], final)
    mine = [coded] + [swap(coded, digit(ARRIVING, entry) << 1) for entry in range(1, NEAR)]
    mine = jnp.stack(mine)
    return mine, swap(mine, 1)


def factor_kernel(start_at, flip, place, factor, stack, *rest):
    before, rest = (rest[0], rest[1:]) if flip else (None, rest)
    out, wide, narrow = rest[0], rest[-2], rest[-1]
    rows, size = factor.shape
    depth = size // GROUP
    columns = narrow.shape[1]
    start = place[start_at]
    wide[...] = jnp.zeros_like(wide)
    narrow[...] = jnp.zeros_like(narrow)

    @pl.loop(0, NEAR // 2)
    def _(number):
        entries = [2 * number, 2 * number + 1]
        chunks = [chunk_at(digit(ARRIVING, entry), place, flip) for entry in entries]
        below = all_of([(chunk + 1) * depth <= start + 1 for chunk in chunks])

        def add(wanted, cut):
            highs, lows, uppers, lowers = [], [], [], []
            for at in wanted:
                block = columns_of(factor, chunks[at], depth)
                high, low = halves(triangular(block, start, chunks[at] * depth) if cut else block)
                upper, lower = halves(decode(stack[entries[at]]))
                highs, lows = highs + [high], lows + [low]
                uppers, lowers = uppers + [upper], lowers + [lower]
            upper = jnp.concatenate(uppers, 0)
            both = jnp.concatenate([upper, jnp.concatenate(lowers, 0)], 1)
            wide[...] += dot(jnp.concatenate(highs, 1), both)
            narrow[...] += dot(jnp.concatenate(lows, 1), upper)

        @pl.when(below)
        def _():
            add(range(2), False)

        for at in range(2):

            @pl.when(jnp.logical_not(below) & (chunks[at] * depth < start + rows))
            def _(at=at):
                add([at], True)

    value = wide[:, :columns] + wide[:, columns:] + narrow[...]
    if flip:
        value = value + before[...]
        rest[1][...] = value.T
    out[...] = value


def factor_apply(place, factor, stacks, start_at):
    count, size = factor.shape
    columns = stacks[0].shape[2]
    result = ()
    for flip in range(2):
        result = held_call(
            functools.partial(factor_kernel, start_at, flip),
            place,
            [((count, columns), F32)] + [((columns, count), F32)] * flip,
            [pltpu.VMEM((count, 2 * columns), F32), pltpu.VMEM((count, columns), F32)],
            [factor, stacks[flip], *result],
            4 * count * size * columns,
            2 * count * size,
        )
    return result


def coupled_kernel(flip, first, count, place, coupling, part, rows, rhs, *rest):
    packed = rest[-1]
    columns = rows.shape[1]
    high, low = halves(rows[...])
    packed[:, :columns] = high
    packed[:, columns:] = low

    def values(steps):
        result = []
        for step in steps:
            chunk = chunk_at(step, place, flip)
            high, low = halves(coupling[chunk])
            product = dot(high, packed[...])
            value = product[:, :columns] + product[:, columns:] + dot(low, packed[:, :columns])
            result.append(with_rows(-(part[chunk] + value), chunk, place[3], rhs))
        return result

    in_pairs(flip, first, count, values, rest[0], rest[0], rest[1:-1])


def back_kernel(start_at, flip, first, count, place, factor, vector, *rest):
    packed, total = rest[-2:]
    columns = vector.shape[0]
    rows, size = factor.shape
    depth = size // GROUP
    start = place[start_at]
    high, low = halves(vector[...])
    packed[:columns, :] = high
    packed[columns:, :] = low

    def values(steps):
        chunks = [chunk_at(step, place, flip) for step in steps]
        below = all_of([(chunk + 1) * depth <= start + 1 for chunk in chunks])
        above = all_of([chunk * depth >= start + rows for chunk in chunks])

        def products(cut):
            for at, chunk in enumerate(chunks):
                block = columns_of(factor, chunk, depth)
                high, low = halves(triangular(block, start, chunk * depth) if cut else block)
                product = dot(packed[...], high)
                total[at] = (
                    product[:columns, :] + product[columns:, :] + dot(packed[:columns, :], low)
                )

        @pl.when(below)
        def _():
            products(False)

        @pl.when(above)
        def _():
            total[...] = jnp.zeros_like(total)

        @pl.when(jnp.logical_not(below | above))
        def _():
            products(True)

        return [total[at] for at in range(len(chunks))]

    in_pairs(flip, first, count, values, rest[0], rest[0], rest[1:-2])


def back_apply(place, factor, vector, start_at):
    count, size = factor.shape
    columns = vector.shape[0]
    chunk = size // GROUP
    return reduced_held(
        place,
        functools.partial(back_kernel, start_at),
        [factor, vector],
        (columns, chunk),
        [pltpu.VMEM((2 * columns, count), BF16), pltpu.VMEM((2, columns, chunk), F32)],
        8 * count * size * columns,
        4 * count * size,
    )


def carry_kernel(flip, place, coupling, stack, before, gap, rounded, wide, narrow):
    columns = before.shape[0]
    wide[...] = jnp.zeros_like(wide)
    narrow[...] = jnp.zeros_like(narrow)

    @pl.loop(0, NEAR // 2)
    def _(number):
        @pl.when(number >= 0)
        def _():
            highs, lows, uppers, lowers = [], [], [], []
            for at in range(2):
                entry = 2 * number + at
                high, low = halves(coupling[chunk_at(digit(ARRIVING, entry), place, flip)])
                upper, lower = halves(decode(stack[entry]))
                rounded[entry] = upper
                highs, lows = highs + [high], lows + [low]
                uppers, lowers = uppers + [upper], lowers + [lower]
            upper = jnp.concatenate(uppers, 1)
            both = jnp.concatenate([upper, jnp.concatenate(lowers, 1)], 0)
            wide[...] += dot(both, jnp.concatenate(highs, 0))
            narrow[...] += dot(upper, jnp.concatenate(lows, 0))

    gap[...] = before[...] - (wide[:columns, :] + wide[columns:, :] + narrow[...])


def own_kernel(place, mine, other, out):
    chunk = place[3] // out.shape[0]
    here = (chunk % 2 == place[0]).astype(F32)
    out[...] = (decode(mine[0]) * here + decode(other[0]) * (1.0 - here)).T


def leaf_products(size, level, flip, place, coupling, spread, path, total):
    @pl.loop(0, NEAR // 2)
    def _(number):
        @pl.when(number >= 0)
        def _():
            left, right = [], []
            for at in range(2):
                entry = 2 * number + at
                chunk = chunk_at(digit(ARRIVING, entry), place, flip)
                left.append(path[entry])
                block = coupling[level, chunk]
                right.append(masked(block, spread.at[level : level + 1], chunk, size))
            total[...] += dot(jnp.concatenate(left, 1), jnp.concatenate(right, 0))


def leaf_back_top_kernel(size, place, coupling, spread, mine, other, out):
    out[...] = jnp.zeros_like(out)
    leaf_products(size, 1, 0, place, coupling, spread, mine, out)
    leaf_products(size, 1, 1, place, coupling, spread, other, out)


def leaf_back_kernel(size, flip, place, coupling, spread, path, before, *rest):
    out, total = rest[-2:]
    total[...] = before[...]
    leaf_products(size, 0, flip, place, coupling, spread, path, total)
    if not flip:
        out[...] = total[...]
    else:
        forward, inverse_t = rest[:2]
        gap = forward[...] - total[...].T
        inverse = inverse_t[...].T
        for at in range(gap.shape[0] // size):
            rows = slice(at * size, (at + 1) * size)
            block = triangular(inverse[rows, :], 0, 0).T
            out[rows, :] = jnp.dot(
                block, gap[rows, :], precision=PRECISE, preferred_element_type=F32
            )


def body(
    leaf_rhs,
    leaf_inverse,
    leaf_coupling,
    tile_mask,
    low_rhs,
    top_rhs,
    low_inverse,
    top_inverse,
    low_coupling,
):
    device_total = lax.axis_size("leaf") * lax.axis_size("sep")
    device = lax.axis_index("leaf") * lax.axis_size("sep") + lax.axis_index("sep")
    local_rows, columns = leaf_rhs.shape
    size = leaf_inverse.shape[1]
    levels = leaf_coupling.shape[0]
    sep_size = low_inverse.shape[1]
    low_count = low_inverse.shape[0]
    top_count = top_inverse.shape[0]
    chunk = sep_size // GROUP
    low_far = list(range(GROUP, device_total // 2, GROUP))
    top_far = list(range(GROUP, device_total, GROUP))
    low_start = device % (device_total // 2) * low_count
    top_start = device * top_count
    place = jnp.stack([device % 2, device % GROUP // 2, low_start, top_start]).astype(jnp.int32)

    inverse_t = leaf_inverse.T
    tiles = at_rest(jnp.transpose(tile_mask, (2, 0, 1)))
    coupling = leaf_coupling.reshape(levels, GROUP, chunk, local_rows)
    low_blocks = low_coupling.reshape(GROUP, chunk, low_count)

    leaf_flops = 2 * sep_size * local_rows * columns
    leaf_moved = 2 * sep_size * local_rows
    leaf_low = over((1, 1, chunk, local_rows), lambda c: (0, c, 0, 0))
    spread_shape = (levels, sep_size // size, local_rows)

    per = 4
    coded = (chunk + PAD, columns)
    sent, forward_leaf, rounded_leaf, spread = call(
        functools.partial(leaf_send_kernel, size, per),
        place,
        NEAR // per,
        [leaf_low(at, per, 1) for at in range(per)]
        + [whole(a.shape) for a in (leaf_rhs, inverse_t, tiles, low_rhs)],
        [
            in_steps(per, coded, I16, NEAR),
            out_whole(leaf_rhs.shape, F32),
            out_whole(leaf_rhs.shape, BF16),
            out_whole(spread_shape, F32),
        ],
        [],
        [at_rest(coupling)] * per + [at_rest(leaf_rhs), at_rest(inverse_t), tiles, at_rest(low_rhs)],
        leaf_flops // 2,
        leaf_moved // 2,
    )

    kept = reduced_held(
        place,
        functools.partial(leaf_keep_kernel, size),
        [coupling, spread, rounded_leaf, low_rhs],
        (chunk, columns),
        [],
        leaf_flops,
        leaf_moved,
        swap(sent, 1),
    )
    part = call(
        functools.partial(leaf_top_kernel, size),
        place,
        GROUP // per,
        [
            pl.BlockSpec((1, *spread_shape[1:]), lambda k, p: (1, 0, 0)),
            whole(rounded_leaf.shape),
            pl.BlockSpec((1, per, chunk, local_rows), lambda k, p: (1, k, 0, 0)),
        ],
        [in_steps(per, (chunk, columns), F32, GROUP)],
        [],
        [spread, rounded_leaf, at_rest(coupling)],
        leaf_flops,
        leaf_moved,
    )[0]
    first_input = reduce_and_gather(place, kept, low_far, before=[part])
    first_rows, first_columns = factor_apply(place, low_inverse, first_input, 2)

    coupled_flops = 8 * sep_size * low_count * columns
    coupled_moved = 4 * sep_size * low_count
    kept = reduced_held(
        place,
        coupled_kernel,
        [low_blocks, part, first_rows, top_rhs],
        (chunk, columns),
        [pltpu.VMEM((low_count, 2 * columns), BF16)],
        coupled_flops,
        coupled_moved,
    )
    top_input = reduce_and_gather(place, kept, top_far)
    _, forward_columns = factor_apply(place, top_inverse, top_input, 3)

    kept = back_apply(place, top_inverse, forward_columns, 3)
    solution_blocks = reduce_and_gather(place, kept, top_far)
    turned = (columns, chunk)
    gap, rounded = first_columns, []
    for flip in range(2):
        gap, near = held_call(
            functools.partial(carry_kernel, flip),
            place,
            [(gap.shape, F32), ((NEAR, *turned), BF16)],
            [pltpu.VMEM((2 * columns, low_count), F32), pltpu.VMEM((columns, low_count), F32)],
            [low_blocks, solution_blocks[flip], gap],
            coupled_flops // 2,
            coupled_moved // 2,
        )
        rounded.append(near)
    top_own = call(
        own_kernel,
        place,
        1,
        [
            pl.BlockSpec(
                (1, *s.shape[1:]), lambda k, p: (digit(PLACE_OF, (p[3] // chunk // 2) ^ p[1]), 0, 0)
            )
            for s in solution_blocks
        ],
        [out_whole((chunk, columns), F32)],
        [],
        list(solution_blocks),
        chunk * columns,
        8 * chunk * columns,
    )[0]
    top_solution = lax.dynamic_slice_in_dim(top_own, top_start % chunk, top_count, 0)
    kept = back_apply(place, low_inverse, gap, 2)
    back_top = held_call(
        functools.partial(leaf_back_top_kernel, size),
        place,
        [((columns, local_rows), F32)],
        [],
        [coupling, spread, *rounded],
        leaf_flops,
        leaf_moved,
    )[0]
    path = reduce_and_gather(place, kept, low_far, True, [back_top, top_own])
    result = back_top
    for flip in range(2):
        last = [forward_leaf, inverse_t] if flip else []
        result = held_call(
            functools.partial(leaf_back_kernel, size, flip),
            place,
            [((local_rows, columns) if flip else (columns, local_rows), F32)],
            [pltpu.VMEM((columns, local_rows), F32)],
            [coupling, spread, path[flip], result, *last],
            leaf_flops // 2,
            leaf_moved // 2,
        )[0]
    return result, top_solution


def solution(mesh):
    return jax.shard_map(
        body,
        mesh=mesh,
        in_specs=(
            P(("leaf", "sep"), None),
            P(("leaf", "sep"), None),
            P(None, None, ("leaf", "sep")),
            P(None, None, ("leaf", "sep")),
            P(("leaf", "sep"), None),
            P(("leaf", "sep"), None),
            P(("leaf", "sep"), None),
            P(("leaf", "sep"), None),
            P(None, ("leaf", "sep")),
        ),
        out_specs=(P(("leaf", "sep"), None), P(("leaf", "sep"), None)),
        check_vma=False,
    )
```

```python
import functools

import jax
import jax.numpy as jnp
from jax import lax
from jax.experimental import pallas as pl
from jax.experimental.pallas import tpu as pltpu
from jax.sharding import PartitionSpec as P

PRECISE = lax.Precision.HIGHEST
F32 = jnp.float32
BF16 = jnp.bfloat16
I16 = jnp.int16
AXES = ("leaf", "sep")
NEAR = 8
GROUP = 2 * NEAR
BATCHES = ((0, 4), (4, 4))
SENDING = 0x32107654
ARRIVING = 0x12345670
PLACE_OF = 0x12345670
PAD = 16
VMEM = 8 << 20


def swap(block, offset):
    count = lax.axis_size("leaf") * lax.axis_size("sep")
    return lax.ppermute(block, AXES, [(at, at ^ offset) for at in range(count)])


def encode(value):
    peak = jnp.maximum(jnp.max(jnp.abs(value), axis=0, keepdims=True), 1e-30)
    power = jnp.ceil(jnp.log2(peak))
    part = jnp.ceil(peak * jnp.exp2(14.0 - power))
    scale = 32767.0 / (part * jnp.exp2(power - 14.0))
    code = jnp.floor(value * scale + 0.5).astype(jnp.int32).astype(I16)
    row = lax.broadcasted_iota(jnp.int32, (PAD, value.shape[1]), 0)
    return code, jnp.where(row == 0, power, part).astype(jnp.int32).astype(I16)


def put(ref, coded):
    code, head = coded
    rows = code.shape[0]
    ref[:rows, :] = code
    ref[rows:, :] = head


def decode(block):
    rows = block.shape[0] - PAD
    head = block[rows:, :].astype(jnp.int32).astype(F32)
    scale = head[1:2, :] * jnp.exp2(head[0:1, :] - 14.0) * (1.0 / 32767.0)
    return block[:rows, :].astype(jnp.int32).astype(F32) * scale


def halves(value):
    high = value.astype(BF16)
    return high, (value - high.astype(F32)).astype(BF16)


def dot(left, right):
    return jnp.dot(left, right, preferred_element_type=F32)


def spread_tiles(tiles, level, width, size):
    across = tiles.shape[0]
    flags = tiles[:, level, :].astype(F32).T
    lane = lax.broadcasted_iota(jnp.int32, (flags.shape[0], width), 1) // size
    spread = jnp.zeros((flags.shape[0], width), F32)
    for at in range(across):
        spread = jnp.where(lane == at, flags[:, at : at + 1], spread)
    return spread


def masked(block, spread, chunk, size):
    width = block.shape[1]
    count = block.shape[0] // size
    flags = spread[0, pl.ds(pl.multiple_of(chunk * count, count), count), :]
    parts = []
    for at in range(count):
        row = jnp.broadcast_to(flags[at : at + 1, :], (16, width)).astype(BF16)
        tile = block[at * size : (at + 1) * size, :].reshape(size // 16, 16, width)
        parts.append((tile * row[None]).reshape(size, width))
    return jnp.concatenate(parts, 0)


def triangular(block, row_start, column_start):
    row = lax.broadcasted_iota(jnp.int32, block.shape, 0) + row_start
    column = lax.broadcasted_iota(jnp.int32, block.shape, 1) + column_start
    return jnp.where(row >= column, block, 0.0)


def with_rows(value, chunk, start, rhs):
    count = rhs.shape[0]
    parts = []
    for at in range(value.shape[0] // count):
        here = (start == chunk * value.shape[0] + at * count).astype(F32)
        parts.append(value[at * count : (at + 1) * count, :] + rhs[...] * here)
    return jnp.concatenate(parts, 0) if len(parts) > 1 else parts[0]


def call(kernel, place, steps, ins, outs, scratch, args, flops, moved):
    return pl.pallas_call(
        kernel,
        grid_spec=pltpu.PrefetchScalarGridSpec(
            num_scalar_prefetch=1,
            grid=(steps,),
            in_specs=ins,
            out_specs=[spec for spec, _ in outs],
            scratch_shapes=scratch,
        ),
        out_shape=[shape for _, shape in outs],
        compiler_params=pltpu.CompilerParams(vmem_limit_bytes=VMEM),
        cost_estimate=pl.CostEstimate(flops=flops, bytes_accessed=moved, transcendentals=0),
    )(place, *args)


def held_call(kernel, place, outs, scratch, args, flops, moved, before=()):
    return pl.pallas_call(
        kernel,
        in_specs=[pl.BlockSpec(memory_space=pltpu.SMEM)]
        + [pl.BlockSpec(memory_space=pltpu.VMEM) for _ in args]
        + [pl.BlockSpec(memory_space=pl.ANY) for _ in before],
        out_specs=[pl.BlockSpec(memory_space=pltpu.VMEM) for _ in outs],
        out_shape=[jax.ShapeDtypeStruct(shape, dtype) for shape, dtype in outs],
        scratch_shapes=scratch,
        compiler_params=pltpu.CompilerParams(vmem_limit_bytes=VMEM),
        cost_estimate=pl.CostEstimate(flops=flops, bytes_accessed=moved, transcendentals=0),
    )(place, *args, *before)


def whole(shape):
    return pl.BlockSpec(shape, lambda *_: (0,) * len(shape))


def out_whole(shape, dtype):
    return whole(shape), jax.ShapeDtypeStruct(shape, dtype)


def in_steps(count, shape, dtype=None, entries=0):
    spec = pl.BlockSpec((count, *shape), lambda k, p: (k,) + (0,) * len(shape))
    return spec if dtype is None else (spec, jax.ShapeDtypeStruct((entries, *shape), dtype))


def at_rest(array):
    return pltpu.with_memory_space_constraint(array, pltpu.HBM)


def chunk_at(step, place, flip):
    return ((place[1] ^ step) << 1) | (place[0] ^ flip)


def digit(table, at):
    return (table >> (4 * at)) & (NEAR - 1)


def over(shape, index, order):
    def spec(at, per, flip):
        return pl.BlockSpec(
            shape, lambda k, p: index(chunk_at(digit(order, k * per + at), p, flip))
        )

    return spec


def columns_of(factor, chunk, depth):
    return factor[:, pl.ds(pl.multiple_of(chunk * depth, depth), depth)]


def all_of(conditions):
    return functools.reduce(jnp.logical_and, conditions)


def reduced_held(place, kernel, args, shape, scratch, flops, moved, received=None):
    coded = (shape[0] + PAD, shape[1])
    batches = BATCHES if received is None else ((0, NEAR),)
    arrivals = [received]
    if received is None:
        arrivals = []
        for first, count in batches:
            sent = held_call(
                functools.partial(kernel, 1, first, count),
                place,
                [((count, *coded), I16)],
                scratch,
                args,
                flops * count // GROUP,
                moved * count // GROUP,
            )
            arrivals.append(swap(sent[0], 1))
    kept = [None] * NEAR
    for (first, count), arrival in zip(batches, arrivals):
        steps = [digit(SENDING, at) for at in range(first, first + count)]
        outs = held_call(
            functools.partial(kernel, 0, first, count),
            place,
            [(coded, I16) if step else (shape, F32) for step in steps],
            scratch,
            [*args, arrival],
            flops * count // GROUP,
            moved * count // GROUP,
        )
        for step, out in zip(steps, outs):
            kept[step] = out
    return kept


def in_pairs(flip, first, count, values, sent, received, outs):
    for begin in range(0, count, 2):
        steps = [digit(SENDING, first + begin + at) for at in range(2)]
        both = values(steps)
        for at, step in enumerate(steps):
            if flip:
                put(sent.at[begin + at], encode(both[at]))
            else:
                value = both[at] + decode(received[begin + at])
                if step == 0:
                    outs[begin + at][...] = value
                else:
                    put(outs[begin + at], encode(value))


def leaf_low_value(size, chunk, place, block, spread, rounded, rhs):
    value = -dot(masked(block, spread, chunk, size), rounded[...])
    return with_rows(value, chunk, place[2], rhs)


def leaf_send_kernel(size, per, place, *rest):
    blocks, (leaf_rhs, inverse_t, tiles, rhs) = rest[:per], rest[per : per + 4]
    sent, forward, rounded, spread = rest[per + 4 :]

    @pl.when(pl.program_id(0) == 0)
    def _():
        inverse = inverse_t[...].T
        for at in range(leaf_rhs.shape[0] // size):
            rows = slice(at * size, (at + 1) * size)
            block = triangular(inverse[rows, :], 0, 0)
            value = jnp.dot(block, leaf_rhs[rows, :], precision=PRECISE, preferred_element_type=F32)
            forward[rows, :] = value
            rounded[rows, :] = value.astype(BF16)
        for level in range(spread.shape[0]):
            spread[level] = spread_tiles(tiles, level, spread.shape[2], size)

    values = []
    for at in range(per):
        chunk = chunk_at(digit(SENDING, pl.program_id(0) * per + at), place, 1)
        values.append(leaf_low_value(size, chunk, place, blocks[at][0, 0], spread, rounded, rhs))
    for at in range(per):
        put(sent.at[at], encode(values[at]))


def leaf_keep_kernel(size, flip, first, count, place, coupling, spread, rounded, rhs, received, *outs):
    def values(steps):
        chunks = [chunk_at(step, place, flip) for step in steps]
        return [
            leaf_low_value(size, chunk, place, coupling[0, chunk], spread, rounded, rhs)
            for chunk in chunks
        ]

    in_pairs(flip, first, count, values, None, received, outs)


def leaf_top_kernel(size, place, spread, rounded, coupling, part):
    group = coupling.shape[1]
    for at in range(group):
        chunk = pl.program_id(0) * group + at
        part[at] = dot(masked(coupling[0, at], spread, chunk, size), rounded[...])


def sum_kernel(final, waits, place, own, *rest):
    blocks, out = rest[: len(rest) - 1 - waits], rest[-1]
    value = own[...] if own.dtype == F32 else decode(own[...])
    for block in blocks:
        value = value + decode(block[...])
    if final:
        out[...] = value.astype(BF16)
    else:
        put(out, encode(value))


def summed(place, own, received, final, before=()):
    rows, columns = received[0].shape
    return held_call(
        functools.partial(sum_kernel, final, len(before)),
        place,
        [((rows - PAD if final else rows, columns), BF16 if final else I16)],
        [],
        [own, *received],
        rows * columns * 8,
        rows * columns * 20,
        before,
    )[0]


def reduce_and_gather(place, kept, far, final=False, before=()):
    received = [swap(kept[at], at << 1) for at in (digit(ARRIVING, n) for n in range(1, NEAR))]
    coded = summed(place, kept[0], received, final and not far, before)
    if far:
        coded = summed(place, coded, [swap(coded, offset) for offset in far], final)
    mine = [coded] + [swap(coded, digit(ARRIVING, entry) << 1) for entry in range(1, NEAR)]
    mine = jnp.stack(mine)
    return mine, swap(mine, 1)


def factor_kernel(start_at, flip, place, factor, stack, *rest):
    before, rest = (rest[0], rest[1:]) if flip else (None, rest)
    out, wide, narrow = rest[0], rest[-2], rest[-1]
    rows, size = factor.shape
    depth = size // GROUP
    columns = narrow.shape[1]
    start = place[start_at]
    wide[...] = jnp.zeros_like(wide)
    narrow[...] = jnp.zeros_like(narrow)

    @pl.loop(0, NEAR // 2)
    def _(number):
        entries = [2 * number, 2 * number + 1]
        chunks = [chunk_at(digit(ARRIVING, entry), place, flip) for entry in entries]
        below = all_of([(chunk + 1) * depth <= start + 1 for chunk in chunks])

        def add(wanted, cut):
            highs, lows, uppers, lowers = [], [], [], []
            for at in wanted:
                block = columns_of(factor, chunks[at], depth)
                high, low = halves(triangular(block, start, chunks[at] * depth) if cut else block)
                upper, lower = halves(decode(stack[entries[at]]))
                highs, lows = highs + [high], lows + [low]
                uppers, lowers = uppers + [upper], lowers + [lower]
            upper = jnp.concatenate(uppers, 0)
            both = jnp.concatenate([upper, jnp.concatenate(lowers, 0)], 1)
            wide[...] += dot(jnp.concatenate(highs, 1), both)
            narrow[...] += dot(jnp.concatenate(lows, 1), upper)

        @pl.when(below)
        def _():
            add(range(2), False)

        for at in range(2):

            @pl.when(jnp.logical_not(below) & (chunks[at] * depth < start + rows))
            def _(at=at):
                add([at], True)

    value = wide[:, :columns] + wide[:, columns:] + narrow[...]
    if flip:
        value = value + before[...]
        rest[1][...] = value.T
    out[...] = value


def factor_apply(place, factor, stacks, start_at):
    count, size = factor.shape
    columns = stacks[0].shape[2]
    result = ()
    for flip in range(2):
        result = held_call(
            functools.partial(factor_kernel, start_at, flip),
            place,
            [((count, columns), F32)] + [((columns, count), F32)] * flip,
            [pltpu.VMEM((count, 2 * columns), F32), pltpu.VMEM((count, columns), F32)],
            [factor, stacks[flip], *result],
            4 * count * size * columns,
            2 * count * size,
        )
    return result


def coupled_kernel(flip, first, count, place, coupling, part, rows, rhs, *rest):
    packed = rest[-1]
    columns = rows.shape[1]
    high, low = halves(rows[...])
    packed[:, :columns] = high
    packed[:, columns:] = low

    def values(steps):
        result = []
        for step in steps:
            chunk = chunk_at(step, place, flip)
            high, low = halves(coupling[chunk])
            product = dot(high, packed[...])
            value = product[:, :columns] + product[:, columns:] + dot(low, packed[:, :columns])
            result.append(with_rows(-(part[chunk] + value), chunk, place[3], rhs))
        return result

    in_pairs(flip, first, count, values, rest[0], rest[0], rest[1:-1])


def back_kernel(start_at, flip, first, count, place, factor, vector, *rest):
    packed, total = rest[-2:]
    columns = vector.shape[0]
    rows, size = factor.shape
    depth = size // GROUP
    start = place[start_at]
    high, low = halves(vector[...])
    packed[:columns, :] = high
    packed[columns:, :] = low

    def values(steps):
        chunks = [chunk_at(step, place, flip) for step in steps]
        below = all_of([(chunk + 1) * depth <= start + 1 for chunk in chunks])
        above = all_of([chunk * depth >= start + rows for chunk in chunks])

        def products(cut):
            for at, chunk in enumerate(chunks):
                block = columns_of(factor, chunk, depth)
                high, low = halves(triangular(block, start, chunk * depth) if cut else block)
                product = dot(packed[...], high)
                total[at] = (
                    product[:columns, :] + product[columns:, :] + dot(packed[:columns, :], low)
                )

        @pl.when(below)
        def _():
            products(False)

        @pl.when(above)
        def _():
            total[...] = jnp.zeros_like(total)

        @pl.when(jnp.logical_not(below | above))
        def _():
            products(True)

        return [total[at] for at in range(len(chunks))]

    in_pairs(flip, first, count, values, rest[0], rest[0], rest[1:-2])


def back_apply(place, factor, vector, start_at):
    count, size = factor.shape
    columns = vector.shape[0]
    chunk = size // GROUP
    return reduced_held(
        place,
        functools.partial(back_kernel, start_at),
        [factor, vector],
        (columns, chunk),
        [pltpu.VMEM((2 * columns, count), BF16), pltpu.VMEM((2, columns, chunk), F32)],
        8 * count * size * columns,
        4 * count * size,
    )


def carry_kernel(flip, place, coupling, stack, before, gap, rounded, wide, narrow):
    columns = before.shape[0]
    wide[...] = jnp.zeros_like(wide)
    narrow[...] = jnp.zeros_like(narrow)

    @pl.loop(0, NEAR // 2)
    def _(number):
        @pl.when(number >= 0)
        def _():
            highs, lows, uppers, lowers = [], [], [], []
            for at in range(2):
                entry = 2 * number + at
                high, low = halves(coupling[chunk_at(digit(ARRIVING, entry), place, flip)])
                upper, lower = halves(decode(stack[entry]))
                rounded[entry] = upper
                highs, lows = highs + [high], lows + [low]
                uppers, lowers = uppers + [upper], lowers + [lower]
            upper = jnp.concatenate(uppers, 1)
            both = jnp.concatenate([upper, jnp.concatenate(lowers, 1)], 0)
            wide[...] += dot(both, jnp.concatenate(highs, 0))
            narrow[...] += dot(upper, jnp.concatenate(lows, 0))

    gap[...] = before[...] - (wide[:columns, :] + wide[columns:, :] + narrow[...])


def own_kernel(place, mine, other, out):
    chunk = place[3] // out.shape[0]
    here = (chunk % 2 == place[0]).astype(F32)
    out[...] = (decode(mine[0]) * here + decode(other[0]) * (1.0 - here)).T


def leaf_products(size, level, flip, place, coupling, spread, path, total):
    @pl.loop(0, NEAR // 2)
    def _(number):
        @pl.when(number >= 0)
        def _():
            left, right = [], []
            for at in range(2):
                entry = 2 * number + at
                chunk = chunk_at(digit(ARRIVING, entry), place, flip)
                left.append(path[entry])
                block = coupling[level, chunk]
                right.append(masked(block, spread.at[level : level + 1], chunk, size))
            total[...] += dot(jnp.concatenate(left, 1), jnp.concatenate(right, 0))


def leaf_back_top_kernel(size, per, place, *rest):
    near, far, (spread, mine, other, out) = rest[:per], rest[per : 2 * per], rest[2 * per :]
    step = pl.program_id(0)

    @pl.when(step == 0)
    def _():
        out[...] = jnp.zeros_like(out)

    @pl.when(step >= 0)
    def _():
        for flip, blocks, path in ((0, near, mine), (1, far, other)):
            left, right = [], []
            for at in range(per):
                chunk = chunk_at(digit(ARRIVING, step * per + at), place, flip)
                left.append(path[at])
                right.append(masked(blocks[at][0, 0], spread, chunk, size))
            out[...] += dot(jnp.concatenate(left, 1), jnp.concatenate(right, 0))


def leaf_back_kernel(size, flip, place, coupling, spread, path, before, *rest):
    out, total = rest[-2:]
    total[...] = before[...]
    leaf_products(size, 0, flip, place, coupling, spread, path, total)
    if not flip:
        out[...] = total[...]
    else:
        forward, inverse_t = rest[:2]
        gap = forward[...] - total[...].T
        inverse = inverse_t[...].T
        for at in range(gap.shape[0] // size):
            rows = slice(at * size, (at + 1) * size)
            block = triangular(inverse[rows, :], 0, 0).T
            out[rows, :] = jnp.dot(
                block, gap[rows, :], precision=PRECISE, preferred_element_type=F32
            )


def body(
    leaf_rhs,
    leaf_inverse,
    leaf_coupling,
    tile_mask,
    low_rhs,
    top_rhs,
    low_inverse,
    top_inverse,
    low_coupling,
):
    device_total = lax.axis_size("leaf") * lax.axis_size("sep")
    device = lax.axis_index("leaf") * lax.axis_size("sep") + lax.axis_index("sep")
    local_rows, columns = leaf_rhs.shape
    size = leaf_inverse.shape[1]
    levels = leaf_coupling.shape[0]
    sep_size = low_inverse.shape[1]
    low_count = low_inverse.shape[0]
    top_count = top_inverse.shape[0]
    chunk = sep_size // GROUP
    low_far = list(range(GROUP, device_total // 2, GROUP))
    top_far = list(range(GROUP, device_total, GROUP))
    low_start = device % (device_total // 2) * low_count
    top_start = device * top_count
    place = jnp.stack([device % 2, device % GROUP // 2, low_start, top_start]).astype(jnp.int32)

    inverse_t = leaf_inverse.T
    tiles = at_rest(jnp.transpose(tile_mask, (2, 0, 1)))
    coupling = leaf_coupling.reshape(levels, GROUP, chunk, local_rows)
    low_blocks = low_coupling.reshape(GROUP, chunk, low_count)

    leaf_flops = 2 * sep_size * local_rows * columns
    leaf_moved = 2 * sep_size * local_rows
    leaf_low = over((1, 1, chunk, local_rows), lambda c: (0, c, 0, 0), SENDING)
    leaf_top = over((1, 1, chunk, local_rows), lambda c: (1, c, 0, 0), ARRIVING)
    spread_shape = (levels, sep_size // size, local_rows)

    per = 4
    coded = (chunk + PAD, columns)
    sent, forward_leaf, rounded_leaf, spread = call(
        functools.partial(leaf_send_kernel, size, per),
        place,
        NEAR // per,
        [leaf_low(at, per, 1) for at in range(per)]
        + [whole(a.shape) for a in (leaf_rhs, inverse_t, tiles, low_rhs)],
        [
            in_steps(per, coded, I16, NEAR),
            out_whole(leaf_rhs.shape, F32),
            out_whole(leaf_rhs.shape, BF16),
            out_whole(spread_shape, F32),
        ],
        [],
        [at_rest(coupling)] * per + [at_rest(leaf_rhs), at_rest(inverse_t), tiles, at_rest(low_rhs)],
        leaf_flops // 2,
        leaf_moved // 2,
    )

    kept = reduced_held(
        place,
        functools.partial(leaf_keep_kernel, size),
        [coupling, spread, rounded_leaf, low_rhs],
        (chunk, columns),
        [],
        leaf_flops,
        leaf_moved,
        swap(sent, 1),
    )
    part = call(
        functools.partial(leaf_top_kernel, size),
        place,
        GROUP // per,
        [
            pl.BlockSpec((1, *spread_shape[1:]), lambda k, p: (1, 0, 0)),
            whole(rounded_leaf.shape),
            pl.BlockSpec((1, per, chunk, local_rows), lambda k, p: (1, k, 0, 0)),
        ],
        [in_steps(per, (chunk, columns), F32, GROUP)],
        [],
        [spread, rounded_leaf, at_rest(coupling)],
        leaf_flops,
        leaf_moved,
    )[0]
    first_input = reduce_and_gather(place, kept, low_far, before=[part])
    first_rows, first_columns = factor_apply(place, low_inverse, first_input, 2)

    coupled_flops = 8 * sep_size * low_count * columns
    coupled_moved = 4 * sep_size * low_count
    kept = reduced_held(
        place,
        coupled_kernel,
        [low_blocks, part, first_rows, top_rhs],
        (chunk, columns),
        [pltpu.VMEM((low_count, 2 * columns), BF16)],
        coupled_flops,
        coupled_moved,
    )
    top_input = reduce_and_gather(place, kept, top_far)
    _, forward_columns = factor_apply(place, top_inverse, top_input, 3)

    kept = back_apply(place, top_inverse, forward_columns, 3)
    solution_blocks = reduce_and_gather(place, kept, top_far)
    turned = (columns, chunk)
    gap, rounded = first_columns, []
    for flip in range(2):
        gap, near = held_call(
            functools.partial(carry_kernel, flip),
            place,
            [(gap.shape, F32), ((NEAR, *turned), BF16)],
            [pltpu.VMEM((2 * columns, low_count), F32), pltpu.VMEM((columns, low_count), F32)],
            [low_blocks, solution_blocks[flip], gap],
            coupled_flops // 2,
            coupled_moved // 2,
        )
        rounded.append(near)
    top_own = call(
        own_kernel,
        place,
        1,
        [
            pl.BlockSpec(
                (1, *s.shape[1:]), lambda k, p: (digit(PLACE_OF, (p[3] // chunk // 2) ^ p[1]), 0, 0)
            )
            for s in solution_blocks
        ],
        [out_whole((chunk, columns), F32)],
        [],
        list(solution_blocks),
        chunk * columns,
        8 * chunk * columns,
    )[0]
    top_solution = lax.dynamic_slice_in_dim(top_own, top_start % chunk, top_count, 0)
    kept = back_apply(place, low_inverse, gap, 2)
    per = 2
    back_top = call(
        functools.partial(leaf_back_top_kernel, size, per),
        place,
        NEAR // per,
        [leaf_top(at, per, flip) for flip in range(2) for at in range(per)]
        + [pl.BlockSpec((1, *spread_shape[1:]), lambda k, p: (1, 0, 0))]
        + [in_steps(per, turned)] * 2,
        [out_whole((columns, local_rows), F32)],
        [],
        [at_rest(coupling)] * (2 * per) + [spread, *rounded],
        leaf_flops,
        leaf_moved,
    )[0]
    path = reduce_and_gather(place, kept, low_far, True, [back_top, top_own])
    result = back_top
    for flip in range(2):
        last = [forward_leaf, inverse_t] if flip else []
        result = held_call(
            functools.partial(leaf_back_kernel, size, flip),
            place,
            [((local_rows, columns) if flip else (columns, local_rows), F32)],
            [pltpu.VMEM((columns, local_rows), F32)],
            [coupling, spread, path[flip], result, *last],
            leaf_flops // 2,
            leaf_moved // 2,
        )[0]
    return result, top_solution


def solution(mesh):
    return jax.shard_map(
        body,
        mesh=mesh,
        in_specs=(
            P(("leaf", "sep"), None),
            P(("leaf", "sep"), None),
            P(None, None, ("leaf", "sep")),
            P(None, None, ("leaf", "sep")),
            P(("leaf", "sep"), None),
            P(("leaf", "sep"), None),
            P(("leaf", "sep"), None),
            P(("leaf", "sep"), None),
            P(None, ("leaf", "sep")),
        ),
        out_specs=(P(("leaf", "sep"), None), P(("leaf", "sep"), None)),
        check_vma=False,
    )
```

```python
import functools

import jax
import jax.numpy as jnp
from jax import lax
from jax.experimental import pallas as pl
from jax.experimental.pallas import tpu as pltpu
from jax.sharding import PartitionSpec as P

PRECISE = lax.Precision.HIGHEST
F32 = jnp.float32
BF16 = jnp.bfloat16
I16 = jnp.int16
AXES = ("leaf", "sep")
NEAR = 8
GROUP = 2 * NEAR
BATCHES = ((0, 4), (4, 4))
SENDING = 0x32107654
ARRIVING = 0x12345670
PLACE_OF = 0x12345670
PAD = 16
VMEM = 8 << 20


def swap(block, offset):
    count = lax.axis_size("leaf") * lax.axis_size("sep")
    return lax.ppermute(block, AXES, [(at, at ^ offset) for at in range(count)])


def encode(value):
    peak = jnp.maximum(jnp.max(jnp.abs(value), axis=0, keepdims=True), 1e-30)
    power = jnp.ceil(jnp.log2(peak))
    part = jnp.ceil(peak * jnp.exp2(14.0 - power))
    scale = 32767.0 / (part * jnp.exp2(power - 14.0))
    code = jnp.floor(value * scale + 0.5).astype(jnp.int32).astype(I16)
    row = lax.broadcasted_iota(jnp.int32, (PAD, value.shape[1]), 0)
    return code, jnp.where(row == 0, power, part).astype(jnp.int32).astype(I16)


def put(ref, coded):
    code, head = coded
    rows = code.shape[0]
    ref[:rows, :] = code
    ref[rows:, :] = head


def decode(block):
    rows = block.shape[0] - PAD
    head = block[rows:, :].astype(jnp.int32).astype(F32)
    scale = head[1:2, :] * jnp.exp2(head[0:1, :] - 14.0) * (1.0 / 32767.0)
    return block[:rows, :].astype(jnp.int32).astype(F32) * scale


def halves(value):
    high = value.astype(BF16)
    return high, (value - high.astype(F32)).astype(BF16)


def dot(left, right):
    return jnp.dot(left, right, preferred_element_type=F32)


def spread_tiles(tiles, level, width, size):
    across = tiles.shape[0]
    flags = tiles[:, level, :].astype(F32).T
    lane = lax.broadcasted_iota(jnp.int32, (flags.shape[0], width), 1) // size
    spread = jnp.zeros((flags.shape[0], width), F32)
    for at in range(across):
        spread = jnp.where(lane == at, flags[:, at : at + 1], spread)
    return spread


def masked(block, spread, chunk, size):
    width = block.shape[1]
    count = block.shape[0] // size
    flags = spread[0, pl.ds(pl.multiple_of(chunk * count, count), count), :]
    parts = []
    for at in range(count):
        row = jnp.broadcast_to(flags[at : at + 1, :], (16, width)).astype(BF16)
        tile = block[at * size : (at + 1) * size, :].reshape(size // 16, 16, width)
        parts.append((tile * row[None]).reshape(size, width))
    return jnp.concatenate(parts, 0)


def triangular(block, row_start, column_start):
    row = lax.broadcasted_iota(jnp.int32, block.shape, 0) + row_start
    column = lax.broadcasted_iota(jnp.int32, block.shape, 1) + column_start
    return jnp.where(row >= column, block, 0.0)


def with_rows(value, chunk, start, rhs):
    count = rhs.shape[0]
    parts = []
    for at in range(value.shape[0] // count):
        here = (start == chunk * value.shape[0] + at * count).astype(F32)
        parts.append(value[at * count : (at + 1) * count, :] + rhs[...] * here)
    return jnp.concatenate(parts, 0) if len(parts) > 1 else parts[0]


def call(kernel, place, steps, ins, outs, scratch, args, flops, moved):
    return pl.pallas_call(
        kernel,
        grid_spec=pltpu.PrefetchScalarGridSpec(
            num_scalar_prefetch=1,
            grid=(steps,),
            in_specs=ins,
            out_specs=[spec for spec, _ in outs],
            scratch_shapes=scratch,
        ),
        out_shape=[shape for _, shape in outs],
        compiler_params=pltpu.CompilerParams(vmem_limit_bytes=VMEM),
        cost_estimate=pl.CostEstimate(flops=flops, bytes_accessed=moved, transcendentals=0),
    )(place, *args)


def held_call(kernel, place, outs, scratch, args, flops, moved, before=()):
    return pl.pallas_call(
        kernel,
        in_specs=[pl.BlockSpec(memory_space=pltpu.SMEM)]
        + [pl.BlockSpec(memory_space=pltpu.VMEM) for _ in args]
        + [pl.BlockSpec(memory_space=pl.ANY) for _ in before],
        out_specs=[pl.BlockSpec(memory_space=pltpu.VMEM) for _ in outs],
        out_shape=[jax.ShapeDtypeStruct(shape, dtype) for shape, dtype in outs],
        scratch_shapes=scratch,
        compiler_params=pltpu.CompilerParams(vmem_limit_bytes=VMEM),
        cost_estimate=pl.CostEstimate(flops=flops, bytes_accessed=moved, transcendentals=0),
    )(place, *args, *before)


def whole(shape):
    return pl.BlockSpec(shape, lambda *_: (0,) * len(shape))


def out_whole(shape, dtype):
    return whole(shape), jax.ShapeDtypeStruct(shape, dtype)


def in_steps(count, shape, dtype=None, entries=0):
    spec = pl.BlockSpec((count, *shape), lambda k, p: (k,) + (0,) * len(shape))
    return spec if dtype is None else (spec, jax.ShapeDtypeStruct((entries, *shape), dtype))


def at_rest(array):
    return pltpu.with_memory_space_constraint(array, pltpu.HBM)


def chunk_at(step, place, flip):
    return ((place[1] ^ step) << 1) | (place[0] ^ flip)


def digit(table, at):
    return (table >> (4 * at)) & (NEAR - 1)


def over(shape, index, order):
    def spec(at, per, flip):
        return pl.BlockSpec(
            shape, lambda k, p: index(chunk_at(digit(order, k * per + at), p, flip))
        )

    return spec


def columns_of(factor, chunk, depth):
    return factor[:, pl.ds(pl.multiple_of(chunk * depth, depth), depth)]


def all_of(conditions):
    return functools.reduce(jnp.logical_and, conditions)


def reduced_held(place, kernel, args, shape, scratch, flops, moved, received=None):
    coded = (shape[0] + PAD, shape[1])
    batches = BATCHES if received is None else ((0, NEAR),)
    arrivals = [received]
    if received is None:
        arrivals = []
        for first, count in batches:
            sent = held_call(
                functools.partial(kernel, 1, first, count),
                place,
                [((count, *coded), I16)],
                scratch,
                args,
                flops * count // GROUP,
                moved * count // GROUP,
            )
            arrivals.append(swap(sent[0], 1))
    kept = [None] * NEAR
    for (first, count), arrival in zip(batches, arrivals):
        steps = [digit(SENDING, at) for at in range(first, first + count)]
        outs = held_call(
            functools.partial(kernel, 0, first, count),
            place,
            [(coded, I16) if step else (shape, F32) for step in steps],
            scratch,
            [*args, arrival],
            flops * count // GROUP,
            moved * count // GROUP,
        )
        for step, out in zip(steps, outs):
            kept[step] = out
    return kept


def in_pairs(flip, first, count, values, sent, received, outs):
    for begin in range(0, count, 2):
        steps = [digit(SENDING, first + begin + at) for at in range(2)]
        both = values(steps)
        for at, step in enumerate(steps):
            if flip:
                put(sent.at[begin + at], encode(both[at]))
            else:
                value = both[at] + decode(received[begin + at])
                if step == 0:
                    outs[begin + at][...] = value
                else:
                    put(outs[begin + at], encode(value))


def leaf_low_value(size, chunk, place, block, spread, rounded, rhs):
    value = -dot(masked(block, spread, chunk, size), rounded[...])
    return with_rows(value, chunk, place[2], rhs)


def leaf_send_kernel(size, per, place, *rest):
    blocks, (leaf_rhs, inverse_t, tiles, rhs) = rest[:per], rest[per : per + 4]
    sent, forward, rounded, spread = rest[per + 4 :]

    @pl.when(pl.program_id(0) == 0)
    def _():
        inverse = inverse_t[...].T
        for at in range(leaf_rhs.shape[0] // size):
            rows = slice(at * size, (at + 1) * size)
            block = triangular(inverse[rows, :], 0, 0)
            value = jnp.dot(block, leaf_rhs[rows, :], precision=PRECISE, preferred_element_type=F32)
            forward[rows, :] = value
            rounded[rows, :] = value.astype(BF16)
        for level in range(spread.shape[0]):
            spread[level] = spread_tiles(tiles, level, spread.shape[2], size)

    values = []
    for at in range(per):
        chunk = chunk_at(digit(SENDING, pl.program_id(0) * per + at), place, 1)
        values.append(leaf_low_value(size, chunk, place, blocks[at][0, 0], spread, rounded, rhs))
    for at in range(per):
        put(sent.at[at], encode(values[at]))


def leaf_keep_kernel(size, flip, first, count, place, coupling, spread, rounded, rhs, received, *outs):
    def values(steps):
        chunks = [chunk_at(step, place, flip) for step in steps]
        return [
            leaf_low_value(size, chunk, place, coupling[0, chunk], spread, rounded, rhs)
            for chunk in chunks
        ]

    in_pairs(flip, first, count, values, None, received, outs)


def leaf_top_kernel(size, place, spread, rounded, coupling, part):
    group = coupling.shape[1]
    for at in range(group):
        chunk = pl.program_id(0) * group + at
        part[at] = dot(masked(coupling[0, at], spread, chunk, size), rounded[...])


def sum_kernel(final, waits, place, own, *rest):
    blocks, out = rest[: len(rest) - 1 - waits], rest[-1]
    value = own[...] if own.dtype == F32 else decode(own[...])
    for block in blocks:
        value = value + decode(block[...])
    if final:
        out[...] = value.astype(BF16)
    else:
        put(out, encode(value))


def summed(place, own, received, final, before=()):
    rows, columns = received[0].shape
    return held_call(
        functools.partial(sum_kernel, final, len(before)),
        place,
        [((rows - PAD if final else rows, columns), BF16 if final else I16)],
        [],
        [own, *received],
        rows * columns * 8,
        rows * columns * 20,
        before,
    )[0]


def reduce_and_gather(place, kept, far, final=False, before=()):
    received = [swap(kept[at], at << 1) for at in (digit(ARRIVING, n) for n in range(1, NEAR))]
    coded = summed(place, kept[0], received, final and not far, before)
    if far:
        coded = summed(place, coded, [swap(coded, offset) for offset in far], final)
    mine = [coded] + [swap(coded, digit(ARRIVING, entry) << 1) for entry in range(1, NEAR)]
    mine = jnp.stack(mine)
    return mine, swap(mine, 1)


def factor_kernel(start_at, flip, place, factor, stack, *rest):
    before, rest = (rest[0], rest[1:]) if flip else (None, rest)
    out, wide, narrow = rest[0], rest[-2], rest[-1]
    rows, size = factor.shape
    depth = size // GROUP
    columns = narrow.shape[1]
    start = place[start_at]
    wide[...] = jnp.zeros_like(wide)
    narrow[...] = jnp.zeros_like(narrow)

    @pl.loop(0, NEAR // 2)
    def _(number):
        entries = [2 * number, 2 * number + 1]
        chunks = [chunk_at(digit(ARRIVING, entry), place, flip) for entry in entries]
        below = all_of([(chunk + 1) * depth <= start + 1 for chunk in chunks])

        def add(wanted, cut):
            highs, lows, uppers, lowers = [], [], [], []
            for at in wanted:
                block = columns_of(factor, chunks[at], depth)
                high, low = halves(triangular(block, start, chunks[at] * depth) if cut else block)
                upper, lower = halves(decode(stack[entries[at]]))
                highs, lows = highs + [high], lows + [low]
                uppers, lowers = uppers + [upper], lowers + [lower]
            upper = jnp.concatenate(uppers, 0)
            both = jnp.concatenate([upper, jnp.concatenate(lowers, 0)], 1)
            wide[...] += dot(jnp.concatenate(highs, 1), both)
            narrow[...] += dot(jnp.concatenate(lows, 1), upper)

        @pl.when(below)
        def _():
            add(range(2), False)

        for at in range(2):

            @pl.when(jnp.logical_not(below) & (chunks[at] * depth < start + rows))
            def _(at=at):
                add([at], True)

    value = wide[:, :columns] + wide[:, columns:] + narrow[...]
    if flip:
        value = value + before[...]
        rest[1][...] = value.T
    out[...] = value


def factor_apply(place, factor, stacks, start_at):
    count, size = factor.shape
    columns = stacks[0].shape[2]
    result = ()
    for flip in range(2):
        result = held_call(
            functools.partial(factor_kernel, start_at, flip),
            place,
            [((count, columns), F32)] + [((columns, count), F32)] * flip,
            [pltpu.VMEM((count, 2 * columns), F32), pltpu.VMEM((count, columns), F32)],
            [factor, stacks[flip], *result],
            4 * count * size * columns,
            2 * count * size,
        )
    return result


def coupled_kernel(flip, first, count, place, coupling, part, rows, rhs, *rest):
    packed = rest[-1]
    columns = rows.shape[1]
    high, low = halves(rows[...])
    packed[:, :columns] = high
    packed[:, columns:] = low

    def values(steps):
        result = []
        for step in steps:
            chunk = chunk_at(step, place, flip)
            high, low = halves(coupling[chunk])
            product = dot(high, packed[...])
            value = product[:, :columns] + product[:, columns:] + dot(low, packed[:, :columns])
            result.append(with_rows(-(part[chunk] + value), chunk, place[3], rhs))
        return result

    in_pairs(flip, first, count, values, rest[0], rest[0], rest[1:-1])


def back_kernel(start_at, flip, first, count, place, factor, vector, *rest):
    packed, total = rest[-2:]
    columns = vector.shape[0]
    rows, size = factor.shape
    depth = size // GROUP
    start = place[start_at]
    high, low = halves(vector[...])
    packed[:columns, :] = high
    packed[columns:, :] = low

    def values(steps):
        chunks = [chunk_at(step, place, flip) for step in steps]
        below = all_of([(chunk + 1) * depth <= start + 1 for chunk in chunks])
        above = all_of([chunk * depth >= start + rows for chunk in chunks])

        def products(cut):
            for at, chunk in enumerate(chunks):
                block = columns_of(factor, chunk, depth)
                high, low = halves(triangular(block, start, chunk * depth) if cut else block)
                product = dot(packed[...], high)
                total[at] = (
                    product[:columns, :] + product[columns:, :] + dot(packed[:columns, :], low)
                )

        @pl.when(below)
        def _():
            products(False)

        @pl.when(above)
        def _():
            total[...] = jnp.zeros_like(total)

        @pl.when(jnp.logical_not(below | above))
        def _():
            products(True)

        return [total[at] for at in range(len(chunks))]

    in_pairs(flip, first, count, values, rest[0], rest[0], rest[1:-2])


def back_apply(place, factor, vector, start_at):
    count, size = factor.shape
    columns = vector.shape[0]
    chunk = size // GROUP
    return reduced_held(
        place,
        functools.partial(back_kernel, start_at),
        [factor, vector],
        (columns, chunk),
        [pltpu.VMEM((2 * columns, count), BF16), pltpu.VMEM((2, columns, chunk), F32)],
        8 * count * size * columns,
        4 * count * size,
    )


def carry_kernel(flip, place, coupling, stack, before, gap, rounded, wide, narrow):
    columns = before.shape[0]
    wide[...] = jnp.zeros_like(wide)
    narrow[...] = jnp.zeros_like(narrow)

    @pl.loop(0, NEAR // 2)
    def _(number):
        @pl.when(number >= 0)
        def _():
            highs, lows, uppers, lowers = [], [], [], []
            for at in range(2):
                entry = 2 * number + at
                high, low = halves(coupling[chunk_at(digit(ARRIVING, entry), place, flip)])
                upper, lower = halves(decode(stack[entry]))
                rounded[entry] = upper
                highs, lows = highs + [high], lows + [low]
                uppers, lowers = uppers + [upper], lowers + [lower]
            upper = jnp.concatenate(uppers, 1)
            both = jnp.concatenate([upper, jnp.concatenate(lowers, 1)], 0)
            wide[...] += dot(both, jnp.concatenate(highs, 0))
            narrow[...] += dot(upper, jnp.concatenate(lows, 0))

    gap[...] = before[...] - (wide[:columns, :] + wide[columns:, :] + narrow[...])


def own_kernel(place, mine, other, out):
    chunk = place[3] // out.shape[0]
    here = (chunk % 2 == place[0]).astype(F32)
    out[...] = (decode(mine[0]) * here + decode(other[0]) * (1.0 - here)).T


def leaf_product(size, flip, per, place, blocks, spread, path):
    left, right = [], []
    for at in range(per):
        chunk = chunk_at(digit(ARRIVING, pl.program_id(0) * per + at), place, flip)
        left.append(path[at])
        right.append(masked(blocks[at][0, 0], spread, chunk, size))
    return dot(jnp.concatenate(left, 1), jnp.concatenate(right, 0))


def leaf_back_top_kernel(size, per, place, *rest):
    near, far, (spread, mine, other, out) = rest[:per], rest[per : 2 * per], rest[2 * per :]

    @pl.when(pl.program_id(0) == 0)
    def _():
        out[...] = jnp.zeros_like(out)

    @pl.when(pl.program_id(0) >= 0)
    def _():
        out[...] += leaf_product(size, 0, per, place, near, spread, mine)
        out[...] += leaf_product(size, 1, per, place, far, spread, other)


def leaf_back_kernel(size, flip, per, place, *rest):
    blocks, (spread, path, before), rest = rest[:per], rest[per : per + 3], rest[per + 3 :]
    out, total = rest[-2:]

    @pl.when(pl.program_id(0) == 0)
    def _():
        total[...] = before[...]

    @pl.when(pl.program_id(0) >= 0)
    def _():
        total[...] += leaf_product(size, flip, per, place, blocks, spread, path)

    @pl.when(pl.program_id(0) == pl.num_programs(0) - 1)
    def _():
        if not flip:
            out[...] = total[...]
        else:
            forward, inverse_t = rest[:2]
            gap = forward[...] - total[...].T
            inverse = inverse_t[...].T
            for at in range(gap.shape[0] // size):
                rows = slice(at * size, (at + 1) * size)
                block = triangular(inverse[rows, :], 0, 0).T
                out[rows, :] = jnp.dot(
                    block, gap[rows, :], precision=PRECISE, preferred_element_type=F32
                )


def body(
    leaf_rhs,
    leaf_inverse,
    leaf_coupling,
    tile_mask,
    low_rhs,
    top_rhs,
    low_inverse,
    top_inverse,
    low_coupling,
):
    device_total = lax.axis_size("leaf") * lax.axis_size("sep")
    device = lax.axis_index("leaf") * lax.axis_size("sep") + lax.axis_index("sep")
    local_rows, columns = leaf_rhs.shape
    size = leaf_inverse.shape[1]
    levels = leaf_coupling.shape[0]
    sep_size = low_inverse.shape[1]
    low_count = low_inverse.shape[0]
    top_count = top_inverse.shape[0]
    chunk = sep_size // GROUP
    low_far = list(range(GROUP, device_total // 2, GROUP))
    top_far = list(range(GROUP, device_total, GROUP))
    low_start = device % (device_total // 2) * low_count
    top_start = device * top_count
    place = jnp.stack([device % 2, device % GROUP // 2, low_start, top_start]).astype(jnp.int32)

    inverse_t = leaf_inverse.T
    tiles = at_rest(jnp.transpose(tile_mask, (2, 0, 1)))
    coupling = leaf_coupling.reshape(levels, GROUP, chunk, local_rows)
    low_blocks = low_coupling.reshape(GROUP, chunk, low_count)

    leaf_flops = 2 * sep_size * local_rows * columns
    leaf_moved = 2 * sep_size * local_rows
    leaf_low = over((1, 1, chunk, local_rows), lambda c: (0, c, 0, 0), SENDING)
    leaf_back = over((1, 1, chunk, local_rows), lambda c: (0, c, 0, 0), ARRIVING)
    leaf_top = over((1, 1, chunk, local_rows), lambda c: (1, c, 0, 0), ARRIVING)
    spread_shape = (levels, sep_size // size, local_rows)

    per = 4
    coded = (chunk + PAD, columns)
    sent, forward_leaf, rounded_leaf, spread = call(
        functools.partial(leaf_send_kernel, size, per),
        place,
        NEAR // per,
        [leaf_low(at, per, 1) for at in range(per)]
        + [whole(a.shape) for a in (leaf_rhs, inverse_t, tiles, low_rhs)],
        [
            in_steps(per, coded, I16, NEAR),
            out_whole(leaf_rhs.shape, F32),
            out_whole(leaf_rhs.shape, BF16),
            out_whole(spread_shape, F32),
        ],
        [],
        [at_rest(coupling)] * per + [at_rest(leaf_rhs), at_rest(inverse_t), tiles, at_rest(low_rhs)],
        leaf_flops // 2,
        leaf_moved // 2,
    )

    kept = reduced_held(
        place,
        functools.partial(leaf_keep_kernel, size),
        [coupling, spread, rounded_leaf, low_rhs],
        (chunk, columns),
        [],
        leaf_flops,
        leaf_moved,
        swap(sent, 1),
    )
    part = call(
        functools.partial(leaf_top_kernel, size),
        place,
        GROUP // per,
        [
            pl.BlockSpec((1, *spread_shape[1:]), lambda k, p: (1, 0, 0)),
            whole(rounded_leaf.shape),
            pl.BlockSpec((1, per, chunk, local_rows), lambda k, p: (1, k, 0, 0)),
        ],
        [in_steps(per, (chunk, columns), F32, GROUP)],
        [],
        [spread, rounded_leaf, at_rest(coupling)],
        leaf_flops,
        leaf_moved,
    )[0]
    first_input = reduce_and_gather(place, kept, low_far, before=[part])
    first_rows, first_columns = factor_apply(place, low_inverse, first_input, 2)

    coupled_flops = 8 * sep_size * low_count * columns
    coupled_moved = 4 * sep_size * low_count
    kept = reduced_held(
        place,
        coupled_kernel,
        [low_blocks, part, first_rows, top_rhs],
        (chunk, columns),
        [pltpu.VMEM((low_count, 2 * columns), BF16)],
        coupled_flops,
        coupled_moved,
    )
    top_input = reduce_and_gather(place, kept, top_far)
    _, forward_columns = factor_apply(place, top_inverse, top_input, 3)

    kept = back_apply(place, top_inverse, forward_columns, 3)
    solution_blocks = reduce_and_gather(place, kept, top_far)
    turned = (columns, chunk)
    gap, rounded = first_columns, []
    for flip in range(2):
        gap, near = held_call(
            functools.partial(carry_kernel, flip),
            place,
            [(gap.shape, F32), ((NEAR, *turned), BF16)],
            [pltpu.VMEM((2 * columns, low_count), F32), pltpu.VMEM((columns, low_count), F32)],
            [low_blocks, solution_blocks[flip], gap],
            coupled_flops // 2,
            coupled_moved // 2,
        )
        rounded.append(near)
    top_own = call(
        own_kernel,
        place,
        1,
        [
            pl.BlockSpec(
                (1, *s.shape[1:]), lambda k, p: (digit(PLACE_OF, (p[3] // chunk // 2) ^ p[1]), 0, 0)
            )
            for s in solution_blocks
        ],
        [out_whole((chunk, columns), F32)],
        [],
        list(solution_blocks),
        chunk * columns,
        8 * chunk * columns,
    )[0]
    top_solution = lax.dynamic_slice_in_dim(top_own, top_start % chunk, top_count, 0)
    kept = back_apply(place, low_inverse, gap, 2)
    per = 2
    back_top = call(
        functools.partial(leaf_back_top_kernel, size, per),
        place,
        NEAR // per,
        [leaf_top(at, per, flip) for flip in range(2) for at in range(per)]
        + [pl.BlockSpec((1, *spread_shape[1:]), lambda k, p: (1, 0, 0))]
        + [in_steps(per, turned)] * 2,
        [out_whole((columns, local_rows), F32)],
        [],
        [at_rest(coupling)] * (2 * per) + [spread, *rounded],
        leaf_flops,
        leaf_moved,
    )[0]
    path = reduce_and_gather(place, kept, low_far, True, [back_top, top_own])
    per = 4
    result = back_top
    for flip in range(2):
        last = [forward_leaf, inverse_t] if flip else []
        result = call(
            functools.partial(leaf_back_kernel, size, flip, per),
            place,
            NEAR // per,
            [leaf_back(at, per, flip) for at in range(per)]
            + [pl.BlockSpec((1, *spread_shape[1:]), lambda k, p: (0, 0, 0))]
            + [in_steps(per, turned), whole(result.shape)]
            + [whole(a.shape) for a in last],
            [out_whole((local_rows, columns) if flip else (columns, local_rows), F32)],
            [pltpu.VMEM((columns, local_rows), F32)],
            [at_rest(coupling)] * per + [spread, path[flip], result, *last],
            leaf_flops // 2,
            leaf_moved // 2,
        )[0]
    return result, top_solution


def solution(mesh):
    return jax.shard_map(
        body,
        mesh=mesh,
        in_specs=(
            P(("leaf", "sep"), None),
            P(("leaf", "sep"), None),
            P(None, None, ("leaf", "sep")),
            P(None, None, ("leaf", "sep")),
            P(("leaf", "sep"), None),
            P(("leaf", "sep"), None),
            P(("leaf", "sep"), None),
            P(("leaf", "sep"), None),
            P(None, ("leaf", "sep")),
        ),
        out_specs=(P(("leaf", "sep"), None), P(("leaf", "sep"), None)),
        check_vma=False,
    )
```

```python
import functools

import jax
import jax.numpy as jnp
from jax import lax
from jax.experimental import pallas as pl
from jax.experimental.pallas import tpu as pltpu
from jax.sharding import PartitionSpec as P

PRECISE = lax.Precision.HIGHEST
F32 = jnp.float32
BF16 = jnp.bfloat16
I16 = jnp.int16
AXES = ("leaf", "sep")
NEAR = 8
GROUP = 2 * NEAR
BATCHES = ((0, 4), (4, 4))
SENDING = 0x32107654
ARRIVING = 0x12345670
PLACE_OF = 0x12345670
PAD = 16
VMEM = 8 << 20


def swap(block, offset):
    count = lax.axis_size("leaf") * lax.axis_size("sep")
    return lax.ppermute(block, AXES, [(at, at ^ offset) for at in range(count)])


def exchange(blocks):
    count = lax.axis_size("leaf") * lax.axis_size("sep")
    groups = [
        [first + 2 * at + core for at in range(NEAR)]
        for first in range(0, count, GROUP)
        for core in range(2)
    ]
    return lax.all_to_all(blocks, AXES, 0, 0, axis_index_groups=groups)


def encode(value):
    peak = jnp.maximum(jnp.max(jnp.abs(value), axis=0, keepdims=True), 1e-30)
    power = jnp.ceil(jnp.log2(peak))
    part = jnp.ceil(peak * jnp.exp2(14.0 - power))
    scale = 32767.0 / (part * jnp.exp2(power - 14.0))
    code = jnp.floor(value * scale + 0.5).astype(jnp.int32).astype(I16)
    row = lax.broadcasted_iota(jnp.int32, (PAD, value.shape[1]), 0)
    return code, jnp.where(row == 0, power, part).astype(jnp.int32).astype(I16)


def put(ref, coded):
    code, head = coded
    rows = code.shape[0]
    ref[:rows, :] = code
    ref[rows:, :] = head


def decode(block):
    rows = block.shape[0] - PAD
    head = block[rows:, :].astype(jnp.int32).astype(F32)
    scale = head[1:2, :] * jnp.exp2(head[0:1, :] - 14.0) * (1.0 / 32767.0)
    return block[:rows, :].astype(jnp.int32).astype(F32) * scale


def halves(value):
    high = value.astype(BF16)
    return high, (value - high.astype(F32)).astype(BF16)


def dot(left, right):
    return jnp.dot(left, right, preferred_element_type=F32)


def spread_tiles(tiles, level, width, size):
    across = tiles.shape[0]
    flags = tiles[:, level, :].astype(F32).T
    lane = lax.broadcasted_iota(jnp.int32, (flags.shape[0], width), 1) // size
    spread = jnp.zeros((flags.shape[0], width), F32)
    for at in range(across):
        spread = jnp.where(lane == at, flags[:, at : at + 1], spread)
    return spread


def masked(block, spread, chunk, size):
    width = block.shape[1]
    count = block.shape[0] // size
    flags = spread[0, pl.ds(pl.multiple_of(chunk * count, count), count), :]
    parts = []
    for at in range(count):
        row = jnp.broadcast_to(flags[at : at + 1, :], (16, width)).astype(BF16)
        tile = block[at * size : (at + 1) * size, :].reshape(size // 16, 16, width)
        parts.append((tile * row[None]).reshape(size, width))
    return jnp.concatenate(parts, 0)


def triangular(block, row_start, column_start):
    row = lax.broadcasted_iota(jnp.int32, block.shape, 0) + row_start
    column = lax.broadcasted_iota(jnp.int32, block.shape, 1) + column_start
    return jnp.where(row >= column, block, 0.0)


def with_rows(value, chunk, start, rhs):
    count = rhs.shape[0]
    parts = []
    for at in range(value.shape[0] // count):
        here = (start == chunk * value.shape[0] + at * count).astype(F32)
        parts.append(value[at * count : (at + 1) * count, :] + rhs[...] * here)
    return jnp.concatenate(parts, 0) if len(parts) > 1 else parts[0]


def call(kernel, place, steps, ins, outs, scratch, args, flops, moved):
    return pl.pallas_call(
        kernel,
        grid_spec=pltpu.PrefetchScalarGridSpec(
            num_scalar_prefetch=1,
            grid=(steps,),
            in_specs=ins,
            out_specs=[spec for spec, _ in outs],
            scratch_shapes=scratch,
        ),
        out_shape=[shape for _, shape in outs],
        compiler_params=pltpu.CompilerParams(vmem_limit_bytes=VMEM),
        cost_estimate=pl.CostEstimate(flops=flops, bytes_accessed=moved, transcendentals=0),
    )(place, *args)


def held_call(kernel, place, outs, scratch, args, flops, moved, before=()):
    return pl.pallas_call(
        kernel,
        in_specs=[pl.BlockSpec(memory_space=pltpu.SMEM)]
        + [pl.BlockSpec(memory_space=pltpu.VMEM) for _ in args]
        + [pl.BlockSpec(memory_space=pl.ANY) for _ in before],
        out_specs=[pl.BlockSpec(memory_space=pltpu.VMEM) for _ in outs],
        out_shape=[jax.ShapeDtypeStruct(shape, dtype) for shape, dtype in outs],
        scratch_shapes=scratch,
        compiler_params=pltpu.CompilerParams(vmem_limit_bytes=VMEM),
        cost_estimate=pl.CostEstimate(flops=flops, bytes_accessed=moved, transcendentals=0),
    )(place, *args, *before)


def whole(shape):
    return pl.BlockSpec(shape, lambda *_: (0,) * len(shape))


def out_whole(shape, dtype):
    return whole(shape), jax.ShapeDtypeStruct(shape, dtype)


def in_steps(count, shape, dtype=None, entries=0):
    spec = pl.BlockSpec((count, *shape), lambda k, p: (k,) + (0,) * len(shape))
    return spec if dtype is None else (spec, jax.ShapeDtypeStruct((entries, *shape), dtype))


def at_rest(array):
    return pltpu.with_memory_space_constraint(array, pltpu.HBM)


def chunk_at(step, place, flip):
    return ((place[1] ^ step) << 1) | (place[0] ^ flip)


def digit(table, at):
    return (table >> (4 * at)) & (NEAR - 1)


def over(shape, index, order):
    def spec(at, per, flip):
        return pl.BlockSpec(
            shape, lambda k, p: index(chunk_at(digit(order, k * per + at), p, flip))
        )

    return spec


def columns_of(factor, chunk, depth):
    return factor[:, pl.ds(pl.multiple_of(chunk * depth, depth), depth)]


def all_of(conditions):
    return functools.reduce(jnp.logical_and, conditions)


def reduced_held(place, kernel, args, shape, scratch, flops, moved, received=None):
    coded = (shape[0] + PAD, shape[1])
    batches = BATCHES if received is None else ((0, NEAR),)
    arrivals = [received]
    if received is None:
        arrivals = []
        for first, count in batches:
            sent = held_call(
                functools.partial(kernel, 1, first, count),
                place,
                [((count, *coded), I16)],
                scratch,
                args,
                flops * count // GROUP,
                moved * count // GROUP,
            )
            arrivals.append(swap(sent[0], 1))
    kept = [None] * NEAR
    for (first, count), arrival in zip(batches, arrivals):
        steps = [digit(SENDING, at) for at in range(first, first + count)]
        outs = held_call(
            functools.partial(kernel, 0, first, count),
            place,
            [(coded, I16) if step else (shape, F32) for step in steps],
            scratch,
            [*args, arrival],
            flops * count // GROUP,
            moved * count // GROUP,
        )
        for step, out in zip(steps, outs):
            kept[step] = out
    return kept


def in_pairs(flip, first, count, values, sent, received, outs):
    for begin in range(0, count, 2):
        steps = [digit(SENDING, first + begin + at) for at in range(2)]
        both = values(steps)
        for at, step in enumerate(steps):
            if flip:
                put(sent.at[begin + at], encode(both[at]))
            else:
                value = both[at] + decode(received[begin + at])
                if step == 0:
                    outs[begin + at][...] = value
                else:
                    put(outs[begin + at], encode(value))


def leaf_low_value(size, chunk, place, block, spread, rounded, rhs):
    value = -dot(masked(block, spread, chunk, size), rounded[...])
    return with_rows(value, chunk, place[2], rhs)


def leaf_send_kernel(size, per, place, *rest):
    blocks, (leaf_rhs, inverse_t, tiles, rhs) = rest[:per], rest[per : per + 4]
    sent, forward, rounded, spread = rest[per + 4 :]

    @pl.when(pl.program_id(0) == 0)
    def _():
        inverse = inverse_t[...].T
        for at in range(leaf_rhs.shape[0] // size):
            rows = slice(at * size, (at + 1) * size)
            block = triangular(inverse[rows, :], 0, 0)
            value = jnp.dot(block, leaf_rhs[rows, :], precision=PRECISE, preferred_element_type=F32)
            forward[rows, :] = value
            rounded[rows, :] = value.astype(BF16)
        for level in range(spread.shape[0]):
            spread[level] = spread_tiles(tiles, level, spread.shape[2], size)

    values = []
    for at in range(per):
        chunk = chunk_at(digit(SENDING, pl.program_id(0) * per + at), place, 1)
        values.append(leaf_low_value(size, chunk, place, blocks[at][0, 0], spread, rounded, rhs))
    for at in range(per):
        put(sent.at[at], encode(values[at]))


def leaf_keep_kernel(size, flip, first, count, place, coupling, spread, rounded, rhs, received, *outs):
    def values(steps):
        chunks = [chunk_at(step, place, flip) for step in steps]
        return [
            leaf_low_value(size, chunk, place, coupling[0, chunk], spread, rounded, rhs)
            for chunk in chunks
        ]

    in_pairs(flip, first, count, values, None, received, outs)


def leaf_top_kernel(size, place, spread, rounded, coupling, part):
    group = coupling.shape[1]
    for at in range(group):
        chunk = pl.program_id(0) * group + at
        part[at] = dot(masked(coupling[0, at], spread, chunk, size), rounded[...])


def sum_kernel(final, waits, place, own, *rest):
    blocks, out = rest[: len(rest) - 1 - waits], rest[-1]
    value = own[...] if own.dtype == F32 else decode(own[...])
    for block in blocks:
        value = value + decode(block[...])
    if final:
        rounded = value.astype(BF16)
        for at in range(NEAR):
            out[at] = rounded
    else:
        put(out, encode(value))


def summed(place, own, received, final, before=()):
    rows, columns = received[0].shape
    return held_call(
        functools.partial(sum_kernel, final, len(before)),
        place,
        [((NEAR, rows - PAD, columns), BF16) if final else ((rows, columns), I16)],
        [],
        [own, *received],
        rows * columns * 8,
        rows * columns * 20,
        before,
    )[0]


def reduce_and_gather(place, kept, far, final=False, before=()):
    received = [swap(kept[at], at << 1) for at in (digit(ARRIVING, n) for n in range(1, NEAR))]
    coded = summed(place, kept[0], received, final and not far, before)
    if far:
        coded = summed(place, coded, [swap(coded, offset) for offset in far], final)
    if final:
        mine = exchange(coded)
        return mine, swap(mine, 1)
    mine = [coded] + [swap(coded, digit(ARRIVING, entry) << 1) for entry in range(1, NEAR)]
    mine = jnp.stack(mine)
    return mine, swap(mine, 1)


def factor_kernel(start_at, flip, place, factor, stack, *rest):
    before, rest = (rest[0], rest[1:]) if flip else (None, rest)
    out, wide, narrow = rest[0], rest[-2], rest[-1]
    rows, size = factor.shape
    depth = size // GROUP
    columns = narrow.shape[1]
    start = place[start_at]
    wide[...] = jnp.zeros_like(wide)
    narrow[...] = jnp.zeros_like(narrow)

    @pl.loop(0, NEAR // 2)
    def _(number):
        entries = [2 * number, 2 * number + 1]
        chunks = [chunk_at(digit(ARRIVING, entry), place, flip) for entry in entries]
        below = all_of([(chunk + 1) * depth <= start + 1 for chunk in chunks])

        def add(wanted, cut):
            highs, lows, uppers, lowers = [], [], [], []
            for at in wanted:
                block = columns_of(factor, chunks[at], depth)
                high, low = halves(triangular(block, start, chunks[at] * depth) if cut else block)
                upper, lower = halves(decode(stack[entries[at]]))
                highs, lows = highs + [high], lows + [low]
                uppers, lowers = uppers + [upper], lowers + [lower]
            upper = jnp.concatenate(uppers, 0)
            both = jnp.concatenate([upper, jnp.concatenate(lowers, 0)], 1)
            wide[...] += dot(jnp.concatenate(highs, 1), both)
            narrow[...] += dot(jnp.concatenate(lows, 1), upper)

        @pl.when(below)
        def _():
            add(range(2), False)

        for at in range(2):

            @pl.when(jnp.logical_not(below) & (chunks[at] * depth < start + rows))
            def _(at=at):
                add([at], True)

    value = wide[:, :columns] + wide[:, columns:] + narrow[...]
    if flip:
        value = value + before[...]
        rest[1][...] = value.T
    out[...] = value


def factor_apply(place, factor, stacks, start_at):
    count, size = factor.shape
    columns = stacks[0].shape[2]
    result = ()
    for flip in range(2):
        result = held_call(
            functools.partial(factor_kernel, start_at, flip),
            place,
            [((count, columns), F32)] + [((columns, count), F32)] * flip,
            [pltpu.VMEM((count, 2 * columns), F32), pltpu.VMEM((count, columns), F32)],
            [factor, stacks[flip], *result],
            4 * count * size * columns,
            2 * count * size,
        )
    return result


def coupled_kernel(flip, first, count, place, coupling, part, rows, rhs, *rest):
    packed = rest[-1]
    columns = rows.shape[1]
    high, low = halves(rows[...])
    packed[:, :columns] = high
    packed[:, columns:] = low

    def values(steps):
        result = []
        for step in steps:
            chunk = chunk_at(step, place, flip)
            high, low = halves(coupling[chunk])
            product = dot(high, packed[...])
            value = product[:, :columns] + product[:, columns:] + dot(low, packed[:, :columns])
            result.append(with_rows(-(part[chunk] + value), chunk, place[3], rhs))
        return result

    in_pairs(flip, first, count, values, rest[0], rest[0], rest[1:-1])


def back_kernel(start_at, flip, first, count, place, factor, vector, *rest):
    packed, total = rest[-2:]
    columns = vector.shape[0]
    rows, size = factor.shape
    depth = size // GROUP
    start = place[start_at]
    high, low = halves(vector[...])
    packed[:columns, :] = high
    packed[columns:, :] = low

    def values(steps):
        chunks = [chunk_at(step, place, flip) for step in steps]
        below = all_of([(chunk + 1) * depth <= start + 1 for chunk in chunks])
        above = all_of([chunk * depth >= start + rows for chunk in chunks])

        def products(cut):
            for at, chunk in enumerate(chunks):
                block = columns_of(factor, chunk, depth)
                high, low = halves(triangular(block, start, chunk * depth) if cut else block)
                product = dot(packed[...], high)
                total[at] = (
                    product[:columns, :] + product[columns:, :] + dot(packed[:columns, :], low)
                )

        @pl.when(below)
        def _():
            products(False)

        @pl.when(above)
        def _():
            total[...] = jnp.zeros_like(total)

        @pl.when(jnp.logical_not(below | above))
        def _():
            products(True)

        return [total[at] for at in range(len(chunks))]

    in_pairs(flip, first, count, values, rest[0], rest[0], rest[1:-2])


def back_apply(place, factor, vector, start_at):
    count, size = factor.shape
    columns = vector.shape[0]
    chunk = size // GROUP
    return reduced_held(
        place,
        functools.partial(back_kernel, start_at),
        [factor, vector],
        (columns, chunk),
        [pltpu.VMEM((2 * columns, count), BF16), pltpu.VMEM((2, columns, chunk), F32)],
        8 * count * size * columns,
        4 * count * size,
    )


def carry_kernel(flip, place, coupling, stack, before, gap, rounded, wide, narrow):
    columns = before.shape[0]
    wide[...] = jnp.zeros_like(wide)
    narrow[...] = jnp.zeros_like(narrow)

    @pl.loop(0, NEAR // 2)
    def _(number):
        @pl.when(number >= 0)
        def _():
            highs, lows, uppers, lowers = [], [], [], []
            for at in range(2):
                entry = 2 * number + at
                high, low = halves(coupling[chunk_at(digit(ARRIVING, entry), place, flip)])
                upper, lower = halves(decode(stack[entry]))
                rounded[entry] = upper
                highs, lows = highs + [high], lows + [low]
                uppers, lowers = uppers + [upper], lowers + [lower]
            upper = jnp.concatenate(uppers, 1)
            both = jnp.concatenate([upper, jnp.concatenate(lowers, 1)], 0)
            wide[...] += dot(both, jnp.concatenate(highs, 0))
            narrow[...] += dot(upper, jnp.concatenate(lows, 0))

    gap[...] = before[...] - (wide[:columns, :] + wide[columns:, :] + narrow[...])


def own_kernel(place, mine, other, out):
    chunk = place[3] // out.shape[0]
    here = (chunk % 2 == place[0]).astype(F32)
    out[...] = (decode(mine[0]) * here + decode(other[0]) * (1.0 - here)).T


def leaf_product(size, flip, per, place, blocks, spread, path, ordered=False):
    left, right = [], []
    for at in range(per):
        entry = pl.program_id(0) * per + at
        if ordered:
            chunk = (entry << 1) | (place[0] ^ flip)
        else:
            chunk = chunk_at(digit(ARRIVING, entry), place, flip)
        left.append(path[at])
        right.append(masked(blocks[at][0, 0], spread, chunk, size))
    return dot(jnp.concatenate(left, 1), jnp.concatenate(right, 0))


def leaf_back_top_kernel(size, per, place, *rest):
    near, far, (spread, mine, other, out) = rest[:per], rest[per : 2 * per], rest[2 * per :]

    @pl.when(pl.program_id(0) == 0)
    def _():
        out[...] = jnp.zeros_like(out)

    @pl.when(pl.program_id(0) >= 0)
    def _():
        out[...] += leaf_product(size, 0, per, place, near, spread, mine)
        out[...] += leaf_product(size, 1, per, place, far, spread, other)


def leaf_back_kernel(size, flip, per, place, *rest):
    blocks, (spread, path, before), rest = rest[:per], rest[per : per + 3], rest[per + 3 :]
    out, total = rest[-2:]

    @pl.when(pl.program_id(0) == 0)
    def _():
        total[...] = before[...]

    @pl.when(pl.program_id(0) >= 0)
    def _():
        total[...] += leaf_product(size, flip, per, place, blocks, spread, path, True)

    @pl.when(pl.program_id(0) == pl.num_programs(0) - 1)
    def _():
        if not flip:
            out[...] = total[...]
        else:
            forward, inverse_t = rest[:2]
            gap = forward[...] - total[...].T
            inverse = inverse_t[...].T
            for at in range(gap.shape[0] // size):
                rows = slice(at * size, (at + 1) * size)
                block = triangular(inverse[rows, :], 0, 0).T
                out[rows, :] = jnp.dot(
                    block, gap[rows, :], precision=PRECISE, preferred_element_type=F32
                )


def body(
    leaf_rhs,
    leaf_inverse,
    leaf_coupling,
    tile_mask,
    low_rhs,
    top_rhs,
    low_inverse,
    top_inverse,
    low_coupling,
):
    device_total = lax.axis_size("leaf") * lax.axis_size("sep")
    device = lax.axis_index("leaf") * lax.axis_size("sep") + lax.axis_index("sep")
    local_rows, columns = leaf_rhs.shape
    size = leaf_inverse.shape[1]
    levels = leaf_coupling.shape[0]
    sep_size = low_inverse.shape[1]
    low_count = low_inverse.shape[0]
    top_count = top_inverse.shape[0]
    chunk = sep_size // GROUP
    low_far = list(range(GROUP, device_total // 2, GROUP))
    top_far = list(range(GROUP, device_total, GROUP))
    low_start = device % (device_total // 2) * low_count
    top_start = device * top_count
    place = jnp.stack([device % 2, device % GROUP // 2, low_start, top_start]).astype(jnp.int32)

    inverse_t = leaf_inverse.T
    tiles = at_rest(jnp.transpose(tile_mask, (2, 0, 1)))
    coupling = leaf_coupling.reshape(levels, GROUP, chunk, local_rows)
    low_blocks = low_coupling.reshape(GROUP, chunk, low_count)

    leaf_flops = 2 * sep_size * local_rows * columns
    leaf_moved = 2 * sep_size * local_rows
    leaf_low = over((1, 1, chunk, local_rows), lambda c: (0, c, 0, 0), SENDING)
    leaf_top = over((1, 1, chunk, local_rows), lambda c: (1, c, 0, 0), ARRIVING)
    spread_shape = (levels, sep_size // size, local_rows)

    per = 4
    coded = (chunk + PAD, columns)
    sent, forward_leaf, rounded_leaf, spread = call(
        functools.partial(leaf_send_kernel, size, per),
        place,
        NEAR // per,
        [leaf_low(at, per, 1) for at in range(per)]
        + [whole(a.shape) for a in (leaf_rhs, inverse_t, tiles, low_rhs)],
        [
            in_steps(per, coded, I16, NEAR),
            out_whole(leaf_rhs.shape, F32),
            out_whole(leaf_rhs.shape, BF16),
            out_whole(spread_shape, F32),
        ],
        [],
        [at_rest(coupling)] * per + [at_rest(leaf_rhs), at_rest(inverse_t), tiles, at_rest(low_rhs)],
        leaf_flops // 2,
        leaf_moved // 2,
    )

    kept = reduced_held(
        place,
        functools.partial(leaf_keep_kernel, size),
        [coupling, spread, rounded_leaf, low_rhs],
        (chunk, columns),
        [],
        leaf_flops,
        leaf_moved,
        swap(sent, 1),
    )
    part = call(
        functools.partial(leaf_top_kernel, size),
        place,
        GROUP // per,
        [
            pl.BlockSpec((1, *spread_shape[1:]), lambda k, p: (1, 0, 0)),
            whole(rounded_leaf.shape),
            pl.BlockSpec((1, per, chunk, local_rows), lambda k, p: (1, k, 0, 0)),
        ],
        [in_steps(per, (chunk, columns), F32, GROUP)],
        [],
        [spread, rounded_leaf, at_rest(coupling)],
        leaf_flops,
        leaf_moved,
    )[0]
    first_input = reduce_and_gather(place, kept, low_far, before=[part])
    first_rows, first_columns = factor_apply(place, low_inverse, first_input, 2)

    coupled_flops = 8 * sep_size * low_count * columns
    coupled_moved = 4 * sep_size * low_count
    kept = reduced_held(
        place,
        coupled_kernel,
        [low_blocks, part, first_rows, top_rhs],
        (chunk, columns),
        [pltpu.VMEM((low_count, 2 * columns), BF16)],
        coupled_flops,
        coupled_moved,
    )
    top_input = reduce_and_gather(place, kept, top_far)
    _, forward_columns = factor_apply(place, top_inverse, top_input, 3)

    kept = back_apply(place, top_inverse, forward_columns, 3)
    solution_blocks = reduce_and_gather(place, kept, top_far)
    turned = (columns, chunk)
    gap, rounded = first_columns, []
    for flip in range(2):
        gap, near = held_call(
            functools.partial(carry_kernel, flip),
            place,
            [(gap.shape, F32), ((NEAR, *turned), BF16)],
            [pltpu.VMEM((2 * columns, low_count), F32), pltpu.VMEM((columns, low_count), F32)],
            [low_blocks, solution_blocks[flip], gap],
            coupled_flops // 2,
            coupled_moved // 2,
        )
        rounded.append(near)
    top_own = call(
        own_kernel,
        place,
        1,
        [
            pl.BlockSpec(
                (1, *s.shape[1:]), lambda k, p: (digit(PLACE_OF, (p[3] // chunk // 2) ^ p[1]), 0, 0)
            )
            for s in solution_blocks
        ],
        [out_whole((chunk, columns), F32)],
        [],
        list(solution_blocks),
        chunk * columns,
        8 * chunk * columns,
    )[0]
    top_solution = lax.dynamic_slice_in_dim(top_own, top_start % chunk, top_count, 0)
    kept = back_apply(place, low_inverse, gap, 2)
    per = 2
    back_top = call(
        functools.partial(leaf_back_top_kernel, size, per),
        place,
        NEAR // per,
        [leaf_top(at, per, flip) for flip in range(2) for at in range(per)]
        + [pl.BlockSpec((1, *spread_shape[1:]), lambda k, p: (1, 0, 0))]
        + [in_steps(per, turned)] * 2,
        [out_whole((columns, local_rows), F32)],
        [],
        [at_rest(coupling)] * (2 * per) + [spread, *rounded],
        leaf_flops,
        leaf_moved,
    )[0]
    path = reduce_and_gather(place, kept, low_far, True, [back_top, top_own])
    per = 4
    result = back_top
    for flip in range(2):
        last = [forward_leaf, inverse_t] if flip else []
        result = call(
            functools.partial(leaf_back_kernel, size, flip, per),
            place,
            NEAR // per,
            [
                pl.BlockSpec(
                    (1, 1, chunk, local_rows),
                    lambda k, p, at=at, flip=flip: (0, ((k * 4 + at) << 1) | (p[0] ^ flip), 0, 0),
                )
                for at in range(per)
            ]
            + [pl.BlockSpec((1, *spread_shape[1:]), lambda k, p: (0, 0, 0))]
            + [in_steps(per, turned), whole(result.shape)]
            + [whole(a.shape) for a in last],
            [out_whole((local_rows, columns) if flip else (columns, local_rows), F32)],
            [pltpu.VMEM((columns, local_rows), F32)],
            [at_rest(coupling)] * per + [spread, path[flip], result, *last],
            leaf_flops // 2,
            leaf_moved // 2,
        )[0]
    return result, top_solution


def solution(mesh):
    return jax.shard_map(
        body,
        mesh=mesh,
        in_specs=(
            P(("leaf", "sep"), None),
            P(("leaf", "sep"), None),
            P(None, None, ("leaf", "sep")),
            P(None, None, ("leaf", "sep")),
            P(("leaf", "sep"), None),
            P(("leaf", "sep"), None),
            P(("leaf", "sep"), None),
            P(("leaf", "sep"), None),
            P(None, ("leaf", "sep")),
        ),
        out_specs=(P(("leaf", "sep"), None), P(("leaf", "sep"), None)),
        check_vma=False,
    )
```

```python
import functools

import jax
import jax.numpy as jnp
from jax import lax
from jax.experimental import pallas as pl
from jax.experimental.pallas import tpu as pltpu
from jax.sharding import PartitionSpec as P

PRECISE = lax.Precision.HIGHEST
F32 = jnp.float32
BF16 = jnp.bfloat16
I16 = jnp.int16
AXES = ("leaf", "sep")
NEAR = 8
GROUP = 2 * NEAR
BATCHES = ((0, 4), (4, 4))
SENDING = 0x32107654
ARRIVING = 0x12345670
PLACE_OF = 0x12345670
PAD = 16
VMEM = 8 << 20


def swap(block, offset):
    count = lax.axis_size("leaf") * lax.axis_size("sep")
    return lax.ppermute(block, AXES, [(at, at ^ offset) for at in range(count)])


def encode(value):
    peak = jnp.maximum(jnp.max(jnp.abs(value), axis=0, keepdims=True), 1e-30)
    power = jnp.ceil(jnp.log2(peak))
    part = jnp.ceil(peak * jnp.exp2(14.0 - power))
    scale = 32767.0 / (part * jnp.exp2(power - 14.0))
    code = jnp.floor(value * scale + 0.5).astype(jnp.int32).astype(I16)
    row = lax.broadcasted_iota(jnp.int32, (PAD, value.shape[1]), 0)
    return code, jnp.where(row == 0, power, part).astype(jnp.int32).astype(I16)


def put(ref, coded):
    code, head = coded
    rows = code.shape[0]
    ref[:rows, :] = code
    ref[rows:, :] = head


def decode(block):
    rows = block.shape[0] - PAD
    head = block[rows:, :].astype(jnp.int32).astype(F32)
    scale = head[1:2, :] * jnp.exp2(head[0:1, :] - 14.0) * (1.0 / 32767.0)
    return block[:rows, :].astype(jnp.int32).astype(F32) * scale


def halves(value):
    high = value.astype(BF16)
    return high, (value - high.astype(F32)).astype(BF16)


def dot(left, right):
    return jnp.dot(left, right, preferred_element_type=F32)


def spread_tiles(tiles, level, width, size):
    across = tiles.shape[0]
    flags = tiles[:, level, :].astype(F32).T
    lane = lax.broadcasted_iota(jnp.int32, (flags.shape[0], width), 1) // size
    spread = jnp.zeros((flags.shape[0], width), F32)
    for at in range(across):
        spread = jnp.where(lane == at, flags[:, at : at + 1], spread)
    return spread


def masked(block, spread, chunk, size):
    width = block.shape[1]
    count = block.shape[0] // size
    flags = spread[0, pl.ds(pl.multiple_of(chunk * count, count), count), :]
    parts = []
    for at in range(count):
        row = jnp.broadcast_to(flags[at : at + 1, :], (16, width)).astype(BF16)
        tile = block[at * size : (at + 1) * size, :].reshape(size // 16, 16, width)
        parts.append((tile * row[None]).reshape(size, width))
    return jnp.concatenate(parts, 0)


def triangular(block, row_start, column_start):
    row = lax.broadcasted_iota(jnp.int32, block.shape, 0) + row_start
    column = lax.broadcasted_iota(jnp.int32, block.shape, 1) + column_start
    return jnp.where(row >= column, block, 0.0)


def with_rows(value, chunk, start, rhs):
    count = rhs.shape[0]
    parts = []
    for at in range(value.shape[0] // count):
        here = (start == chunk * value.shape[0] + at * count).astype(F32)
        parts.append(value[at * count : (at + 1) * count, :] + rhs[...] * here)
    return jnp.concatenate(parts, 0) if len(parts) > 1 else parts[0]


def call(kernel, place, steps, ins, outs, scratch, args, flops, moved):
    return pl.pallas_call(
        kernel,
        grid_spec=pltpu.PrefetchScalarGridSpec(
            num_scalar_prefetch=1,
            grid=(steps,),
            in_specs=ins,
            out_specs=[spec for spec, _ in outs],
            scratch_shapes=scratch,
        ),
        out_shape=[shape for _, shape in outs],
        compiler_params=pltpu.CompilerParams(vmem_limit_bytes=VMEM),
        cost_estimate=pl.CostEstimate(flops=flops, bytes_accessed=moved, transcendentals=0),
    )(place, *args)


def held_call(kernel, place, outs, scratch, args, flops, moved, before=()):
    return pl.pallas_call(
        kernel,
        in_specs=[pl.BlockSpec(memory_space=pltpu.SMEM)]
        + [pl.BlockSpec(memory_space=pltpu.VMEM) for _ in args]
        + [pl.BlockSpec(memory_space=pl.ANY) for _ in before],
        out_specs=[pl.BlockSpec(memory_space=pltpu.VMEM) for _ in outs],
        out_shape=[jax.ShapeDtypeStruct(shape, dtype) for shape, dtype in outs],
        scratch_shapes=scratch,
        compiler_params=pltpu.CompilerParams(vmem_limit_bytes=VMEM),
        cost_estimate=pl.CostEstimate(flops=flops, bytes_accessed=moved, transcendentals=0),
    )(place, *args, *before)


def whole(shape):
    return pl.BlockSpec(shape, lambda *_: (0,) * len(shape))


def out_whole(shape, dtype):
    return whole(shape), jax.ShapeDtypeStruct(shape, dtype)


def in_steps(count, shape, dtype=None, entries=0):
    spec = pl.BlockSpec((count, *shape), lambda k, p: (k,) + (0,) * len(shape))
    return spec if dtype is None else (spec, jax.ShapeDtypeStruct((entries, *shape), dtype))


def at_rest(array):
    return pltpu.with_memory_space_constraint(array, pltpu.HBM)


def chunk_at(step, place, flip):
    return ((place[1] ^ step) << 1) | (place[0] ^ flip)


def digit(table, at):
    return (table >> (4 * at)) & (NEAR - 1)


def over(shape, index, order):
    def spec(at, per, flip):
        return pl.BlockSpec(
            shape, lambda k, p: index(chunk_at(digit(order, k * per + at), p, flip))
        )

    return spec


def columns_of(factor, chunk, depth):
    return factor[:, pl.ds(pl.multiple_of(chunk * depth, depth), depth)]


def all_of(conditions):
    return functools.reduce(jnp.logical_and, conditions)


def reduced_held(place, kernel, args, shape, scratch, flops, moved, received=None):
    coded = (shape[0] + PAD, shape[1])
    batches = BATCHES if received is None else ((0, NEAR),)
    arrivals = [received]
    if received is None:
        arrivals = []
        for first, count in batches:
            sent = held_call(
                functools.partial(kernel, 1, first, count),
                place,
                [((count, *coded), I16)],
                scratch,
                args,
                flops * count // GROUP,
                moved * count // GROUP,
            )
            arrivals.append(swap(sent[0], 1))
    kept = [None] * NEAR
    for (first, count), arrival in zip(batches, arrivals):
        steps = [digit(SENDING, at) for at in range(first, first + count)]
        outs = held_call(
            functools.partial(kernel, 0, first, count),
            place,
            [(coded, I16) if step else (shape, F32) for step in steps],
            scratch,
            [*args, arrival],
            flops * count // GROUP,
            moved * count // GROUP,
        )
        for step, out in zip(steps, outs):
            kept[step] = out
    return kept


def in_pairs(flip, first, count, values, sent, received, outs):
    def pair(begin):
        steps = [digit(SENDING, first + begin + at) for at in range(2)]
        both = values(steps)
        for at, step in enumerate(steps):
            if flip:
                put(sent.at[begin + at], encode(both[at]))
            else:
                value = both[at] + decode(received[begin + at])
                if step == 0:
                    outs[begin + at][...] = value
                else:
                    put(outs[begin + at], encode(value))

    if flip:
        pl.loop(0, count // 2)(lambda number: pair(2 * number))
    else:
        for begin in range(0, count, 2):
            pair(begin)


def leaf_low_value(size, chunk, place, block, spread, rounded, rhs):
    value = -dot(masked(block, spread, chunk, size), rounded[...])
    return with_rows(value, chunk, place[2], rhs)


def leaf_send_kernel(size, per, place, *rest):
    blocks, (leaf_rhs, inverse_t, tiles, rhs) = rest[:per], rest[per : per + 4]
    sent, forward, rounded, spread = rest[per + 4 :]

    @pl.when(pl.program_id(0) == 0)
    def _():
        inverse = inverse_t[...].T
        for at in range(leaf_rhs.shape[0] // size):
            rows = slice(at * size, (at + 1) * size)
            block = triangular(inverse[rows, :], 0, 0)
            value = jnp.dot(block, leaf_rhs[rows, :], precision=PRECISE, preferred_element_type=F32)
            forward[rows, :] = value
            rounded[rows, :] = value.astype(BF16)
        for level in range(spread.shape[0]):
            spread[level] = spread_tiles(tiles, level, spread.shape[2], size)

    values = []
    for at in range(per):
        chunk = chunk_at(digit(SENDING, pl.program_id(0) * per + at), place, 1)
        values.append(leaf_low_value(size, chunk, place, blocks[at][0, 0], spread, rounded, rhs))
    for at in range(per):
        put(sent.at[at], encode(values[at]))


def leaf_keep_kernel(size, flip, first, count, place, coupling, spread, rounded, rhs, received, *outs):
    def values(steps):
        chunks = [chunk_at(step, place, flip) for step in steps]
        return [
            leaf_low_value(size, chunk, place, coupling[0, chunk], spread, rounded, rhs)
            for chunk in chunks
        ]

    in_pairs(flip, first, count, values, None, received, outs)


def leaf_top_kernel(size, place, spread, rounded, coupling, part):
    group = coupling.shape[1]
    for at in range(group):
        chunk = pl.program_id(0) * group + at
        part[at] = dot(masked(coupling[0, at], spread, chunk, size), rounded[...])


def sum_kernel(final, waits, place, own, *rest):
    blocks, out = rest[: len(rest) - 1 - waits], rest[-1]
    value = own[...] if own.dtype == F32 else decode(own[...])
    for block in blocks:
        value = value + decode(block[...])
    if final:
        out[...] = value.astype(BF16)
    else:
        put(out, encode(value))


def summed(place, own, received, final, before=()):
    rows, columns = received[0].shape
    return held_call(
        functools.partial(sum_kernel, final, len(before)),
        place,
        [((rows - PAD if final else rows, columns), BF16 if final else I16)],
        [],
        [own, *received],
        rows * columns * 8,
        rows * columns * 20,
        before,
    )[0]


def reduce_and_gather(place, kept, far, final=False, before=()):
    received = [swap(kept[at], at << 1) for at in (digit(ARRIVING, n) for n in range(1, NEAR))]
    coded = summed(place, kept[0], received, final and not far, before)
    if far:
        coded = summed(place, coded, [swap(coded, offset) for offset in far], final)
    mine = [coded] + [swap(coded, digit(ARRIVING, entry) << 1) for entry in range(1, NEAR)]
    mine = jnp.stack(mine)
    return mine, swap(mine, 1)


def factor_kernel(start_at, flip, place, factor, stack, *rest):
    before, rest = (rest[0], rest[1:]) if flip else (None, rest)
    out, wide, narrow = rest[0], rest[-2], rest[-1]
    rows, size = factor.shape
    depth = size // GROUP
    columns = narrow.shape[1]
    start = place[start_at]
    wide[...] = jnp.zeros_like(wide)
    narrow[...] = jnp.zeros_like(narrow)

    @pl.loop(0, NEAR // 2)
    def _(number):
        entries = [2 * number, 2 * number + 1]
        chunks = [chunk_at(digit(ARRIVING, entry), place, flip) for entry in entries]
        below = all_of([(chunk + 1) * depth <= start + 1 for chunk in chunks])

        def add(wanted, cut):
            highs, lows, uppers, lowers = [], [], [], []
            for at in wanted:
                block = columns_of(factor, chunks[at], depth)
                high, low = halves(triangular(block, start, chunks[at] * depth) if cut else block)
                upper, lower = halves(decode(stack[entries[at]]))
                highs, lows = highs + [high], lows + [low]
                uppers, lowers = uppers + [upper], lowers + [lower]
            upper = jnp.concatenate(uppers, 0)
            both = jnp.concatenate([upper, jnp.concatenate(lowers, 0)], 1)
            wide[...] += dot(jnp.concatenate(highs, 1), both)
            narrow[...] += dot(jnp.concatenate(lows, 1), upper)

        @pl.when(below)
        def _():
            add(range(2), False)

        for at in range(2):

            @pl.when(jnp.logical_not(below) & (chunks[at] * depth < start + rows))
            def _(at=at):
                add([at], True)

    value = wide[:, :columns] + wide[:, columns:] + narrow[...]
    if flip:
        value = value + before[...]
        rest[1][...] = value.T
    out[...] = value


def factor_apply(place, factor, stacks, start_at):
    count, size = factor.shape
    columns = stacks[0].shape[2]
    result = ()
    for flip in range(2):
        result = held_call(
            functools.partial(factor_kernel, start_at, flip),
            place,
            [((count, columns), F32)] + [((columns, count), F32)] * flip,
            [pltpu.VMEM((count, 2 * columns), F32), pltpu.VMEM((count, columns), F32)],
            [factor, stacks[flip], *result],
            4 * count * size * columns,
            2 * count * size,
        )
    return result


def coupled_kernel(flip, first, count, place, coupling, part, rows, rhs, *rest):
    packed = rest[-1]
    columns = rows.shape[1]
    high, low = halves(rows[...])
    packed[:, :columns] = high
    packed[:, columns:] = low

    def values(steps):
        result = []
        for step in steps:
            chunk = chunk_at(step, place, flip)
            high, low = halves(coupling[chunk])
            product = dot(high, packed[...])
            value = product[:, :columns] + product[:, columns:] + dot(low, packed[:, :columns])
            result.append(with_rows(-(part[chunk] + value), chunk, place[3], rhs))
        return result

    in_pairs(flip, first, count, values, rest[0], rest[0], rest[1:-1])


def back_kernel(start_at, flip, first, count, place, factor, vector, *rest):
    packed, total = rest[-2:]
    columns = vector.shape[0]
    rows, size = factor.shape
    depth = size // GROUP
    start = place[start_at]
    high, low = halves(vector[...])
    packed[:columns, :] = high
    packed[columns:, :] = low

    def values(steps):
        chunks = [chunk_at(step, place, flip) for step in steps]
        above = all_of([chunk * depth >= start + rows for chunk in chunks])

        def products():
            for at, chunk in enumerate(chunks):
                block = columns_of(factor, chunk, depth)
                high, low = halves(triangular(block, start, chunk * depth))
                product = dot(packed[...], high)
                total[at] = (
                    product[:columns, :] + product[columns:, :] + dot(packed[:columns, :], low)
                )

        @pl.when(above)
        def _():
            total[...] = jnp.zeros_like(total)

        @pl.when(jnp.logical_not(above))
        def _():
            products()

        return [total[at] for at in range(len(chunks))]

    in_pairs(flip, first, count, values, rest[0], rest[0], rest[1:-2])


def back_apply(place, factor, vector, start_at):
    count, size = factor.shape
    columns = vector.shape[0]
    chunk = size // GROUP
    return reduced_held(
        place,
        functools.partial(back_kernel, start_at),
        [factor, vector],
        (columns, chunk),
        [pltpu.VMEM((2 * columns, count), BF16), pltpu.VMEM((2, columns, chunk), F32)],
        8 * count * size * columns,
        4 * count * size,
    )


def carry_kernel(flip, place, coupling, stack, before, gap, rounded, wide, narrow):
    columns = before.shape[0]
    wide[...] = jnp.zeros_like(wide)
    narrow[...] = jnp.zeros_like(narrow)

    @pl.loop(0, NEAR // 2)
    def _(number):
        @pl.when(number >= 0)
        def _():
            highs, lows, uppers, lowers = [], [], [], []
            for at in range(2):
                entry = 2 * number + at
                high, low = halves(coupling[chunk_at(digit(ARRIVING, entry), place, flip)])
                upper, lower = halves(decode(stack[entry]))
                rounded[entry] = upper
                highs, lows = highs + [high], lows + [low]
                uppers, lowers = uppers + [upper], lowers + [lower]
            upper = jnp.concatenate(uppers, 1)
            both = jnp.concatenate([upper, jnp.concatenate(lowers, 1)], 0)
            wide[...] += dot(both, jnp.concatenate(highs, 0))
            narrow[...] += dot(upper, jnp.concatenate(lows, 0))

    gap[...] = before[...] - (wide[:columns, :] + wide[columns:, :] + narrow[...])


def own_kernel(place, mine, other, out):
    chunk = place[3] // out.shape[0]
    here = (chunk % 2 == place[0]).astype(F32)
    out[...] = (decode(mine[0]) * here + decode(other[0]) * (1.0 - here)).T


def leaf_product(size, flip, per, place, blocks, spread, path):
    left, right = [], []
    for at in range(per):
        chunk = chunk_at(digit(ARRIVING, pl.program_id(0) * per + at), place, flip)
        left.append(path[at])
        right.append(masked(blocks[at][0, 0], spread, chunk, size))
    return dot(jnp.concatenate(left, 1), jnp.concatenate(right, 0))


def leaf_back_top_kernel(size, per, place, *rest):
    near, far, (spread, mine, other, out) = rest[:per], rest[per : 2 * per], rest[2 * per :]

    @pl.when(pl.program_id(0) == 0)
    def _():
        out[...] = jnp.zeros_like(out)

    @pl.when(pl.program_id(0) >= 0)
    def _():
        out[...] += leaf_product(size, 0, per, place, near, spread, mine)
        out[...] += leaf_product(size, 1, per, place, far, spread, other)


def leaf_back_kernel(size, flip, per, place, *rest):
    blocks, (spread, path, before), rest = rest[:per], rest[per : per + 3], rest[per + 3 :]
    out, total = rest[-2:]

    @pl.when(pl.program_id(0) == 0)
    def _():
        total[...] = before[...]

    @pl.when(pl.program_id(0) >= 0)
    def _():
        total[...] += leaf_product(size, flip, per, place, blocks, spread, path)

    @pl.when(pl.program_id(0) == pl.num_programs(0) - 1)
    def _():
        if not flip:
            out[...] = total[...]
        else:
            forward, inverse_t = rest[:2]
            gap = forward[...] - total[...].T
            inverse = inverse_t[...].T
            for at in range(gap.shape[0] // size):
                rows = slice(at * size, (at + 1) * size)
                block = triangular(inverse[rows, :], 0, 0).T
                out[rows, :] = jnp.dot(
                    block, gap[rows, :], precision=PRECISE, preferred_element_type=F32
                )


def body(
    leaf_rhs,
    leaf_inverse,
    leaf_coupling,
    tile_mask,
    low_rhs,
    top_rhs,
    low_inverse,
    top_inverse,
    low_coupling,
):
    device_total = lax.axis_size("leaf") * lax.axis_size("sep")
    device = lax.axis_index("leaf") * lax.axis_size("sep") + lax.axis_index("sep")
    local_rows, columns = leaf_rhs.shape
    size = leaf_inverse.shape[1]
    levels = leaf_coupling.shape[0]
    sep_size = low_inverse.shape[1]
    low_count = low_inverse.shape[0]
    top_count = top_inverse.shape[0]
    chunk = sep_size // GROUP
    low_far = list(range(GROUP, device_total // 2, GROUP))
    top_far = list(range(GROUP, device_total, GROUP))
    low_start = device % (device_total // 2) * low_count
    top_start = device * top_count
    place = jnp.stack([device % 2, device % GROUP // 2, low_start, top_start]).astype(jnp.int32)

    inverse_t = leaf_inverse.T
    tiles = at_rest(jnp.transpose(tile_mask, (2, 0, 1)))
    coupling = leaf_coupling.reshape(levels, GROUP, chunk, local_rows)
    low_blocks = low_coupling.reshape(GROUP, chunk, low_count)

    leaf_flops = 2 * sep_size * local_rows * columns
    leaf_moved = 2 * sep_size * local_rows
    leaf_low = over((1, 1, chunk, local_rows), lambda c: (0, c, 0, 0), SENDING)
    leaf_back = over((1, 1, chunk, local_rows), lambda c: (0, c, 0, 0), ARRIVING)
    leaf_top = over((1, 1, chunk, local_rows), lambda c: (1, c, 0, 0), ARRIVING)
    spread_shape = (levels, sep_size // size, local_rows)

    per = 4
    coded = (chunk + PAD, columns)
    sent, forward_leaf, rounded_leaf, spread = call(
        functools.partial(leaf_send_kernel, size, per),
        place,
        NEAR // per,
        [leaf_low(at, per, 1) for at in range(per)]
        + [whole(a.shape) for a in (leaf_rhs, inverse_t, tiles, low_rhs)],
        [
            in_steps(per, coded, I16, NEAR),
            out_whole(leaf_rhs.shape, F32),
            out_whole(leaf_rhs.shape, BF16),
            out_whole(spread_shape, F32),
        ],
        [],
        [at_rest(coupling)] * per + [at_rest(leaf_rhs), at_rest(inverse_t), tiles, at_rest(low_rhs)],
        leaf_flops // 2,
        leaf_moved // 2,
    )

    kept = reduced_held(
        place,
        functools.partial(leaf_keep_kernel, size),
        [coupling, spread, rounded_leaf, low_rhs],
        (chunk, columns),
        [],
        leaf_flops,
        leaf_moved,
        swap(sent, 1),
    )
    part = call(
        functools.partial(leaf_top_kernel, size),
        place,
        GROUP // per,
        [
            pl.BlockSpec((1, *spread_shape[1:]), lambda k, p: (1, 0, 0)),
            whole(rounded_leaf.shape),
            pl.BlockSpec((1, per, chunk, local_rows), lambda k, p: (1, k, 0, 0)),
        ],
        [in_steps(per, (chunk, columns), F32, GROUP)],
        [],
        [spread, rounded_leaf, at_rest(coupling)],
        leaf_flops,
        leaf_moved,
    )[0]
    first_input = reduce_and_gather(place, kept, low_far, before=[part])
    first_rows, first_columns = factor_apply(place, low_inverse, first_input, 2)

    coupled_flops = 8 * sep_size * low_count * columns
    coupled_moved = 4 * sep_size * low_count
    kept = reduced_held(
        place,
        coupled_kernel,
        [low_blocks, part, first_rows, top_rhs],
        (chunk, columns),
        [pltpu.VMEM((low_count, 2 * columns), BF16)],
        coupled_flops,
        coupled_moved,
    )
    top_input = reduce_and_gather(place, kept, top_far)
    _, forward_columns = factor_apply(place, top_inverse, top_input, 3)

    kept = back_apply(place, top_inverse, forward_columns, 3)
    solution_blocks = reduce_and_gather(place, kept, top_far)
    turned = (columns, chunk)
    gap, rounded = first_columns, []
    for flip in range(2):
        gap, near = held_call(
            functools.partial(carry_kernel, flip),
            place,
            [(gap.shape, F32), ((NEAR, *turned), BF16)],
            [pltpu.VMEM((2 * columns, low_count), F32), pltpu.VMEM((columns, low_count), F32)],
            [low_blocks, solution_blocks[flip], gap],
            coupled_flops // 2,
            coupled_moved // 2,
        )
        rounded.append(near)
    top_own = call(
        own_kernel,
        place,
        1,
        [
            pl.BlockSpec(
                (1, *s.shape[1:]), lambda k, p: (digit(PLACE_OF, (p[3] // chunk // 2) ^ p[1]), 0, 0)
            )
            for s in solution_blocks
        ],
        [out_whole((chunk, columns), F32)],
        [],
        list(solution_blocks),
        chunk * columns,
        8 * chunk * columns,
    )[0]
    top_solution = lax.dynamic_slice_in_dim(top_own, top_start % chunk, top_count, 0)
    kept = back_apply(place, low_inverse, gap, 2)
    per = 2
    back_top = call(
        functools.partial(leaf_back_top_kernel, size, per),
        place,
        NEAR // per,
        [leaf_top(at, per, flip) for flip in range(2) for at in range(per)]
        + [pl.BlockSpec((1, *spread_shape[1:]), lambda k, p: (1, 0, 0))]
        + [in_steps(per, turned)] * 2,
        [out_whole((columns, local_rows), F32)],
        [],
        [at_rest(coupling)] * (2 * per) + [spread, *rounded],
        leaf_flops,
        leaf_moved,
    )[0]
    path = reduce_and_gather(place, kept, low_far, True, [back_top, top_own])
    per = 4
    result = back_top
    for flip in range(2):
        last = [forward_leaf, inverse_t] if flip else []
        result = call(
            functools.partial(leaf_back_kernel, size, flip, per),
            place,
            NEAR // per,
            [leaf_back(at, per, flip) for at in range(per)]
            + [pl.BlockSpec((1, *spread_shape[1:]), lambda k, p: (0, 0, 0))]
            + [in_steps(per, turned), whole(result.shape)]
            + [whole(a.shape) for a in last],
            [out_whole((local_rows, columns) if flip else (columns, local_rows), F32)],
            [pltpu.VMEM((columns, local_rows), F32)],
            [at_rest(coupling)] * per + [spread, path[flip], result, *last],
            leaf_flops // 2,
            leaf_moved // 2,
        )[0]
    return result, top_solution


def solution(mesh):
    return jax.shard_map(
        body,
        mesh=mesh,
        in_specs=(
            P(("leaf", "sep"), None),
            P(("leaf", "sep"), None),
            P(None, None, ("leaf", "sep")),
            P(None, None, ("leaf", "sep")),
            P(("leaf", "sep"), None),
            P(("leaf", "sep"), None),
            P(("leaf", "sep"), None),
            P(("leaf", "sep"), None),
            P(None, ("leaf", "sep")),
        ),
        out_specs=(P(("leaf", "sep"), None), P(("leaf", "sep"), None)),
        check_vma=False,
    )
```
